32 devices in a mesh: branch: 2 (over y), rows: 16 (over z, x, core).
Axes of the slice: x: 2, y: 2, z: 4, core: 2. Of those that a mesh axis runs over, the one named last changes fastest.
Arguments:
- homolog_features: bfloat16 [32, 256, 256], P(('branch', 'rows')), may hold values from -6 to 6
- pairwise_input: bfloat16 [256, 256, 128], P('rows', 'branch'), may hold values from -6 to 6
- transition_expand_matrix: bfloat16 [256, 1024], replicated, may hold values from -0.375 to 0.375
- transition_contract_matrix: bfloat16 [1024, 256], replicated, may hold values from -0.1875 to 0.1875
- factor_pair_matrices: bfloat16 [256, 64], replicated, may hold values from -0.375 to 0.375
- outer_output_weight: bfloat16 [1024, 128], replicated, may hold values from -0.75 to 0.75
- triangle_projection_weight: bfloat16 [128, 640], replicated, may hold values from -0.5 to 0.5
- triangle_output_weight: bfloat16 [128, 128], replicated, may hold values from -1 to 1
- pairwise_up_weight: bfloat16 [128, 512], replicated, may hold values from -0.5 to 0.5
- pairwise_down_weight: bfloat16 [512, 128], replicated, may hold values from -0.25 to 0.25
Outputs:
- refreshed_homolog_features: bfloat16 [32, 256, 256], P(('branch', 'rows'))
- pairwise_output: bfloat16 [256, 256, 128], P('rows', 'branch')
The draws below stay inside these ranges and needn't reach their ends.
All inputs are finite; a program needn't handle non-finite values.
Results may differ from the reference program's by a relative error of at most 0.0085.
Values may be sent and summed in bfloat16 or wider, within the bound.
No kernel may reach another device: no remote copies, remote signals or barrier semaphores. Data moves between devices by JAX's collectives and lax.ppermute only.
A program may use at most 128 MiB of HBM per device.

```python
import jax
import jax.numpy as jnp
from jax import lax

FEATURE_DEPTH = 256
EXPANDED_DEPTH = 1024
FACTOR_DEPTH = 32
PAIR = 128
PAIR_HID = 512
ROW_DEV = 16
AMINO_TOTAL = 256
HOMOLOG_TOTAL = 32
N_ROWS = 16


def block_levels(key, shape, shards, low, top_value):
    def one(axis_at, blocks):
        draws = jax.random.uniform(jax.random.fold_in(jax.random.fold_in(key, 6), axis_at), (blocks,), jnp.float32, low / len(shards), top_value / len(shards))
        return jnp.repeat(jnp.exp(draws), shape[axis_at] // blocks).reshape((-1,) + (1,) * (len(shape) - axis_at - 1))

    factor_of = one(*shards[0])
    for cut in shards[1:]:
        factor_of = factor_of * one(*cut)
    return factor_of


def normal_values(key, shape, deviation, bound, shards=(), held_as=jnp.bfloat16):
    drawn = jax.random.normal(key, shape, jnp.float32) * deviation
    if len(shards) > 0:
        drawn = block_levels(key, shape, shards, -0.22, 0.18) * drawn
    return jnp.clip(drawn, min=-bound, max=bound).astype(held_as)


def setup_inputs(seed: int = 0) -> dict:
    key_list = jax.random.split(jax.random.key(seed), 11)
    return {
        "homolog_features": normal_values(key_list[0], (HOMOLOG_TOTAL, AMINO_TOTAL, FEATURE_DEPTH), 1.0, 6.0, ((0, 32),)),
        "pairwise_input": normal_values(key_list[1], (AMINO_TOTAL, AMINO_TOTAL, PAIR), 1.0, 6.0, ((0, 16), (1, 2))),
        "transition_expand_matrix": normal_values(key_list[2], (FEATURE_DEPTH, EXPANDED_DEPTH), FEATURE_DEPTH ** -0.5, 0.375),
        "transition_contract_matrix": normal_values(key_list[3], (EXPANDED_DEPTH, FEATURE_DEPTH), EXPANDED_DEPTH ** -0.5, 0.1875),
        "factor_pair_matrices": normal_values(key_list[4], (FEATURE_DEPTH, 2 * FACTOR_DEPTH), FEATURE_DEPTH ** -0.5, 0.375),
        "outer_output_weight": normal_values(key_list[5], (FACTOR_DEPTH * FACTOR_DEPTH, PAIR), (2 * FACTOR_DEPTH) ** -0.5, 0.75),
        "triangle_projection_weight": normal_values(key_list[6], (PAIR, 5 * PAIR), PAIR ** -0.5, 0.5),
        "triangle_output_weight": normal_values(key_list[7], (PAIR, PAIR), (PAIR // 4) ** -0.5, 1.0),
        "pairwise_up_weight": normal_values(key_list[8], (PAIR, PAIR_HID), PAIR ** -0.5, 0.5),
        "pairwise_down_weight": normal_values(key_list[9], (PAIR_HID, PAIR), PAIR_HID ** -0.5, 0.25),
    }


def standardize_features(values, dimension):
    average = lax.optimization_barrier(jnp.mean(values, axis=dimension, keepdims=True))
    centered = values - average
    variance = lax.optimization_barrier(jnp.mean(centered * centered, axis=dimension, keepdims=True))
    return centered * lax.rsqrt(variance + 1e-05)

def rounded(values):
    return lax.optimization_barrier(values.astype(jnp.bfloat16)).astype(jnp.float32)

def reference(homolog_features, pairwise_input, transition_expand_matrix, transition_contract_matrix, factor_pair_matrices, outer_output_weight, triangle_projection_weight, triangle_output_weight, pairwise_up_weight, pairwise_down_weight):
    homolog_real_matrix = homolog_features.astype(jnp.float32)
    standardized_homologs = standardize_features(homolog_real_matrix, -1).astype(jnp.bfloat16).reshape(HOMOLOG_TOTAL * AMINO_TOTAL, FEATURE_DEPTH)
    expanded_activations = jax.nn.relu(jnp.dot(standardized_homologs, transition_expand_matrix, preferred_element_type=jnp.float32)).astype(jnp.bfloat16)
    refreshed_homolog_features = (homolog_real_matrix + jnp.dot(expanded_activations, transition_contract_matrix, preferred_element_type=jnp.float32).reshape(HOMOLOG_TOTAL, AMINO_TOTAL, FEATURE_DEPTH)).astype(jnp.bfloat16)
    standardized_for_factors = standardize_features(refreshed_homolog_features.astype(jnp.float32), -1).astype(jnp.bfloat16).reshape(HOMOLOG_TOTAL * AMINO_TOTAL, FEATURE_DEPTH)
    projected = jnp.dot(standardized_for_factors, factor_pair_matrices, preferred_element_type=jnp.float32).reshape(HOMOLOG_TOTAL, AMINO_TOTAL, 2 * FACTOR_DEPTH)
    left_side = projected[..., :FACTOR_DEPTH].astype(jnp.bfloat16)
    right_side = projected[..., FACTOR_DEPTH:].astype(jnp.bfloat16)
    right_flat = right_side.reshape(HOMOLOG_TOTAL, AMINO_TOTAL * FACTOR_DEPTH)
    outer_weight = outer_output_weight.astype(jnp.float32).reshape(FACTOR_DEPTH, FACTOR_DEPTH, PAIR)
    left_tiles = jnp.moveaxis(left_side.reshape(HOMOLOG_TOTAL, N_ROWS, ROW_DEV * FACTOR_DEPTH), 1, 0)
    pair_tiles = pairwise_input.reshape(N_ROWS, ROW_DEV, AMINO_TOTAL, PAIR)
    tri_weight = triangle_projection_weight.astype(jnp.float32)

    def tri_inputs(pair_tile):
        pair_norm = rounded(standardize_features(pair_tile.astype(jnp.float32), -1))
        proj_tile = jnp.einsum('ikd,de->eik', pair_norm, tri_weight[:, :4 * PAIR])
        left_tri = (jax.nn.sigmoid(proj_tile[PAIR:2 * PAIR]) * proj_tile[:PAIR]).astype(jnp.bfloat16)
        right_tri = (jax.nn.sigmoid(proj_tile[3 * PAIR:]) * proj_tile[2 * PAIR:3 * PAIR]).astype(jnp.bfloat16)
        return (left_tri, right_tri)
    left_stack, right_stack = lax.map(tri_inputs, pair_tiles)
    left_chan = jnp.moveaxis(left_stack, 1, 0).reshape(PAIR, AMINO_TOTAL, AMINO_TOTAL)
    right_chan = jnp.moveaxis(right_stack, 1, 0).reshape(PAIR, AMINO_TOTAL, AMINO_TOTAL)

    def channel_product(operands):
        left_one, right_one = operands
        return jnp.dot(left_one, right_one.T, preferred_element_type=jnp.float32).astype(jnp.bfloat16)
    product = lax.map(channel_product, (left_chan, right_chan))
    product_tiles = jnp.moveaxis(product.reshape(PAIR, N_ROWS, ROW_DEV, AMINO_TOTAL), 1, 0)

    def tile_output(operands):
        pair_tile, product_tile, left_tile = operands
        pair_float = pair_tile.astype(jnp.float32)
        pair_norm = rounded(standardize_features(pair_float, -1))
        gate_vals = jax.nn.sigmoid(jnp.einsum('ijd,de->ije', pair_norm, tri_weight[:, 4 * PAIR:]))
        prod_norm = rounded(standardize_features(product_tile.astype(jnp.float32), 0))
        tri_update = jnp.einsum('cij,ce->ije', prod_norm, triangle_output_weight.astype(jnp.float32))
        pair_mid = pair_float + gate_vals * tri_update
        mid_norm = rounded(standardize_features(pair_mid, -1))
        pair_hidden = rounded(jax.nn.relu(jnp.einsum('ijd,dh->ijh', mid_norm, pairwise_up_weight.astype(jnp.float32))))
        pair_mid = pair_mid + jnp.einsum('ijh,hd->ijd', pair_hidden, pairwise_down_weight.astype(jnp.float32))
        outer_vals = jnp.dot(left_tile.T, right_flat, preferred_element_type=jnp.float32)
        outer_vals = rounded(outer_vals / HOMOLOG_TOTAL).reshape(ROW_DEV, FACTOR_DEPTH, AMINO_TOTAL, FACTOR_DEPTH)
        outer_update = jnp.einsum('icjd,cde->ije', outer_vals, outer_weight)
        return (pair_mid + outer_update).astype(jnp.bfloat16)
    pairwise_output = lax.map(tile_output, (pair_tiles, product_tiles, left_tiles)).reshape(AMINO_TOTAL, AMINO_TOTAL, PAIR)
    return (refreshed_homolog_features, pairwise_output)
```

```python
import functools

import jax
import jax.numpy as jnp
from jax import lax
from jax.experimental import pallas as pl
from jax.experimental.pallas import tpu as pltpu
from jax.sharding import PartitionSpec as P

BF16 = jnp.bfloat16
F32 = jnp.float32
AXES = ("branch", "rows")
NT = (((1,), (1,)), ((), ()))
TN = (((0,), (0,)), ((), ()))
VMEM = pl.BlockSpec(memory_space=pltpu.VMEM)
SMEM = pl.BlockSpec(memory_space=pltpu.SMEM)
PARAMS = pltpu.CompilerParams(vmem_limit_bytes=48 * 1024 * 1024)

def standardize_features(values, dimension):
    average = jnp.mean(values, axis=dimension, keepdims=True)
    centered = values - average
    variance = jnp.mean(centered * centered, axis=dimension, keepdims=True)
    return centered * lax.rsqrt(variance + 1e-05)


def alignment_branch(
    homolog_features, transition_expand_matrix, transition_contract_matrix, factor_pair_matrices
):
    local_rows, sequence_length, channel_width = homolog_features.shape
    homolog_real_matrix = homolog_features.astype(jnp.float32)
    standardized_homologs = (
        standardize_features(homolog_real_matrix, -1)
        .astype(jnp.bfloat16)
        .reshape(local_rows * sequence_length, channel_width)
    )
    expanded_activations = jax.nn.relu(
        jnp.dot(standardized_homologs, transition_expand_matrix, preferred_element_type=jnp.float32)
    ).astype(jnp.bfloat16)
    refreshed_homolog_features = (
        homolog_real_matrix
        + jnp.dot(
            expanded_activations, transition_contract_matrix, preferred_element_type=jnp.float32
        ).reshape(homolog_features.shape)
    ).astype(jnp.bfloat16)
    standardized_for_factors = (
        standardize_features(refreshed_homolog_features.astype(jnp.float32), -1)
        .astype(jnp.bfloat16)
        .reshape(local_rows * sequence_length, channel_width)
    )
    projected = jnp.dot(
        standardized_for_factors, factor_pair_matrices, preferred_element_type=jnp.float32
    ).reshape(local_rows, sequence_length, -1)
    channels = projected.shape[-1] // 2
    left_side = projected[..., :channels].astype(jnp.bfloat16)
    right_side = jnp.swapaxes(projected[..., channels:].astype(jnp.bfloat16), 1, 2)
    left_pair = lax.all_gather(left_side, "branch", axis=0, tiled=True)
    left_gathered = lax.all_to_all(left_pair, "rows", split_axis=1, concat_axis=0, tiled=True)
    right_pair = lax.all_to_all(right_side, "branch", split_axis=2, concat_axis=0, tiled=True)
    right_gathered = lax.all_gather(right_pair, "rows", axis=0, tiled=True)
    return (refreshed_homolog_features, left_gathered, right_gathered)


def send_whole(tri_left, tri_right):
    return (
        lax.all_to_all(
            lax.all_to_all(tri_left, "branch", split_axis=0, concat_axis=2, tiled=True),
            "rows",
            split_axis=0,
            concat_axis=1,
            tiled=True,
        ),
        lax.all_to_all(
            lax.all_to_all(tri_right, "branch", split_axis=0, concat_axis=2, tiled=True),
            "rows",
            split_axis=0,
            concat_axis=1,
            tiled=True,
        ),
    )


def send_back(product):
    return lax.all_to_all(
        lax.all_to_all(product, "rows", split_axis=1, concat_axis=0, tiled=True),
        "branch",
        split_axis=2,
        concat_axis=0,
        tiled=True,
    )


def pair_branch(
    pairwise_input,
    triangle_projection_weight,
    triangle_output_weight,
    pairwise_up_weight,
    pairwise_down_weight,
):
    tile_rows, columns, chans = pairwise_input.shape
    pair_float = pairwise_input.astype(jnp.float32)
    pair_norm = standardize_features(pair_float, -1).astype(jnp.bfloat16)
    norm_flat = pair_norm.reshape(tile_rows * columns, chans)
    proj_flat = lax.dot_general(
        triangle_projection_weight,
        norm_flat,
        (((0,), (1,)), ((), ())),
        preferred_element_type=jnp.float32,
    )
    proj_tile = proj_flat[: 4 * chans].reshape(4 * chans, tile_rows, columns)
    gate_vals = jax.nn.sigmoid(proj_flat[4 * chans :])
    tri_left = (jax.nn.sigmoid(proj_tile[chans : 2 * chans]) * proj_tile[:chans]).astype(
        jnp.bfloat16
    )
    tri_right = (jax.nn.sigmoid(proj_tile[3 * chans :]) * proj_tile[2 * chans : 3 * chans]).astype(
        jnp.bfloat16
    )
    left_chan, right_chan = send_whole(tri_left, tri_right)
    product = jnp.einsum(
        "cik,cjk->cij", left_chan, right_chan, preferred_element_type=jnp.float32
    ).astype(jnp.bfloat16)
    product_tile = send_back(product)
    prod_norm = (
        standardize_features(product_tile.astype(jnp.float32), 0)
        .astype(jnp.bfloat16)
        .reshape(chans, tile_rows * columns)
    )
    tri_update = lax.dot_general(
        triangle_output_weight,
        prod_norm,
        (((0,), (0,)), ((), ())),
        preferred_element_type=jnp.float32,
    )
    gated_update = jnp.transpose(gate_vals * tri_update).reshape(tile_rows, columns, chans)
    pair_mid = pair_float + gated_update
    mid_norm = standardize_features(pair_mid, -1).astype(jnp.bfloat16)
    pair_hidden = jax.nn.relu(
        jnp.einsum("ijd,dh->ijh", mid_norm, pairwise_up_weight, preferred_element_type=jnp.float32)
    ).astype(jnp.bfloat16)
    return pair_mid + jnp.einsum(
        "ijh,hd->ijd", pair_hidden, pairwise_down_weight, preferred_element_type=jnp.float32
    )


def outer_product(left_gathered, right_gathered, outer_output_weight):
    total_rows, tile_rows, channels = left_gathered.shape
    columns = right_gathered.shape[2]
    span_cols = 128
    left_flat = left_gathered.reshape(total_rows, tile_rows * channels)
    pieces = []
    for offset in range(0, columns, span_cols):
        right_piece = right_gathered[:, :, offset : offset + span_cols].reshape(
            total_rows, channels * span_cols
        )
        outer_vals = lax.dot_general(
            left_flat, right_piece, (((0,), (0,)), ((), ())), preferred_element_type=jnp.float32
        )
        outer_vals = (
            (outer_vals / total_rows)
            .astype(jnp.bfloat16)
            .reshape(tile_rows, channels * channels, span_cols)
        )
        pieces.append(
            lax.dot_general(
                outer_output_weight,
                outer_vals,
                (((0,), (1,)), ((), ())),
                preferred_element_type=jnp.float32,
            )
        )
    outer_eij = jnp.concatenate(pieces, axis=2)
    return jnp.transpose(outer_eij, (1, 2, 0))


def general_device(
    homolog_features,
    pairwise_input,
    transition_expand_matrix,
    transition_contract_matrix,
    factor_pair_matrices,
    outer_output_weight,
    triangle_projection_weight,
    triangle_output_weight,
    pairwise_up_weight,
    pairwise_down_weight,
):
    refreshed_homolog_features, left_gathered, right_gathered = alignment_branch(
        homolog_features, transition_expand_matrix, transition_contract_matrix, factor_pair_matrices
    )
    pair_mid = pair_branch(
        pairwise_input,
        triangle_projection_weight,
        triangle_output_weight,
        pairwise_up_weight,
        pairwise_down_weight,
    )
    outer_update = outer_product(left_gathered, right_gathered, outer_output_weight)
    pairwise_output = (pair_mid + outer_update).astype(jnp.bfloat16)
    return (refreshed_homolog_features, pairwise_output)


def normed(values, axis):
    average = jnp.mean(values, axis=axis, keepdims=True)
    centered = values - average
    variance = jnp.mean(centered * centered, axis=axis, keepdims=True)
    return (centered * lax.rsqrt(variance + 1e-05)).astype(BF16)


def sigmoid(values):
    return 0.5 * jnp.tanh(0.5 * values) + 0.5


def dot(a, b, dims=(((1,), (0,)), ((), ()))):
    return lax.dot_general(a, b, dims, preferred_element_type=F32)


def cost(flops, nbytes, transcendentals=0):
    return pl.CostEstimate(flops=flops, bytes_accessed=nbytes, transcendentals=transcendentals)


def operands_kernel(x_ref, w_ref, out_ref, scr):
    rows, _, chans = x_ref.shape
    per = out_ref.shape[1] // 2
    n = 2 * chans
    row = lax.broadcasted_iota(jnp.int32, (n, n), 0)
    col = lax.broadcasted_iota(jnp.int32, (n, n), 1)
    source = (row % (2 * per)) // per * chans + row // (2 * per) * per + row % per
    order = jnp.where(col == source, 1.0, 0.0).astype(BF16)
    w = w_ref[...]
    values = jnp.concatenate([w[:, :chans], w[:, 2 * chans : 3 * chans]], axis=1)
    gates = jnp.concatenate([w[:, chans : 2 * chans], w[:, 3 * chans : 4 * chans]], axis=1)
    values = dot(order, values, NT).astype(BF16)
    gates = dot(order, gates, NT).astype(BF16)
    width = x_ref.shape[1]
    for i in range(0, rows, 2):
        pair = x_ref[i : i + 2].astype(F32).reshape(2 * width, chans)
        tokens = normed(pair, -1)
        result = dot(values, tokens, NT) * sigmoid(dot(gates, tokens, NT))
        scr[pl.ds(i, n, stride=rows), :] = result[:, :width]
        scr[pl.ds(i + 1, n, stride=rows), :] = result[:, width:]
    for q in range(n):
        out_ref[q // (2 * per), q % (2 * per)] = scr[q * rows : (q + 1) * rows, :].astype(BF16)


def operands(x, w, devices):
    rows, width, chans = x.shape
    return pl.pallas_call(
        operands_kernel,
        out_shape=jax.ShapeDtypeStruct((devices, 2 * chans // devices, rows, width), BF16),
        in_specs=[VMEM, VMEM],
        out_specs=VMEM,
        scratch_shapes=[pltpu.VMEM((2 * chans * rows, width), F32)],
        compiler_params=PARAMS,
        cost_estimate=cost(2 * rows * width * chans * 4 * chans, 3 * rows * width * chans * 2),
        name="triangle_operands",
    )(x, w)


def gate_kernel(x_ref, w_ref, out_ref):
    rows, width, chans = x_ref.shape
    tokens = normed(x_ref[...].astype(F32).reshape(rows * width, chans), -1)
    out_ref[...] = sigmoid(dot(tokens, w_ref[:, 4 * chans :])).reshape(rows, width, chans)


def output_gate(x, w):
    rows, width, chans = x.shape
    step = 4
    spec = pl.BlockSpec((step, width, chans), lambda i: (i, 0, 0))
    return pl.pallas_call(
        gate_kernel,
        grid=(rows // step,),
        out_shape=jax.ShapeDtypeStruct(x.shape, F32),
        in_specs=[spec, pl.BlockSpec(w.shape, lambda i: (0, 0))],
        out_specs=spec,
        compiler_params=PARAMS,
        cost_estimate=cost(2 * rows * width * chans * chans, rows * width * chans * 6),
        name="triangle_output_gate",
    )(x, w)


def product_kernel(n_branch, in_ref, out_ref):
    devices, double, rows, width = in_ref.shape
    per = double // 2
    n_rows = devices // n_branch
    total = n_rows * rows

    def side(c):
        halves = [
            in_ref[b * n_rows : (b + 1) * n_rows, c].reshape(total, width) for b in range(n_branch)
        ]
        return jnp.concatenate(halves, axis=1)

    for c in range(per):
        product = dot(side(c), side(per + c), NT).astype(BF16)
        for b in range(n_branch):
            out_ref[b * n_rows : (b + 1) * n_rows, c] = product[
                :, b * width : (b + 1) * width
            ].reshape(n_rows, rows, width)


def triangle_product(received, n_branch):
    devices, double, rows, width = received.shape
    return pl.pallas_call(
        functools.partial(product_kernel, n_branch),
        out_shape=jax.ShapeDtypeStruct((devices, double // 2, rows, width), BF16),
        in_specs=[VMEM],
        out_specs=VMEM,
        compiler_params=PARAMS,
        cost_estimate=cost(double * (devices // n_branch * rows) ** 3, received.size * 3),
        name="triangle_product",
    )(received)


def pair_output_kernel(
    p_ref, x_ref, gate_ref, outer_ref, w_ref, up_ref, down_ref, out_ref, scr
):
    devices, per, rows, width = p_ref.shape
    chans = devices * per
    for g in range(devices):
        for c in range(per):
            scr[pl.ds(g * per + c, rows, stride=chans), :] = p_ref[g, c].astype(F32)
    step = 4
    for i in range(0, rows, step):
        parts = [
            normed(scr[(i + k) * chans : (i + k + 1) * chans, :], 0) for k in range(step)
        ]
        update = dot(jnp.concatenate(parts, axis=1), w_ref[...], TN)
        shape = (step * width, chans)
        x = x_ref[i : i + step].astype(F32).reshape(shape)
        middle = x + gate_ref[i : i + step].reshape(shape) * update
        hidden = jnp.maximum(dot(normed(middle, -1), up_ref[...]), 0.0).astype(BF16)
        result = middle + dot(hidden, down_ref[...]) + outer_ref[i : i + step].reshape(shape)
        out_ref[i : i + step] = result.astype(BF16).reshape(step, width, chans)


def pair_output(product, x, gate, outer, w, up, down):
    devices, per, rows, width = product.shape
    chans = devices * per
    return pl.pallas_call(
        pair_output_kernel,
        out_shape=jax.ShapeDtypeStruct(x.shape, BF16),
        in_specs=[VMEM] * 7,
        out_specs=VMEM,
        scratch_shapes=[pltpu.VMEM((rows * chans, width), F32)],
        compiler_params=PARAMS,
        cost_estimate=cost(2 * x.size * (chans + 2 * up.shape[1]), x.size * 14),
        name="pair_output",
    )(product, x, gate, outer, w, up, down)


def msa_kernel(n_branch, where_ref, x_ref, up_ref, down_ref, factor_ref, fresh_ref, *rest):
    out_refs, right_scr, left_scr = rest[:-2], rest[-2], rest[-1]
    x = x_ref[0].astype(F32)
    hidden = jnp.maximum(dot(normed(x, -1), up_ref[...]), 0.0).astype(BF16)
    fresh = (x + dot(hidden, down_ref[...])).astype(BF16)
    fresh_ref[0] = fresh
    tokens = normed(fresh.astype(F32), -1)
    factor = factor_ref[...]
    both = dot(tokens, factor).astype(BF16)
    both_t = dot(factor, tokens, (((0,), (1,)), ((), ()))).astype(BF16)
    depth = factor.shape[1] // 2
    length = x.shape[0]
    width = length // n_branch
    for b in range(n_branch):
        right_scr[b] = both_t[depth:, b * width : (b + 1) * width]
    planes, span = left_scr.shape[:2]
    padded = jnp.concatenate([both, jnp.zeros((length, width - 2 * depth), BF16)], axis=1)
    left_scr[...] = padded.reshape(planes, span, width)
    branch, plane = where_ref[0], where_ref[1]
    for t, out_ref in enumerate(out_refs):
        out_ref[:depth] = right_scr[lax.bitwise_xor(branch, t // planes)]
        out_ref[depth:] = left_scr[lax.bitwise_xor(plane, t % planes)]


def msa(where, x, up, down, factor, n_branch, planes):
    _, length, feats = x.shape
    depth = factor.shape[1] // 2
    width, span = length // n_branch, length // planes
    piece = jax.ShapeDtypeStruct((depth + span, width), BF16)
    count = n_branch * planes
    fresh, *pieces = pl.pallas_call(
        functools.partial(msa_kernel, n_branch),
        out_shape=[jax.ShapeDtypeStruct(x.shape, BF16)] + [piece] * count,
        in_specs=[SMEM] + [VMEM] * 4,
        out_specs=[VMEM] * (1 + count),
        scratch_shapes=[
            pltpu.VMEM((n_branch, depth, width), BF16),
            pltpu.VMEM((planes, span, width), BF16),
        ],
        compiler_params=PARAMS,
        cost_estimate=cost(4 * length * feats * up.shape[1], 4 * feats * up.shape[1]),
        name="msa_transition",
    )(where, x, up, down, factor)
    return fresh, pieces


def outer_kernel(where_ref, *refs):
    groups, (w_ref, out_ref, right_scr, left_scr, w_scr, m_scr) = refs[:-6], refs[-6:]
    rows, width, chans = out_ref.shape
    total = sum(ref.shape[0] for ref in groups)
    depth = m_scr.shape[1] // total
    tile = where_ref[2]
    s = 0
    for ref in groups:
        for k in range(ref.shape[0]):
            right_scr[pl.ds(s, depth, stride=total), :] = ref[k, :depth].astype(F32)
            start = pl.multiple_of(depth + tile * rows, rows)
            left_scr[pl.ds(s, rows, stride=total), :] = ref[k, pl.ds(start, rows)].astype(F32)
            s += 1
    right = jnp.transpose(right_scr[...]).astype(BF16)
    left = left_scr[...][:, :depth].astype(BF16)
    w_scr[...] = w_ref[...].astype(F32)
    for d in range(depth):
        part = w_scr[pl.ds(d, depth, stride=depth), :].astype(BF16)
        m_scr[:, d * total : (d + 1) * total] = (
            dot(left, part).astype(BF16).reshape(rows, total, chans)
        )
    for i in range(0, rows, 2):
        pair = jnp.concatenate([m_scr[i], m_scr[i + 1]], axis=1)
        result = dot(right, pair) / total
        out_ref[i] = result[:, :chans]
        out_ref[i + 1] = result[:, chans:]


def outer_update(where, groups, w, rows, chans):
    total = sum(group.shape[0] for group in groups)
    width = groups[0].shape[2]
    depth = int(round(w.shape[0] ** 0.5))
    return pl.pallas_call(
        outer_kernel,
        out_shape=jax.ShapeDtypeStruct((rows, width, chans), F32),
        in_specs=[SMEM] + [VMEM] * (len(groups) + 1),
        out_specs=VMEM,
        scratch_shapes=[
            pltpu.VMEM((depth * total, width), F32),
            pltpu.VMEM((rows * total, width), F32),
            pltpu.VMEM((depth * depth, chans), F32),
            pltpu.VMEM((rows, depth * total, chans), BF16),
        ],
        compiler_params=PARAMS,
        cost_estimate=cost(2 * rows * width * depth * total * chans * 2, rows * width * chans * 4),
        name="outer_product_mean",
    )(where, *groups, w)


def swap(x, n_branch, n_rows, mask):
    count = n_branch * n_rows
    return lax.ppermute(x, AXES, [(d, d ^ mask) for d in range(count)])


def own_channels_device(
    n_branch,
    n_rows,
    homolog_features,
    pairwise_input,
    transition_expand_matrix,
    transition_contract_matrix,
    factor_pair_matrices,
    outer_output_weight,
    triangle_projection_weight,
    triangle_output_weight,
    pairwise_up_weight,
    pairwise_down_weight,
):
    rows, _, chans = pairwise_input.shape
    near = 4
    planes = n_rows // near
    r = lax.axis_index("rows")
    where = jnp.stack([lax.axis_index("branch"), r // near, r % near]).astype(jnp.int32)

    sent = operands(pairwise_input, triangle_projection_weight, n_branch * n_rows)
    received = lax.all_to_all(sent, AXES, 0, 0, tiled=True)

    fresh, pieces = msa(
        where,
        homolog_features,
        transition_expand_matrix,
        transition_contract_matrix,
        factor_pair_matrices,
        n_branch,
        planes,
    )
    moved = [
        piece if t == 0 else swap(piece, n_branch, n_rows, t // planes * n_rows + t % planes * near)
        for t, piece in enumerate(pieces)
    ]
    mine = jnp.stack(moved)
    beside = swap(mine, n_branch, n_rows, 2)
    groups = [mine, beside, swap(mine, n_branch, n_rows, 1), swap(beside, n_branch, n_rows, 1)]
    outer = outer_update(where, groups, outer_output_weight, rows, chans)
    gate = output_gate(pairwise_input, triangle_projection_weight)

    product = triangle_product(received, n_branch)
    returned = lax.all_to_all(product, AXES, 0, 0, tiled=True)
    pairwise_output = pair_output(
        returned,
        pairwise_input,
        gate,
        outer,
        triangle_output_weight,
        pairwise_up_weight,
        pairwise_down_weight,
    )
    return (fresh, pairwise_output)


def on_device(n_branch, n_rows, homolog_features, pairwise_input, *weights):
    rows, width, chans = pairwise_input.shape
    devices = n_branch * n_rows
    planes = n_rows // 4
    fits = (
        homolog_features.shape[0] == 1
        and n_branch & (n_branch - 1) == 0
        and n_rows % 4 == 0
        and n_rows & (n_rows - 1) == 0
        and chans % devices == 0
        and rows % 16 == 0
        and width == 128
        and homolog_features.shape[1] // planes == 4 * rows
        and devices * chans * rows * width <= 2**25
    )
    if fits:
        return own_channels_device(n_branch, n_rows, homolog_features, pairwise_input, *weights)
    return general_device(homolog_features, pairwise_input, *weights)


def solution(mesh):
    return jax.shard_map(
        functools.partial(on_device, mesh.shape["branch"], mesh.shape["rows"]),
        mesh=mesh,
        in_specs=(
            P(("branch", "rows"), None, None),
            P("rows", "branch", None),
            P(),
            P(),
            P(),
            P(),
            P(),
            P(),
            P(),
            P(),
        ),
        out_specs=(P(("branch", "rows"), None, None), P("rows", "branch", None)),
        check_vma=False,
    )
```

```python
import functools

import jax
import jax.numpy as jnp
from jax import lax
from jax.experimental import pallas as pl
from jax.experimental.pallas import tpu as pltpu
from jax.sharding import PartitionSpec as P

BF16 = jnp.bfloat16
F32 = jnp.float32
AXES = ("branch", "rows")
NT = (((1,), (1,)), ((), ()))
TN = (((0,), (0,)), ((), ()))
VMEM = pl.BlockSpec(memory_space=pltpu.VMEM)
SMEM = pl.BlockSpec(memory_space=pltpu.SMEM)
PARAMS = pltpu.CompilerParams(vmem_limit_bytes=48 * 1024 * 1024)

def standardize_features(values, dimension):
    average = jnp.mean(values, axis=dimension, keepdims=True)
    centered = values - average
    variance = jnp.mean(centered * centered, axis=dimension, keepdims=True)
    return centered * lax.rsqrt(variance + 1e-05)


def alignment_branch(
    homolog_features, transition_expand_matrix, transition_contract_matrix, factor_pair_matrices
):
    local_rows, sequence_length, channel_width = homolog_features.shape
    homolog_real_matrix = homolog_features.astype(jnp.float32)
    standardized_homologs = (
        standardize_features(homolog_real_matrix, -1)
        .astype(jnp.bfloat16)
        .reshape(local_rows * sequence_length, channel_width)
    )
    expanded_activations = jax.nn.relu(
        jnp.dot(standardized_homologs, transition_expand_matrix, preferred_element_type=jnp.float32)
    ).astype(jnp.bfloat16)
    refreshed_homolog_features = (
        homolog_real_matrix
        + jnp.dot(
            expanded_activations, transition_contract_matrix, preferred_element_type=jnp.float32
        ).reshape(homolog_features.shape)
    ).astype(jnp.bfloat16)
    standardized_for_factors = (
        standardize_features(refreshed_homolog_features.astype(jnp.float32), -1)
        .astype(jnp.bfloat16)
        .reshape(local_rows * sequence_length, channel_width)
    )
    projected = jnp.dot(
        standardized_for_factors, factor_pair_matrices, preferred_element_type=jnp.float32
    ).reshape(local_rows, sequence_length, -1)
    channels = projected.shape[-1] // 2
    left_side = projected[..., :channels].astype(jnp.bfloat16)
    right_side = jnp.swapaxes(projected[..., channels:].astype(jnp.bfloat16), 1, 2)
    left_pair = lax.all_gather(left_side, "branch", axis=0, tiled=True)
    left_gathered = lax.all_to_all(left_pair, "rows", split_axis=1, concat_axis=0, tiled=True)
    right_pair = lax.all_to_all(right_side, "branch", split_axis=2, concat_axis=0, tiled=True)
    right_gathered = lax.all_gather(right_pair, "rows", axis=0, tiled=True)
    return (refreshed_homolog_features, left_gathered, right_gathered)


def send_whole(tri_left, tri_right):
    return (
        lax.all_to_all(
            lax.all_to_all(tri_left, "branch", split_axis=0, concat_axis=2, tiled=True),
            "rows",
            split_axis=0,
            concat_axis=1,
            tiled=True,
        ),
        lax.all_to_all(
            lax.all_to_all(tri_right, "branch", split_axis=0, concat_axis=2, tiled=True),
            "rows",
            split_axis=0,
            concat_axis=1,
            tiled=True,
        ),
    )


def send_back(product):
    return lax.all_to_all(
        lax.all_to_all(product, "rows", split_axis=1, concat_axis=0, tiled=True),
        "branch",
        split_axis=2,
        concat_axis=0,
        tiled=True,
    )


def pair_branch(
    pairwise_input,
    triangle_projection_weight,
    triangle_output_weight,
    pairwise_up_weight,
    pairwise_down_weight,
):
    tile_rows, columns, chans = pairwise_input.shape
    pair_float = pairwise_input.astype(jnp.float32)
    pair_norm = standardize_features(pair_float, -1).astype(jnp.bfloat16)
    norm_flat = pair_norm.reshape(tile_rows * columns, chans)
    proj_flat = lax.dot_general(
        triangle_projection_weight,
        norm_flat,
        (((0,), (1,)), ((), ())),
        preferred_element_type=jnp.float32,
    )
    proj_tile = proj_flat[: 4 * chans].reshape(4 * chans, tile_rows, columns)
    gate_vals = jax.nn.sigmoid(proj_flat[4 * chans :])
    tri_left = (jax.nn.sigmoid(proj_tile[chans : 2 * chans]) * proj_tile[:chans]).astype(
        jnp.bfloat16
    )
    tri_right = (jax.nn.sigmoid(proj_tile[3 * chans :]) * proj_tile[2 * chans : 3 * chans]).astype(
        jnp.bfloat16
    )
    left_chan, right_chan = send_whole(tri_left, tri_right)
    product = jnp.einsum(
        "cik,cjk->cij", left_chan, right_chan, preferred_element_type=jnp.float32
    ).astype(jnp.bfloat16)
    product_tile = send_back(product)
    prod_norm = (
        standardize_features(product_tile.astype(jnp.float32), 0)
        .astype(jnp.bfloat16)
        .reshape(chans, tile_rows * columns)
    )
    tri_update = lax.dot_general(
        triangle_output_weight,
        prod_norm,
        (((0,), (0,)), ((), ())),
        preferred_element_type=jnp.float32,
    )
    gated_update = jnp.transpose(gate_vals * tri_update).reshape(tile_rows, columns, chans)
    pair_mid = pair_float + gated_update
    mid_norm = standardize_features(pair_mid, -1).astype(jnp.bfloat16)
    pair_hidden = jax.nn.relu(
        jnp.einsum("ijd,dh->ijh", mid_norm, pairwise_up_weight, preferred_element_type=jnp.float32)
    ).astype(jnp.bfloat16)
    return pair_mid + jnp.einsum(
        "ijh,hd->ijd", pair_hidden, pairwise_down_weight, preferred_element_type=jnp.float32
    )


def outer_product(left_gathered, right_gathered, outer_output_weight):
    total_rows, tile_rows, channels = left_gathered.shape
    columns = right_gathered.shape[2]
    span_cols = 128
    left_flat = left_gathered.reshape(total_rows, tile_rows * channels)
    pieces = []
    for offset in range(0, columns, span_cols):
        right_piece = right_gathered[:, :, offset : offset + span_cols].reshape(
            total_rows, channels * span_cols
        )
        outer_vals = lax.dot_general(
            left_flat, right_piece, (((0,), (0,)), ((), ())), preferred_element_type=jnp.float32
        )
        outer_vals = (
            (outer_vals / total_rows)
            .astype(jnp.bfloat16)
            .reshape(tile_rows, channels * channels, span_cols)
        )
        pieces.append(
            lax.dot_general(
                outer_output_weight,
                outer_vals,
                (((0,), (1,)), ((), ())),
                preferred_element_type=jnp.float32,
            )
        )
    outer_eij = jnp.concatenate(pieces, axis=2)
    return jnp.transpose(outer_eij, (1, 2, 0))


def general_device(
    homolog_features,
    pairwise_input,
    transition_expand_matrix,
    transition_contract_matrix,
    factor_pair_matrices,
    outer_output_weight,
    triangle_projection_weight,
    triangle_output_weight,
    pairwise_up_weight,
    pairwise_down_weight,
):
    refreshed_homolog_features, left_gathered, right_gathered = alignment_branch(
        homolog_features, transition_expand_matrix, transition_contract_matrix, factor_pair_matrices
    )
    pair_mid = pair_branch(
        pairwise_input,
        triangle_projection_weight,
        triangle_output_weight,
        pairwise_up_weight,
        pairwise_down_weight,
    )
    outer_update = outer_product(left_gathered, right_gathered, outer_output_weight)
    pairwise_output = (pair_mid + outer_update).astype(jnp.bfloat16)
    return (refreshed_homolog_features, pairwise_output)


def normed(values, axis):
    average = jnp.mean(values, axis=axis, keepdims=True)
    centered = values - average
    variance = jnp.mean(centered * centered, axis=axis, keepdims=True)
    return (centered * lax.rsqrt(variance + 1e-05)).astype(BF16)


def sigmoid(values):
    return 0.5 * jnp.tanh(0.5 * values) + 0.5


def dot(a, b, dims=(((1,), (0,)), ((), ()))):
    return lax.dot_general(a, b, dims, preferred_element_type=F32)


def cost(flops, nbytes, transcendentals=0):
    return pl.CostEstimate(flops=flops, bytes_accessed=nbytes, transcendentals=transcendentals)


def channel_order(w, sides, source, count):
    chans = w.shape[0]
    col = lax.broadcasted_iota(jnp.int32, (count, chans), 1)
    order = jnp.where(col == source, 1.0, 0.0).astype(BF16)
    return [dot(order, w[:, s * chans : (s + 1) * chans], NT).astype(BF16) for s in sides]


def gated_rows(values, gates, rows_ref, store):
    rows, width, chans = rows_ref.shape
    for i in range(0, rows, 2):
        tokens = normed(rows_ref[i : i + 2].astype(F32).reshape(2 * width, chans), -1)
        result = dot(values, tokens, NT) * sigmoid(dot(gates, tokens, NT))
        store(i, result[:, :width])
        store(i + 1, result[:, width:])


def right_kernel(n_branch, x_hbm, w_hbm, out_ref, x_ref, w_ref, scr, sems):
    rows, _, chans = x_ref.shape
    devices, per = out_ref.shape[:2]
    groups = chans // per
    near = groups // n_branch
    halves = devices // groups
    copies = [
        pltpu.make_async_copy(w_hbm, w_ref, sems.at[0]),
        pltpu.make_async_copy(x_hbm, x_ref, sems.at[1]),
    ]
    for copy in copies:
        copy.start()
    for copy in copies:
        copy.wait()
    source = lax.broadcasted_iota(jnp.int32, (chans, chans), 0)
    values, gates = channel_order(w_ref[...], (2, 3), source, chans)

    def store(i, block):
        scr[pl.ds(i, chans, stride=rows), :] = block

    gated_rows(values, gates, x_ref, store)
    for q in range(chans):
        g, c = q // per, q % per
        block = scr[q * rows : (q + 1) * rows, :].astype(BF16)
        for h in range(halves):
            out_ref[(g // near * halves + h) * near + g % near, c] = block


def right_operand(x, w, n_branch, devices, per):
    rows, width, chans = x.shape
    hbm = pl.BlockSpec(memory_space=pl.ANY)
    return pl.pallas_call(
        functools.partial(right_kernel, n_branch),
        out_shape=jax.ShapeDtypeStruct((devices, per, rows, width), BF16),
        in_specs=[hbm, hbm],
        out_specs=VMEM,
        scratch_shapes=[
            pltpu.VMEM(x.shape, BF16),
            pltpu.VMEM(w.shape, BF16),
            pltpu.VMEM((chans * rows, width), F32),
            pltpu.SemaphoreType.DMA((2,)),
        ],
        compiler_params=PARAMS,
        cost_estimate=cost(2 * rows * width * chans * 2 * chans, 3 * rows * width * chans * 2),
        name="right_operand",
    )(x, w)


def beside_kernel(
    n_branch, near, where_ref, x_ref, other_ref, w_ref, seq_ref, up_ref, down_ref, factor_ref,
    fresh_ref, *rest
):
    out_refs, (scr, right_scr, left_scr) = rest[:-3], rest[-3:]
    rows, width, chans = x_ref.shape
    branch, row_at = where_ref[0], where_ref[1]
    core = lax.bitwise_and(row_at, 1)
    place = lax.shift_right_logical(lax.bitwise_and(row_at, near - 1), 1)
    count = len(out_refs)
    places = count // n_branch
    per = chans // (n_branch * near)

    x = seq_ref[0].astype(F32)
    hidden = jnp.maximum(dot(normed(x, -1), up_ref[...]), 0.0).astype(BF16)
    fresh = (x + dot(hidden, down_ref[...])).astype(BF16)
    fresh_ref[0] = fresh
    tokens = normed(fresh.astype(F32), -1)
    factor = factor_ref[...]
    depth = factor.shape[1] // 2
    left = dot(tokens, factor[:, :depth]).astype(BF16)
    right = dot(factor[:, depth:], tokens, (((0,), (1,)), ((), ()))).astype(BF16)
    for b in range(n_branch):
        right_scr[b] = right[:, b * width : (b + 1) * width]
    tiles = left.reshape(-1, places, 2, rows, depth)
    for t in range(places):
        left_scr[t] = jnp.concatenate(
            [tiles[h, t, c] for h in range(tiles.shape[0]) for c in range(2)], axis=1
        )

    total = count * per
    q = lax.broadcasted_iota(jnp.int32, (total, chans), 0)
    t = q // per
    group = lax.bitwise_xor(t // places, branch) * near + (
        lax.bitwise_xor(t % places, place) * 2 + core
    )
    values, gates = channel_order(w_ref[...], (0, 1), group * per + q % per, total)

    def store_at(at):
        def store(i, block):
            scr[at, pl.ds(i, total, stride=rows), :] = block

        return store

    gated_rows(values, gates, x_ref, store_at(core))
    gated_rows(values, gates, other_ref, store_at(1 - core))
    for t, out_ref in enumerate(out_refs):
        for c in range(per):
            for k in range(2):
                start = (t * per + c) * rows
                out_ref[pl.ds((c * 2 + k) * rows, rows)] = scr[k, start : start + rows, :].astype(
                    BF16
                )
        base = per * 2 * rows
        out_ref[base : base + depth] = right_scr[lax.bitwise_xor(branch, t // places)]
        out_ref[base + depth :] = left_scr[lax.bitwise_xor(place, t % places)]


def beside(where, x, other, w, seq, up, down, factor, n_branch, near):
    rows, width, chans = x.shape
    _, length, feats = seq.shape
    depth = factor.shape[1] // 2
    places = near // 2
    count = n_branch * places
    per = chans // (n_branch * near)
    piece = jax.ShapeDtypeStruct((per * 2 * rows + depth + rows, width), BF16)
    fresh, *pieces = pl.pallas_call(
        functools.partial(beside_kernel, n_branch, near),
        out_shape=[jax.ShapeDtypeStruct(seq.shape, BF16)] + [piece] * count,
        in_specs=[SMEM] + [VMEM] * 7,
        out_specs=[VMEM] * (1 + count),
        scratch_shapes=[
            pltpu.VMEM((2, count * per * rows, width), F32),
            pltpu.VMEM((n_branch, depth, width), BF16),
            pltpu.VMEM((places, rows, width), BF16),
        ],
        compiler_params=PARAMS,
        cost_estimate=cost(
            4 * length * feats * up.shape[1] + 4 * x.size * 2 * chans, 4 * feats * up.shape[1]
        ),
        name="left_operand_and_msa",
    )(where, x, other, w, seq, up, down, factor)
    return fresh, pieces


def gate_kernel(x_ref, w_ref, out_ref):
    rows, width, chans = x_ref.shape
    tokens = normed(x_ref[...].astype(F32).reshape(rows * width, chans), -1)
    out_ref[...] = sigmoid(dot(tokens, w_ref[:, 4 * chans :])).reshape(rows, width, chans)


def output_gate(x, w):
    rows, width, chans = x.shape
    step = 4
    spec = pl.BlockSpec((step, width, chans), lambda i: (i, 0, 0))
    return pl.pallas_call(
        gate_kernel,
        grid=(rows // step,),
        out_shape=jax.ShapeDtypeStruct(x.shape, F32),
        in_specs=[spec, pl.BlockSpec(w.shape, lambda i: (0, 0))],
        out_specs=spec,
        compiler_params=PARAMS,
        cost_estimate=cost(2 * rows * width * chans * chans, rows * width * chans * 6),
        name="triangle_output_gate",
    )(x, w)


def product_kernel(n_branch, near, where_ref, in_ref, *rest):
    left_refs, (out_ref, left_scr) = rest[:-2], rest[-2:]
    devices, per, rows, width = in_ref.shape
    n_rows = devices // n_branch
    branch, row_at = where_ref[0], where_ref[1]
    place = lax.shift_right_logical(lax.bitwise_and(row_at, near - 1), 1)
    places = near // 2
    for t, ref in enumerate(left_refs):
        b = lax.bitwise_xor(branch, t // places)
        p = lax.bitwise_xor(place, t % places)
        for c in range(per):
            left_scr[b, c, p] = ref[c * 2 * rows : (c + 1) * 2 * rows]
    for c in range(per):
        left = jnp.concatenate(
            [left_scr[b, c].reshape(near * rows, width) for b in range(n_branch)], axis=1
        )
        right = jnp.concatenate(
            [
                in_ref[b * n_rows : (b + 1) * n_rows, c].reshape(n_rows * rows, width)
                for b in range(n_branch)
            ],
            axis=1,
        )
        product = dot(left, right, NT).astype(BF16)
        for b in range(n_branch):
            out_ref[b * near : (b + 1) * near, c] = product[
                :, b * width : (b + 1) * width
            ].reshape(near, rows, width)


def triangle_product(where, received, pieces, n_branch, near):
    devices, per, rows, width = received.shape
    return pl.pallas_call(
        functools.partial(product_kernel, n_branch, near),
        out_shape=jax.ShapeDtypeStruct((n_branch * near, per, rows, width), BF16),
        in_specs=[SMEM] + [VMEM] * (1 + len(pieces)),
        out_specs=VMEM,
        scratch_shapes=[pltpu.VMEM((n_branch, per, near // 2, 2 * rows, width), BF16)],
        compiler_params=PARAMS,
        cost_estimate=cost(
            2 * per * near * rows * received.size // per, received.size * 4
        ),
        name="triangle_product",
    )(where, received, *pieces)


def pair_output_kernel(
    p_ref, x_ref, gate_ref, outer_ref, w_ref, up_ref, down_ref, out_ref, scr
):
    devices, per, rows, width = p_ref.shape
    chans = devices * per
    for g in range(devices):
        for c in range(per):
            scr[pl.ds(g * per + c, rows, stride=chans), :] = p_ref[g, c].astype(F32)
    step = 4
    for i in range(0, rows, step):
        parts = [
            normed(scr[(i + k) * chans : (i + k + 1) * chans, :], 0) for k in range(step)
        ]
        update = dot(jnp.concatenate(parts, axis=1), w_ref[...], TN)
        shape = (step * width, chans)
        x = x_ref[i : i + step].astype(F32).reshape(shape)
        middle = x + gate_ref[i : i + step].reshape(shape) * update
        hidden = jnp.maximum(dot(normed(middle, -1), up_ref[...]), 0.0).astype(BF16)
        result = middle + dot(hidden, down_ref[...]) + outer_ref[i : i + step].reshape(shape)
        out_ref[i : i + step] = result.astype(BF16).reshape(step, width, chans)


def pair_output(product, x, gate, outer, w, up, down):
    devices, per, rows, width = product.shape
    chans = devices * per
    return pl.pallas_call(
        pair_output_kernel,
        out_shape=jax.ShapeDtypeStruct(x.shape, BF16),
        in_specs=[VMEM] * 7,
        out_specs=VMEM,
        scratch_shapes=[pltpu.VMEM((rows * chans, width), F32)],
        compiler_params=PARAMS,
        cost_estimate=cost(2 * x.size * (chans + 2 * up.shape[1]), x.size * 14),
        name="pair_output",
    )(product, x, gate, outer, w, up, down)


def outer_kernel(where_ref, *refs):
    groups, (w_ref, out_ref, right_scr, left_scr, w_scr, m_scr) = refs[:-6], refs[-6:]
    rows, width, chans = out_ref.shape
    total = sum(ref.shape[0] for ref in groups)
    depth = m_scr.shape[1] // total
    s = 0
    for ref in groups:
        for k in range(ref.shape[0]):
            right_scr[pl.ds(s, depth, stride=total), :] = ref[k, :depth].astype(F32)
            left_scr[pl.ds(s, rows, stride=total), :] = ref[k, depth:].astype(F32)
            s += 1
    right = jnp.transpose(right_scr[...]).astype(BF16)
    left = pltpu.roll(left_scr[...], width - where_ref[2] * depth, 1)[:, :depth].astype(BF16)
    w_scr[...] = w_ref[...].astype(F32)
    for d in range(depth):
        part = w_scr[pl.ds(d, depth, stride=depth), :].astype(BF16)
        m_scr[:, d * total : (d + 1) * total] = (
            dot(left, part).astype(BF16).reshape(rows, total, chans)
        )
    for i in range(0, rows, 2):
        pair = jnp.concatenate([m_scr[i], m_scr[i + 1]], axis=1)
        result = dot(right, pair) / total
        out_ref[i] = result[:, :chans]
        out_ref[i + 1] = result[:, chans:]


def outer_update(where, groups, w, rows, chans):
    total = sum(group.shape[0] for group in groups)
    width = groups[0].shape[2]
    depth = groups[0].shape[1] - rows
    return pl.pallas_call(
        outer_kernel,
        out_shape=jax.ShapeDtypeStruct((rows, width, chans), F32),
        in_specs=[SMEM] + [VMEM] * (len(groups) + 1),
        out_specs=VMEM,
        scratch_shapes=[
            pltpu.VMEM((depth * total, width), F32),
            pltpu.VMEM((rows * total, width), F32),
            pltpu.VMEM((depth * depth, chans), F32),
            pltpu.VMEM((rows, depth * total, chans), BF16),
        ],
        compiler_params=PARAMS,
        cost_estimate=cost(2 * rows * width * depth * total * chans * 2, rows * width * chans * 4),
        name="outer_product_mean",
    )(where, *groups, w)


def swap(x, n_branch, n_rows, mask):
    count = n_branch * n_rows
    return lax.ppermute(x, AXES, [(d, d ^ mask) for d in range(count)])


def own_channels_device(
    n_branch,
    n_rows,
    homolog_features,
    pairwise_input,
    transition_expand_matrix,
    transition_contract_matrix,
    factor_pair_matrices,
    outer_output_weight,
    triangle_projection_weight,
    triangle_output_weight,
    pairwise_up_weight,
    pairwise_down_weight,
):
    rows, _, chans = pairwise_input.shape
    near = 8
    halves = n_rows // near
    places = near // 2
    per = chans // (n_branch * near)
    r = lax.axis_index("rows")
    where = jnp.stack([lax.axis_index("branch"), r, r // near * 2 + r % 2]).astype(jnp.int32)

    sent = right_operand(
        pairwise_input, triangle_projection_weight, n_branch, n_branch * n_rows, per
    )
    received = lax.all_to_all(sent, AXES, 0, 0, tiled=True)

    other = swap(pairwise_input, n_branch, n_rows, 1)
    fresh, pieces = beside(
        where,
        pairwise_input,
        other,
        triangle_projection_weight,
        homolog_features,
        transition_expand_matrix,
        transition_contract_matrix,
        factor_pair_matrices,
        n_branch,
        near,
    )
    moved = [
        piece if t == 0 else swap(piece, n_branch, n_rows, t // places * n_rows + t % places * 2)
        for t, piece in enumerate(pieces)
    ]
    groups = [jnp.stack([piece[per * 2 * rows :] for piece in moved])]
    for mask in [1] + [near << k for k in range(halves.bit_length() - 1)]:
        groups += [swap(group, n_branch, n_rows, mask) for group in groups]
    outer = outer_update(where, groups, outer_output_weight, rows, chans)
    gate = output_gate(pairwise_input, triangle_projection_weight)

    product = triangle_product(where, received, moved, n_branch, near)
    members = [
        [b * n_rows + h * near + k for b in range(n_branch) for k in range(near)]
        for h in range(halves)
    ]
    returned = lax.all_to_all(product, AXES, 0, 0, axis_index_groups=members, tiled=True)
    pairwise_output = pair_output(
        returned,
        pairwise_input,
        gate,
        outer,
        triangle_output_weight,
        pairwise_up_weight,
        pairwise_down_weight,
    )
    return (fresh, pairwise_output)


def on_device(n_branch, n_rows, homolog_features, pairwise_input, *weights):
    rows, width, chans = pairwise_input.shape
    near = 8
    halves = n_rows // near
    fits = (
        homolog_features.shape[0] == 1
        and n_branch == 2
        and n_rows % near == 0
        and halves & (halves - 1) == 0
        and chans % (n_branch * near) == 0
        and rows == 16
        and width == 128
        and homolog_features.shape[1] == n_rows * rows == n_branch * width
        and halves * weights[2].shape[1] == width
    )
    if fits:
        return own_channels_device(n_branch, n_rows, homolog_features, pairwise_input, *weights)
    return general_device(homolog_features, pairwise_input, *weights)


def solution(mesh):
    return jax.shard_map(
        functools.partial(on_device, mesh.shape["branch"], mesh.shape["rows"]),
        mesh=mesh,
        in_specs=(
            P(("branch", "rows"), None, None),
            P("rows", "branch", None),
            P(),
            P(),
            P(),
            P(),
            P(),
            P(),
            P(),
            P(),
        ),
        out_specs=(P(("branch", "rows"), None, None), P("rows", "branch", None)),
        check_vma=False,
    )
```

```python
import functools

import jax
import jax.numpy as jnp
from jax import lax
from jax.experimental import pallas as pl
from jax.experimental.pallas import tpu as pltpu
from jax.sharding import PartitionSpec as P

BF16 = jnp.bfloat16
F32 = jnp.float32
AXES = ("branch", "rows")
NT = (((1,), (1,)), ((), ()))
TN = (((0,), (0,)), ((), ()))
VMEM = pl.BlockSpec(memory_space=pltpu.VMEM)
SMEM = pl.BlockSpec(memory_space=pltpu.SMEM)
HBM = pl.BlockSpec(memory_space=pltpu.HBM)
PARAMS = pltpu.CompilerParams(vmem_limit_bytes=48 * 1024 * 1024)

def standardize_features(values, dimension):
    average = jnp.mean(values, axis=dimension, keepdims=True)
    centered = values - average
    variance = jnp.mean(centered * centered, axis=dimension, keepdims=True)
    return centered * lax.rsqrt(variance + 1e-05)


def alignment_branch(
    homolog_features, transition_expand_matrix, transition_contract_matrix, factor_pair_matrices
):
    local_rows, sequence_length, channel_width = homolog_features.shape
    homolog_real_matrix = homolog_features.astype(jnp.float32)
    standardized_homologs = (
        standardize_features(homolog_real_matrix, -1)
        .astype(jnp.bfloat16)
        .reshape(local_rows * sequence_length, channel_width)
    )
    expanded_activations = jax.nn.relu(
        jnp.dot(standardized_homologs, transition_expand_matrix, preferred_element_type=jnp.float32)
    ).astype(jnp.bfloat16)
    refreshed_homolog_features = (
        homolog_real_matrix
        + jnp.dot(
            expanded_activations, transition_contract_matrix, preferred_element_type=jnp.float32
        ).reshape(homolog_features.shape)
    ).astype(jnp.bfloat16)
    standardized_for_factors = (
        standardize_features(refreshed_homolog_features.astype(jnp.float32), -1)
        .astype(jnp.bfloat16)
        .reshape(local_rows * sequence_length, channel_width)
    )
    projected = jnp.dot(
        standardized_for_factors, factor_pair_matrices, preferred_element_type=jnp.float32
    ).reshape(local_rows, sequence_length, -1)
    channels = projected.shape[-1] // 2
    left_side = projected[..., :channels].astype(jnp.bfloat16)
    right_side = jnp.swapaxes(projected[..., channels:].astype(jnp.bfloat16), 1, 2)
    left_pair = lax.all_gather(left_side, "branch", axis=0, tiled=True)
    left_gathered = lax.all_to_all(left_pair, "rows", split_axis=1, concat_axis=0, tiled=True)
    right_pair = lax.all_to_all(right_side, "branch", split_axis=2, concat_axis=0, tiled=True)
    right_gathered = lax.all_gather(right_pair, "rows", axis=0, tiled=True)
    return (refreshed_homolog_features, left_gathered, right_gathered)


def send_whole(tri_left, tri_right):
    return (
        lax.all_to_all(
            lax.all_to_all(tri_left, "branch", split_axis=0, concat_axis=2, tiled=True),
            "rows",
            split_axis=0,
            concat_axis=1,
            tiled=True,
        ),
        lax.all_to_all(
            lax.all_to_all(tri_right, "branch", split_axis=0, concat_axis=2, tiled=True),
            "rows",
            split_axis=0,
            concat_axis=1,
            tiled=True,
        ),
    )


def send_back(product):
    return lax.all_to_all(
        lax.all_to_all(product, "rows", split_axis=1, concat_axis=0, tiled=True),
        "branch",
        split_axis=2,
        concat_axis=0,
        tiled=True,
    )


def pair_branch(
    pairwise_input,
    triangle_projection_weight,
    triangle_output_weight,
    pairwise_up_weight,
    pairwise_down_weight,
):
    tile_rows, columns, chans = pairwise_input.shape
    pair_float = pairwise_input.astype(jnp.float32)
    pair_norm = standardize_features(pair_float, -1).astype(jnp.bfloat16)
    norm_flat = pair_norm.reshape(tile_rows * columns, chans)
    proj_flat = lax.dot_general(
        triangle_projection_weight,
        norm_flat,
        (((0,), (1,)), ((), ())),
        preferred_element_type=jnp.float32,
    )
    proj_tile = proj_flat[: 4 * chans].reshape(4 * chans, tile_rows, columns)
    gate_vals = jax.nn.sigmoid(proj_flat[4 * chans :])
    tri_left = (jax.nn.sigmoid(proj_tile[chans : 2 * chans]) * proj_tile[:chans]).astype(
        jnp.bfloat16
    )
    tri_right = (jax.nn.sigmoid(proj_tile[3 * chans :]) * proj_tile[2 * chans : 3 * chans]).astype(
        jnp.bfloat16
    )
    left_chan, right_chan = send_whole(tri_left, tri_right)
    product = jnp.einsum(
        "cik,cjk->cij", left_chan, right_chan, preferred_element_type=jnp.float32
    ).astype(jnp.bfloat16)
    product_tile = send_back(product)
    prod_norm = (
        standardize_features(product_tile.astype(jnp.float32), 0)
        .astype(jnp.bfloat16)
        .reshape(chans, tile_rows * columns)
    )
    tri_update = lax.dot_general(
        triangle_output_weight,
        prod_norm,
        (((0,), (0,)), ((), ())),
        preferred_element_type=jnp.float32,
    )
    gated_update = jnp.transpose(gate_vals * tri_update).reshape(tile_rows, columns, chans)
    pair_mid = pair_float + gated_update
    mid_norm = standardize_features(pair_mid, -1).astype(jnp.bfloat16)
    pair_hidden = jax.nn.relu(
        jnp.einsum("ijd,dh->ijh", mid_norm, pairwise_up_weight, preferred_element_type=jnp.float32)
    ).astype(jnp.bfloat16)
    return pair_mid + jnp.einsum(
        "ijh,hd->ijd", pair_hidden, pairwise_down_weight, preferred_element_type=jnp.float32
    )


def outer_product(left_gathered, right_gathered, outer_output_weight):
    total_rows, tile_rows, channels = left_gathered.shape
    columns = right_gathered.shape[2]
    span_cols = 128
    left_flat = left_gathered.reshape(total_rows, tile_rows * channels)
    pieces = []
    for offset in range(0, columns, span_cols):
        right_piece = right_gathered[:, :, offset : offset + span_cols].reshape(
            total_rows, channels * span_cols
        )
        outer_vals = lax.dot_general(
            left_flat, right_piece, (((0,), (0,)), ((), ())), preferred_element_type=jnp.float32
        )
        outer_vals = (
            (outer_vals / total_rows)
            .astype(jnp.bfloat16)
            .reshape(tile_rows, channels * channels, span_cols)
        )
        pieces.append(
            lax.dot_general(
                outer_output_weight,
                outer_vals,
                (((0,), (1,)), ((), ())),
                preferred_element_type=jnp.float32,
            )
        )
    outer_eij = jnp.concatenate(pieces, axis=2)
    return jnp.transpose(outer_eij, (1, 2, 0))


def general_device(
    homolog_features,
    pairwise_input,
    transition_expand_matrix,
    transition_contract_matrix,
    factor_pair_matrices,
    outer_output_weight,
    triangle_projection_weight,
    triangle_output_weight,
    pairwise_up_weight,
    pairwise_down_weight,
):
    refreshed_homolog_features, left_gathered, right_gathered = alignment_branch(
        homolog_features, transition_expand_matrix, transition_contract_matrix, factor_pair_matrices
    )
    pair_mid = pair_branch(
        pairwise_input,
        triangle_projection_weight,
        triangle_output_weight,
        pairwise_up_weight,
        pairwise_down_weight,
    )
    outer_update = outer_product(left_gathered, right_gathered, outer_output_weight)
    pairwise_output = (pair_mid + outer_update).astype(jnp.bfloat16)
    return (refreshed_homolog_features, pairwise_output)


def normed(values, axis):
    average = jnp.mean(values, axis=axis, keepdims=True)
    centered = values - average
    variance = jnp.mean(centered * centered, axis=axis, keepdims=True)
    return (centered * lax.rsqrt(variance + 1e-05)).astype(BF16)


def sigmoid(values):
    return 0.5 * jnp.tanh(0.5 * values) + 0.5


def dot(a, b, dims=(((1,), (0,)), ((), ()))):
    return lax.dot_general(a, b, dims, preferred_element_type=F32)


def cost(flops, nbytes, transcendentals=0):
    return pl.CostEstimate(flops=flops, bytes_accessed=nbytes, transcendentals=transcendentals)


def channel_order(w, sides, source, count):
    chans = w.shape[0]
    col = lax.broadcasted_iota(jnp.int32, (count, chans), 1)
    order = jnp.where(col == source, 1.0, 0.0).astype(BF16)
    return [dot(order, w[:, s * chans : (s + 1) * chans], NT).astype(BF16) for s in sides]


def gated_rows(values, gates, rows_ref, store):
    rows, width, chans = rows_ref.shape
    for i in range(0, rows, 2):
        tokens = normed(rows_ref[i : i + 2].astype(F32).reshape(2 * width, chans), -1)
        result = dot(values, tokens, NT) * sigmoid(dot(gates, tokens, NT))
        store(i, result[:, :width])
        store(i + 1, result[:, width:])


def right_kernel(n_branch, x_ref, w_ref, out_ref, scr):
    rows, _, chans = x_ref.shape
    devices, per = out_ref.shape[:2]
    groups = chans // per
    near = groups // n_branch
    halves = devices // groups
    source = lax.broadcasted_iota(jnp.int32, (chans, chans), 0)
    values, gates = channel_order(w_ref[...], (2, 3), source, chans)

    def store(i, block):
        scr[pl.ds(i, chans, stride=rows), :] = block

    gated_rows(values, gates, x_ref, store)
    for q in range(chans):
        g, c = q // per, q % per
        block = scr[q * rows : (q + 1) * rows, :].astype(BF16)
        for h in range(halves):
            out_ref[(g // near * halves + h) * near + g % near, c] = block


def right_operand(x, w, n_branch, devices, per):
    rows, width, chans = x.shape
    return pl.pallas_call(
        functools.partial(right_kernel, n_branch),
        out_shape=jax.ShapeDtypeStruct((devices, per, rows, width), BF16),
        in_specs=[VMEM, VMEM],
        out_specs=VMEM,
        scratch_shapes=[pltpu.VMEM((chans * rows, width), F32)],
        compiler_params=PARAMS,
        cost_estimate=cost(2 * rows * width * chans * 2 * chans, 3 * rows * width * chans * 2),
        name="right_operand",
    )(x, w)


def msa_kernel(
    n_branch, near, x_hbm, up_hbm, down_hbm, factor_ref, fresh_ref, right_ref, left_ref,
    x_ref, up_ref, down_ref, sems
):
    pairs = [(x_hbm, x_ref), (up_hbm, up_ref), (down_hbm, down_ref)]
    copies = [pltpu.make_async_copy(a, b, sems.at[k]) for k, (a, b) in enumerate(pairs)]
    for copy in copies:
        copy.start()
    copies[0].wait()
    x = x_ref[0].astype(F32)
    tokens = normed(x, -1)
    copies[1].wait()
    hidden = jnp.maximum(dot(tokens, up_ref[...]), 0.0).astype(BF16)
    copies[2].wait()
    fresh = (x + dot(hidden, down_ref[...])).astype(BF16)
    fresh_ref[0] = fresh
    tokens = normed(fresh.astype(F32), -1)
    factor = factor_ref[...]
    depth = factor.shape[1] // 2
    left = dot(tokens, factor[:, :depth]).astype(BF16)
    right = dot(factor[:, depth:], tokens, (((0,), (1,)), ((), ()))).astype(BF16)
    width = right_ref.shape[2]
    for b in range(n_branch):
        right_ref[b] = right[:, b * width : (b + 1) * width]
    halves, places, rows, _ = left_ref.shape
    tiles = left.reshape(halves, places, 2, rows, depth)
    blank = jnp.zeros((rows, width - 2 * depth), BF16)
    for h in range(halves):
        for t in range(places):
            left_ref[h, t] = jnp.concatenate([tiles[h, t, 0], tiles[h, t, 1], blank], axis=1)


def msa(x, up, down, factor, n_branch, near, halves, rows):
    _, length, feats = x.shape
    depth = factor.shape[1] // 2
    width = length // n_branch
    return pl.pallas_call(
        functools.partial(msa_kernel, n_branch, near),
        out_shape=[
            jax.ShapeDtypeStruct(x.shape, BF16),
            jax.ShapeDtypeStruct((n_branch, depth, width), BF16),
            jax.ShapeDtypeStruct((halves, near // 2, rows, width), BF16),
        ],
        in_specs=[HBM] * 3 + [VMEM],
        out_specs=[VMEM] * 3,
        scratch_shapes=[
            pltpu.VMEM(x.shape, BF16),
            pltpu.VMEM(up.shape, BF16),
            pltpu.VMEM(down.shape, BF16),
            pltpu.SemaphoreType.DMA((3,)),
        ],
        compiler_params=PARAMS,
        cost_estimate=cost(4 * length * feats * up.shape[1], 4 * feats * up.shape[1]),
        name="msa_transition",
    )(x, up, down, factor)


def beside_kernel(
    n_branch, near, where_ref, x_ref, other_ref, w_ref, right_ref, left_ref, far_right_ref,
    far_left_ref, *rest
):
    out_refs, scr = rest[:-1], rest[-1]
    rows, _, chans = x_ref.shape
    branch, row_at = where_ref[0], where_ref[1]
    core = lax.bitwise_and(row_at, 1)
    place = lax.shift_right_logical(lax.bitwise_and(row_at, near - 1), 1)
    half = row_at // near
    count = len(out_refs)
    places = count // n_branch
    per = chans // (n_branch * near)

    total = count * per
    q = lax.broadcasted_iota(jnp.int32, (total, chans), 0)
    t = q // per
    group = lax.bitwise_xor(t // places, branch) * near + (
        lax.bitwise_xor(t % places, place) * 2 + core
    )
    values, gates = channel_order(w_ref[...], (0, 1), group * per + q % per, total)

    def store_at(at):
        def store(i, block):
            scr[at, pl.ds(i, total, stride=rows), :] = block

        return store

    gated_rows(values, gates, x_ref, store_at(core))
    gated_rows(values, gates, other_ref, store_at(1 - core))
    depth = right_ref.shape[1]
    base = per * 2 * rows
    for t, out_ref in enumerate(out_refs):
        for c in range(per):
            for k in range(2):
                start = (t * per + c) * rows
                out_ref[pl.ds((c * 2 + k) * rows, rows)] = scr[k, start : start + rows, :].astype(
                    BF16
                )
        b = lax.bitwise_xor(branch, t // places)
        p = lax.bitwise_xor(place, t % places)
        out_ref[base : base + depth] = right_ref[b]
        out_ref[base + depth : base + 2 * depth] = far_right_ref[b]
        out_ref[base + 2 * depth :] = jnp.concatenate(
            [left_ref[half, p][:, : 2 * depth], far_left_ref[half, p][:, : 2 * depth]], axis=1
        )


def beside(where, x, other, w, sides, far_sides, n_branch, near):
    rows, width, chans = x.shape
    depth = sides[0].shape[1]
    count = n_branch * near // 2
    per = chans // (n_branch * near)
    piece = jax.ShapeDtypeStruct((per * 2 * rows + 2 * depth + rows, width), BF16)
    return pl.pallas_call(
        functools.partial(beside_kernel, n_branch, near),
        out_shape=[piece] * count,
        in_specs=[SMEM] + [VMEM] * 7,
        out_specs=[VMEM] * count,
        scratch_shapes=[pltpu.VMEM((2, count * per * rows, width), F32)],
        compiler_params=PARAMS,
        cost_estimate=cost(4 * x.size * 2 * chans, x.size * 8),
        name="left_operand",
    )(where, x, other, w, *sides, *far_sides)


def gate_kernel(x_ref, w_ref, out_ref):
    rows, width, chans = x_ref.shape
    tokens = normed(x_ref[...].astype(F32).reshape(rows * width, chans), -1)
    out_ref[...] = sigmoid(dot(tokens, w_ref[:, 4 * chans :])).reshape(rows, width, chans)


def output_gate(x, w):
    rows, width, chans = x.shape
    step = 4
    spec = pl.BlockSpec((step, width, chans), lambda i: (i, 0, 0))
    return pl.pallas_call(
        gate_kernel,
        grid=(rows // step,),
        out_shape=jax.ShapeDtypeStruct(x.shape, F32),
        in_specs=[spec, pl.BlockSpec(w.shape, lambda i: (0, 0))],
        out_specs=spec,
        compiler_params=PARAMS,
        cost_estimate=cost(2 * rows * width * chans * chans, rows * width * chans * 6),
        name="triangle_output_gate",
    )(x, w)


def product_kernel(n_branch, near, where_ref, in_ref, *rest):
    left_refs, (out_ref, left_scr) = rest[:-2], rest[-2:]
    devices, per, rows, width = in_ref.shape
    n_rows = devices // n_branch
    branch, row_at = where_ref[0], where_ref[1]
    place = lax.shift_right_logical(lax.bitwise_and(row_at, near - 1), 1)
    places = near // 2
    for t, ref in enumerate(left_refs):
        b = lax.bitwise_xor(branch, t // places)
        p = lax.bitwise_xor(place, t % places)
        for c in range(per):
            left_scr[b, c, p] = ref[c * 2 * rows : (c + 1) * 2 * rows]
    for c in range(per):
        left = jnp.concatenate(
            [left_scr[b, c].reshape(near * rows, width) for b in range(n_branch)], axis=1
        )
        right = jnp.concatenate(
            [
                in_ref[b * n_rows : (b + 1) * n_rows, c].reshape(n_rows * rows, width)
                for b in range(n_branch)
            ],
            axis=1,
        )
        product = dot(left, right, NT).astype(BF16)
        for b in range(n_branch):
            out_ref[b * near : (b + 1) * near, c] = product[
                :, b * width : (b + 1) * width
            ].reshape(near, rows, width)


def triangle_product(where, received, pieces, n_branch, near):
    devices, per, rows, width = received.shape
    return pl.pallas_call(
        functools.partial(product_kernel, n_branch, near),
        out_shape=jax.ShapeDtypeStruct((n_branch * near, per, rows, width), BF16),
        in_specs=[SMEM] + [VMEM] * (1 + len(pieces)),
        out_specs=VMEM,
        scratch_shapes=[pltpu.VMEM((n_branch, per, near // 2, 2 * rows, width), BF16)],
        compiler_params=PARAMS,
        cost_estimate=cost(
            2 * per * near * rows * received.size // per, received.size * 4
        ),
        name="triangle_product",
    )(where, received, *pieces)


def pair_output_kernel(
    p_ref, x_ref, gate_ref, outer_ref, w_ref, up_ref, down_ref, out_ref, scr
):
    devices, per, rows, width = p_ref.shape
    chans = devices * per
    for g in range(devices):
        for c in range(per):
            scr[pl.ds(g * per + c, rows, stride=chans), :] = p_ref[g, c].astype(F32)
    step = 4
    for i in range(0, rows, step):
        parts = [
            normed(scr[(i + k) * chans : (i + k + 1) * chans, :], 0) for k in range(step)
        ]
        update = dot(jnp.concatenate(parts, axis=1), w_ref[...], TN)
        shape = (step * width, chans)
        x = x_ref[i : i + step].astype(F32).reshape(shape)
        middle = x + gate_ref[i : i + step].reshape(shape) * update
        hidden = jnp.maximum(dot(normed(middle, -1), up_ref[...]), 0.0).astype(BF16)
        result = middle + dot(hidden, down_ref[...]) + outer_ref[i : i + step].reshape(shape)
        out_ref[i : i + step] = result.astype(BF16).reshape(step, width, chans)


def pair_output(product, x, gate, outer, w, up, down):
    devices, per, rows, width = product.shape
    chans = devices * per
    return pl.pallas_call(
        pair_output_kernel,
        out_shape=jax.ShapeDtypeStruct(x.shape, BF16),
        in_specs=[VMEM] * 7,
        out_specs=VMEM,
        scratch_shapes=[pltpu.VMEM((rows * chans, width), F32)],
        compiler_params=PARAMS,
        cost_estimate=cost(2 * x.size * (chans + 2 * up.shape[1]), x.size * 14),
        name="pair_output",
    )(product, x, gate, outer, w, up, down)


def outer_kernel(where_ref, *refs):
    groups, (w_ref, out_ref, right_scr, left_scr, w_scr, m_scr) = refs[:-6], refs[-6:]
    rows, width, chans = out_ref.shape
    total = 2 * sum(ref.shape[0] for ref in groups)
    depth = m_scr.shape[1] // total
    s = 0
    for ref in groups:
        for k in range(ref.shape[0]):
            both = ref[k, 2 * depth :].astype(F32)
            for far in range(2):
                at = s + far * (total // 2)
                side = ref[k, far * depth : (far + 1) * depth].astype(F32)
                right_scr[pl.ds(at, depth, stride=total), :] = side
                left_scr[pl.ds(at, rows, stride=total), :] = both
            s += 1
    right = jnp.transpose(right_scr[...]).astype(BF16)
    both = left_scr[...]
    shift = lax.bitwise_and(where_ref[1], 1) * depth
    first = pltpu.roll(both, width - shift, 1)[:, :depth]
    second = pltpu.roll(both, width - 2 * depth - shift, 1)[:, :depth]
    row = lax.broadcasted_iota(jnp.int32, first.shape, 0)
    left = jnp.where(row % total < total // 2, first, second).astype(BF16)
    w_scr[...] = w_ref[...].astype(F32)
    for d in range(depth):
        part = w_scr[pl.ds(d, depth, stride=depth), :].astype(BF16)
        m_scr[:, d * total : (d + 1) * total] = (
            dot(left, part).astype(BF16).reshape(rows, total, chans)
        )
    for i in range(0, rows, 2):
        pair = jnp.concatenate([m_scr[i], m_scr[i + 1]], axis=1)
        result = dot(right, pair) / total
        out_ref[i] = result[:, :chans]
        out_ref[i + 1] = result[:, chans:]


def outer_update(where, groups, w, rows, chans):
    total = 2 * sum(group.shape[0] for group in groups)
    width = groups[0].shape[2]
    depth = (groups[0].shape[1] - rows) // 2
    return pl.pallas_call(
        outer_kernel,
        out_shape=jax.ShapeDtypeStruct((rows, width, chans), F32),
        in_specs=[SMEM] + [VMEM] * (len(groups) + 1),
        out_specs=VMEM,
        scratch_shapes=[
            pltpu.VMEM((depth * total, width), F32),
            pltpu.VMEM((rows * total, width), F32),
            pltpu.VMEM((depth * depth, chans), F32),
            pltpu.VMEM((rows, depth * total, chans), BF16),
        ],
        compiler_params=PARAMS,
        cost_estimate=cost(2 * rows * width * depth * total * chans * 2, rows * width * chans * 4),
        name="outer_product_mean",
    )(where, *groups, w)


def swap(x, n_branch, n_rows, mask):
    count = n_branch * n_rows
    return lax.ppermute(x, AXES, [(d, d ^ mask) for d in range(count)])


def own_channels_device(
    n_branch,
    n_rows,
    homolog_features,
    pairwise_input,
    transition_expand_matrix,
    transition_contract_matrix,
    factor_pair_matrices,
    outer_output_weight,
    triangle_projection_weight,
    triangle_output_weight,
    pairwise_up_weight,
    pairwise_down_weight,
):
    rows, _, chans = pairwise_input.shape
    near = 8
    halves = n_rows // near
    places = near // 2
    per = chans // (n_branch * near)
    where = jnp.stack([lax.axis_index("branch"), lax.axis_index("rows")]).astype(jnp.int32)

    fresh, *sides = msa(
        homolog_features,
        transition_expand_matrix,
        transition_contract_matrix,
        factor_pair_matrices,
        n_branch,
        near,
        halves,
        rows,
    )
    pairwise_input, sides = lax.optimization_barrier((pairwise_input, sides))
    far_sides = [swap(side, n_branch, n_rows, near) for side in sides]
    sent = right_operand(
        pairwise_input, triangle_projection_weight, n_branch, n_branch * n_rows, per
    )
    received = lax.all_to_all(sent, AXES, 0, 0, tiled=True)

    other = swap(pairwise_input, n_branch, n_rows, 1)
    pieces = beside(
        where, pairwise_input, other, triangle_projection_weight, sides, far_sides, n_branch, near
    )
    moved = [
        piece if t == 0 else swap(piece, n_branch, n_rows, t // places * n_rows + t % places * 2)
        for t, piece in enumerate(pieces)
    ]
    mine = jnp.stack([piece[per * 2 * rows :] for piece in moved])
    groups = [mine, swap(mine, n_branch, n_rows, 1)]
    outer = outer_update(where, groups, outer_output_weight, rows, chans)
    gate = output_gate(pairwise_input, triangle_projection_weight)

    product = triangle_product(where, received, moved, n_branch, near)
    members = [
        [b * n_rows + h * near + k for b in range(n_branch) for k in range(near)]
        for h in range(halves)
    ]
    returned = lax.all_to_all(product, AXES, 0, 0, axis_index_groups=members, tiled=True)
    pairwise_output = pair_output(
        returned,
        pairwise_input,
        gate,
        outer,
        triangle_output_weight,
        pairwise_up_weight,
        pairwise_down_weight,
    )
    return (fresh, pairwise_output)


def on_device(n_branch, n_rows, homolog_features, pairwise_input, *weights):
    rows, width, chans = pairwise_input.shape
    near = 8
    halves = n_rows // near
    fits = (
        homolog_features.shape[0] == 1
        and halves == 2
        and n_branch == 2
        and n_rows % near == 0
        and chans % (n_branch * near) == 0
        and rows == 16
        and width == 128
        and homolog_features.shape[1] == n_rows * rows == n_branch * width
        and 2 * weights[2].shape[1] == width
    )
    if fits:
        return own_channels_device(n_branch, n_rows, homolog_features, pairwise_input, *weights)
    return general_device(homolog_features, pairwise_input, *weights)


def solution(mesh):
    return jax.shard_map(
        functools.partial(on_device, mesh.shape["branch"], mesh.shape["rows"]),
        mesh=mesh,
        in_specs=(
            P(("branch", "rows"), None, None),
            P("rows", "branch", None),
            P(),
            P(),
            P(),
            P(),
            P(),
            P(),
            P(),
            P(),
        ),
        out_specs=(P(("branch", "rows"), None, None), P("rows", "branch", None)),
        check_vma=False,
    )
```

```python
import functools

import jax
import jax.numpy as jnp
from jax import lax
from jax.experimental import pallas as pl
from jax.experimental.pallas import tpu as pltpu
from jax.sharding import PartitionSpec as P

BF16 = jnp.bfloat16
F32 = jnp.float32
AXES = ("branch", "rows")
NT = (((1,), (1,)), ((), ()))
TN = (((0,), (0,)), ((), ()))
VMEM = pl.BlockSpec(memory_space=pltpu.VMEM)
SMEM = pl.BlockSpec(memory_space=pltpu.SMEM)
TARGETS = (0, 1, 4, 7, 3, 6, 2, 5)
HBM = pl.BlockSpec(memory_space=pltpu.HBM)
PARAMS = pltpu.CompilerParams(vmem_limit_bytes=48 * 1024 * 1024)

def standardize_features(values, dimension):
    average = jnp.mean(values, axis=dimension, keepdims=True)
    centered = values - average
    variance = jnp.mean(centered * centered, axis=dimension, keepdims=True)
    return centered * lax.rsqrt(variance + 1e-05)


def alignment_branch(
    homolog_features, transition_expand_matrix, transition_contract_matrix, factor_pair_matrices
):
    local_rows, sequence_length, channel_width = homolog_features.shape
    homolog_real_matrix = homolog_features.astype(jnp.float32)
    standardized_homologs = (
        standardize_features(homolog_real_matrix, -1)
        .astype(jnp.bfloat16)
        .reshape(local_rows * sequence_length, channel_width)
    )
    expanded_activations = jax.nn.relu(
        jnp.dot(standardized_homologs, transition_expand_matrix, preferred_element_type=jnp.float32)
    ).astype(jnp.bfloat16)
    refreshed_homolog_features = (
        homolog_real_matrix
        + jnp.dot(
            expanded_activations, transition_contract_matrix, preferred_element_type=jnp.float32
        ).reshape(homolog_features.shape)
    ).astype(jnp.bfloat16)
    standardized_for_factors = (
        standardize_features(refreshed_homolog_features.astype(jnp.float32), -1)
        .astype(jnp.bfloat16)
        .reshape(local_rows * sequence_length, channel_width)
    )
    projected = jnp.dot(
        standardized_for_factors, factor_pair_matrices, preferred_element_type=jnp.float32
    ).reshape(local_rows, sequence_length, -1)
    channels = projected.shape[-1] // 2
    left_side = projected[..., :channels].astype(jnp.bfloat16)
    right_side = jnp.swapaxes(projected[..., channels:].astype(jnp.bfloat16), 1, 2)
    left_pair = lax.all_gather(left_side, "branch", axis=0, tiled=True)
    left_gathered = lax.all_to_all(left_pair, "rows", split_axis=1, concat_axis=0, tiled=True)
    right_pair = lax.all_to_all(right_side, "branch", split_axis=2, concat_axis=0, tiled=True)
    right_gathered = lax.all_gather(right_pair, "rows", axis=0, tiled=True)
    return (refreshed_homolog_features, left_gathered, right_gathered)


def send_whole(tri_left, tri_right):
    return (
        lax.all_to_all(
            lax.all_to_all(tri_left, "branch", split_axis=0, concat_axis=2, tiled=True),
            "rows",
            split_axis=0,
            concat_axis=1,
            tiled=True,
        ),
        lax.all_to_all(
            lax.all_to_all(tri_right, "branch", split_axis=0, concat_axis=2, tiled=True),
            "rows",
            split_axis=0,
            concat_axis=1,
            tiled=True,
        ),
    )


def send_back(product):
    return lax.all_to_all(
        lax.all_to_all(product, "rows", split_axis=1, concat_axis=0, tiled=True),
        "branch",
        split_axis=2,
        concat_axis=0,
        tiled=True,
    )


def pair_branch(
    pairwise_input,
    triangle_projection_weight,
    triangle_output_weight,
    pairwise_up_weight,
    pairwise_down_weight,
):
    tile_rows, columns, chans = pairwise_input.shape
    pair_float = pairwise_input.astype(jnp.float32)
    pair_norm = standardize_features(pair_float, -1).astype(jnp.bfloat16)
    norm_flat = pair_norm.reshape(tile_rows * columns, chans)
    proj_flat = lax.dot_general(
        triangle_projection_weight,
        norm_flat,
        (((0,), (1,)), ((), ())),
        preferred_element_type=jnp.float32,
    )
    proj_tile = proj_flat[: 4 * chans].reshape(4 * chans, tile_rows, columns)
    gate_vals = jax.nn.sigmoid(proj_flat[4 * chans :])
    tri_left = (jax.nn.sigmoid(proj_tile[chans : 2 * chans]) * proj_tile[:chans]).astype(
        jnp.bfloat16
    )
    tri_right = (jax.nn.sigmoid(proj_tile[3 * chans :]) * proj_tile[2 * chans : 3 * chans]).astype(
        jnp.bfloat16
    )
    left_chan, right_chan = send_whole(tri_left, tri_right)
    product = jnp.einsum(
        "cik,cjk->cij", left_chan, right_chan, preferred_element_type=jnp.float32
    ).astype(jnp.bfloat16)
    product_tile = send_back(product)
    prod_norm = (
        standardize_features(product_tile.astype(jnp.float32), 0)
        .astype(jnp.bfloat16)
        .reshape(chans, tile_rows * columns)
    )
    tri_update = lax.dot_general(
        triangle_output_weight,
        prod_norm,
        (((0,), (0,)), ((), ())),
        preferred_element_type=jnp.float32,
    )
    gated_update = jnp.transpose(gate_vals * tri_update).reshape(tile_rows, columns, chans)
    pair_mid = pair_float + gated_update
    mid_norm = standardize_features(pair_mid, -1).astype(jnp.bfloat16)
    pair_hidden = jax.nn.relu(
        jnp.einsum("ijd,dh->ijh", mid_norm, pairwise_up_weight, preferred_element_type=jnp.float32)
    ).astype(jnp.bfloat16)
    return pair_mid + jnp.einsum(
        "ijh,hd->ijd", pair_hidden, pairwise_down_weight, preferred_element_type=jnp.float32
    )


def outer_product(left_gathered, right_gathered, outer_output_weight):
    total_rows, tile_rows, channels = left_gathered.shape
    columns = right_gathered.shape[2]
    span_cols = 128
    left_flat = left_gathered.reshape(total_rows, tile_rows * channels)
    pieces = []
    for offset in range(0, columns, span_cols):
        right_piece = right_gathered[:, :, offset : offset + span_cols].reshape(
            total_rows, channels * span_cols
        )
        outer_vals = lax.dot_general(
            left_flat, right_piece, (((0,), (0,)), ((), ())), preferred_element_type=jnp.float32
        )
        outer_vals = (
            (outer_vals / total_rows)
            .astype(jnp.bfloat16)
            .reshape(tile_rows, channels * channels, span_cols)
        )
        pieces.append(
            lax.dot_general(
                outer_output_weight,
                outer_vals,
                (((0,), (1,)), ((), ())),
                preferred_element_type=jnp.float32,
            )
        )
    outer_eij = jnp.concatenate(pieces, axis=2)
    return jnp.transpose(outer_eij, (1, 2, 0))


def general_device(
    homolog_features,
    pairwise_input,
    transition_expand_matrix,
    transition_contract_matrix,
    factor_pair_matrices,
    outer_output_weight,
    triangle_projection_weight,
    triangle_output_weight,
    pairwise_up_weight,
    pairwise_down_weight,
):
    refreshed_homolog_features, left_gathered, right_gathered = alignment_branch(
        homolog_features, transition_expand_matrix, transition_contract_matrix, factor_pair_matrices
    )
    pair_mid = pair_branch(
        pairwise_input,
        triangle_projection_weight,
        triangle_output_weight,
        pairwise_up_weight,
        pairwise_down_weight,
    )
    outer_update = outer_product(left_gathered, right_gathered, outer_output_weight)
    pairwise_output = (pair_mid + outer_update).astype(jnp.bfloat16)
    return (refreshed_homolog_features, pairwise_output)


def normed(values, axis):
    average = jnp.mean(values, axis=axis, keepdims=True)
    centered = values - average
    variance = jnp.mean(centered * centered, axis=axis, keepdims=True)
    return (centered * lax.rsqrt(variance + 1e-05)).astype(BF16)


def sigmoid(values):
    return 0.5 * jnp.tanh(0.5 * values) + 0.5


def dot(a, b, dims=(((1,), (0,)), ((), ()))):
    return lax.dot_general(a, b, dims, preferred_element_type=F32)


def cost(flops, nbytes, transcendentals=0):
    return pl.CostEstimate(flops=flops, bytes_accessed=nbytes, transcendentals=transcendentals)


def channel_order(w, sides, source, count):
    chans = w.shape[0]
    col = lax.broadcasted_iota(jnp.int32, (count, chans), 1)
    order = jnp.where(col == source, 1.0, 0.0).astype(BF16)
    return [dot(order, w[:, s * chans : (s + 1) * chans], NT).astype(BF16) for s in sides]


def gated_rows(values, gates, rows_ref, store):
    rows, width, chans = rows_ref.shape
    for i in range(0, rows, 2):
        tokens = rows_ref[i : i + 2].reshape(2 * width, chans)
        result = dot(values, tokens, NT) * sigmoid(dot(gates, tokens, NT))
        store(i, result[:, :width])
        store(i + 1, result[:, width:])


def fill_right(n_branch, tokens_ref, w, out_ref, scr):
    rows, _, chans = tokens_ref.shape
    devices, per = out_ref.shape[:2]
    groups = chans // per
    near = groups // n_branch
    halves = devices // groups
    own = lax.broadcasted_iota(jnp.int32, (chans, chans), 0)
    values, gates = channel_order(w, (2, 3), own, chans)

    def store(i, block):
        scr[pl.ds(i, chans, stride=rows), :] = block

    gated_rows(values, gates, tokens_ref, store)
    for q in range(chans):
        g, c = q // per, q % per
        block = scr[q * rows : (q + 1) * rows, :].astype(BF16)
        for h in range(halves):
            out_ref[(g // near * halves + h) * near + g % near, c] = block


def right_kernel(
    n_branch, x_hbm, w_hbm, sent_hbm, tokens_hbm, x_ref, w_ref, sent_ref, tokens_ref, scr, sems
):
    rows = x_ref.shape[0]
    step = rows // 4
    copies = [pltpu.make_async_copy(w_hbm, w_ref, sems.at[0])]
    for k in range(4):
        part = pl.ds(k * step, step)
        copies.append(pltpu.make_async_copy(x_hbm.at[part], x_ref.at[part], sems.at[k + 1]))
    for copy in copies:
        copy.start()
    for k in range(4):
        copies[k + 1].wait()
        part = slice(k * step, (k + 1) * step)
        tokens_ref[part] = normed(x_ref[part].astype(F32), -1)
    copies[0].wait()
    keep = pltpu.make_async_copy(tokens_ref, tokens_hbm, sems.at[5])
    keep.start()
    fill_right(n_branch, tokens_ref, w_ref[...], sent_ref, scr)
    send = pltpu.make_async_copy(sent_ref, sent_hbm, sems.at[6])
    send.start()
    keep.wait()
    send.wait()


def right_operand(x, w, n_branch, devices, per):
    rows, width, chans = x.shape
    sent = jax.ShapeDtypeStruct((devices, per, rows, width), BF16)
    return pl.pallas_call(
        functools.partial(right_kernel, n_branch),
        out_shape=[sent, jax.ShapeDtypeStruct(x.shape, BF16)],
        in_specs=[HBM] * 2,
        out_specs=[HBM] * 2,
        scratch_shapes=[pltpu.VMEM(array.shape, BF16) for array in (x, w, sent, x)]
        + [pltpu.VMEM((chans * rows, width), F32), pltpu.SemaphoreType.DMA((7,))],
        cost_estimate=cost(2 * rows * width * chans * 2 * chans, 3 * rows * width * chans * 2),
        name="right_operand",
    )(x, w)


def msa_kernel(
    n_branch, rows, seq_hbm, up_hbm, down_hbm, factor_hbm, fresh_ref, sides_ref,
    seq_ref, up_ref, down_ref, factor_ref, sems
):
    pairs = [
        (seq_hbm, seq_ref),
        (up_hbm, up_ref),
        (down_hbm, down_ref),
        (factor_hbm, factor_ref),
    ]
    copies = [pltpu.make_async_copy(a, b, sems.at[k]) for k, (a, b) in enumerate(pairs)]
    for copy in copies:
        copy.start()
    copies[0].wait()
    x = seq_ref[0].astype(F32)
    tokens = normed(x, -1)
    copies[1].wait()
    hidden = jnp.maximum(dot(tokens, up_ref[...]), 0.0).astype(BF16)
    copies[2].wait()
    fresh = (x + dot(hidden, down_ref[...])).astype(BF16)
    fresh_ref[0] = fresh
    tokens = normed(fresh.astype(F32), -1)
    copies[3].wait()
    factor = factor_ref[...]
    depth = factor.shape[0] // 2
    left = dot(tokens, factor[:depth], NT).astype(BF16)
    right = dot(factor[depth:], tokens, NT).astype(BF16)
    width = sides_ref.shape[1]
    for b in range(n_branch):
        sides_ref[b * depth : (b + 1) * depth] = right[:, b * width : (b + 1) * width]
    tiles = left.reshape(-1, 2, rows, depth)
    blank = jnp.zeros((rows, width - 2 * depth), BF16)
    base = n_branch * depth
    for t in range(tiles.shape[0]):
        sides_ref[base + t * rows : base + (t + 1) * rows] = jnp.concatenate(
            [tiles[t, 0], tiles[t, 1], blank], axis=1
        )


def msa(seq, up, down, factor, rows, width):
    _, length, feats = seq.shape
    depth = factor.shape[0] // 2
    n_branch = length // width
    operands = (seq, up, down, factor)
    return pl.pallas_call(
        functools.partial(msa_kernel, n_branch, rows),
        out_shape=[
            jax.ShapeDtypeStruct(seq.shape, BF16),
            jax.ShapeDtypeStruct((n_branch * depth + length // 2, width), BF16),
        ],
        in_specs=[HBM] * 4,
        out_specs=[VMEM] * 2,
        scratch_shapes=[pltpu.VMEM(array.shape, BF16) for array in operands]
        + [pltpu.SemaphoreType.DMA((4,))],
        cost_estimate=cost(4 * length * feats * up.shape[1], 4 * feats * up.shape[1]),
        name="msa_transition",
    )(*operands)


def beside_kernel(
    n_branch, near, where_ref, x_ref, other_ref, w_ref, sides_ref, far_ref, *rest
):
    out_refs, scr = rest[:-1], rest[-1]
    rows, _, chans = x_ref.shape
    branch, row_at = where_ref[0], where_ref[1]
    core = lax.bitwise_and(row_at, 1)
    place = lax.shift_right_logical(lax.bitwise_and(row_at, near - 1), 1)
    half = row_at // near
    count = len(out_refs)
    places = count // n_branch
    per = chans // (n_branch * near)

    total = count * per
    q = lax.broadcasted_iota(jnp.int32, (total, chans), 0)
    t = q // per
    group = lax.bitwise_xor(t // places, branch) * near + (
        lax.bitwise_xor(t % places, place) * 2 + core
    )
    values, gates = channel_order(w_ref[...], (0, 1), group * per + q % per, total)

    def store_at(at):
        def store(i, block):
            scr[at, pl.ds(i, total, stride=rows), :] = block

        return store

    gated_rows(values, gates, x_ref, store_at(core))
    gated_rows(values, gates, other_ref, store_at(1 - core))
    depth = (out_refs[0].shape[0] - per * 2 * rows - rows) // 2
    base = per * 2 * rows
    for t, out_ref in zip(TARGETS, out_refs):
        for c in range(per):
            for k in range(2):
                start = (t * per + c) * rows
                out_ref[pl.ds((c * 2 + k) * rows, rows)] = scr[k, start : start + rows, :].astype(
                    BF16
                )
        b = lax.bitwise_xor(branch, t // places)
        p = lax.bitwise_xor(place, t % places)
        right = pl.ds(pl.multiple_of(b * depth, depth), depth)
        start = n_branch * depth + (half * places + p) * rows
        left = pl.ds(pl.multiple_of(start, rows), rows)
        out_ref[base : base + depth] = sides_ref[right]
        out_ref[base + depth : base + 2 * depth] = far_ref[right]
        out_ref[base + 2 * depth :] = jnp.concatenate(
            [sides_ref[left][:, : 2 * depth], far_ref[left][:, : 2 * depth]], axis=1
        )


def beside(where, x, other, w, sides, far_sides, depth, n_branch, near):
    rows, width, chans = x.shape
    count = n_branch * near // 2
    per = chans // (n_branch * near)
    piece = jax.ShapeDtypeStruct((per * 2 * rows + 2 * depth + rows, width), BF16)
    return pl.pallas_call(
        functools.partial(beside_kernel, n_branch, near),
        out_shape=[piece] * count,
        in_specs=[SMEM] + [VMEM] * 5,
        out_specs=[VMEM] * count,
        scratch_shapes=[pltpu.VMEM((2, count * per * rows, width), F32)],
        compiler_params=PARAMS,
        cost_estimate=cost(4 * x.size * 2 * chans, x.size * 8),
        name="left_operand",
    )(where, x, other, w, sides, far_sides)


def gate_kernel(x_ref, w_ref, out_ref):
    rows, width, chans = x_ref.shape
    tokens = x_ref[...].reshape(rows * width, chans)
    out_ref[...] = sigmoid(dot(tokens, w_ref[:, 4 * chans :])).reshape(rows, width, chans)


def output_gate(x, w):
    rows, width, chans = x.shape
    step = 4
    spec = pl.BlockSpec((step, width, chans), lambda i: (i, 0, 0))
    return pl.pallas_call(
        gate_kernel,
        grid=(rows // step,),
        out_shape=jax.ShapeDtypeStruct(x.shape, F32),
        in_specs=[spec, pl.BlockSpec(w.shape, lambda i: (0, 0))],
        out_specs=spec,
        compiler_params=PARAMS,
        cost_estimate=cost(2 * rows * width * chans * chans, rows * width * chans * 6),
        name="triangle_output_gate",
    )(x, w)


def product_kernel(n_branch, near, where_ref, in_ref, *rest):
    left_refs, (out_ref, left_scr) = rest[:-2], rest[-2:]
    devices, per, rows, width = in_ref.shape
    n_rows = devices // n_branch
    branch, row_at = where_ref[0], where_ref[1]
    place = lax.shift_right_logical(lax.bitwise_and(row_at, near - 1), 1)
    places = near // 2
    for t, ref in zip(TARGETS, left_refs):
        b = lax.bitwise_xor(branch, t // places)
        p = lax.bitwise_xor(place, t % places)
        for c in range(per):
            left_scr[b, c, p] = ref[c * 2 * rows : (c + 1) * 2 * rows]
    for c in range(per):
        left = jnp.concatenate(
            [left_scr[b, c].reshape(near * rows, width) for b in range(n_branch)], axis=1
        )
        right = jnp.concatenate(
            [
                in_ref[b * n_rows : (b + 1) * n_rows, c].reshape(n_rows * rows, width)
                for b in range(n_branch)
            ],
            axis=1,
        )
        product = dot(left, right, NT).astype(BF16)
        for b in range(n_branch):
            out_ref[b * near : (b + 1) * near, c] = product[
                :, b * width : (b + 1) * width
            ].reshape(near, rows, width)


def triangle_product(where, received, pieces, n_branch, near):
    devices, per, rows, width = received.shape
    return pl.pallas_call(
        functools.partial(product_kernel, n_branch, near),
        out_shape=jax.ShapeDtypeStruct((n_branch * near, per, rows, width), BF16),
        in_specs=[SMEM] + [VMEM] * (1 + len(pieces)),
        out_specs=VMEM,
        scratch_shapes=[pltpu.VMEM((n_branch, per, near // 2, 2 * rows, width), BF16)],
        compiler_params=PARAMS,
        cost_estimate=cost(
            2 * per * near * rows * received.size // per, received.size * 4
        ),
        name="triangle_product",
    )(where, received, *pieces)


def pair_output_kernel(
    p_ref, x_ref, gate_ref, outer_ref, w_ref, up_ref, down_ref, out_ref, scr
):
    devices, per, rows, width = p_ref.shape
    chans = devices * per
    for g in range(devices):
        for c in range(per):
            scr[pl.ds(g * per + c, rows, stride=chans), :] = p_ref[g, c].astype(F32)
    step = 4
    for i in range(0, rows, step):
        parts = [
            normed(scr[(i + k) * chans : (i + k + 1) * chans, :], 0) for k in range(step)
        ]
        update = dot(jnp.concatenate(parts, axis=1), w_ref[...], TN)
        shape = (step * width, chans)
        x = x_ref[i : i + step].astype(F32).reshape(shape)
        middle = x + gate_ref[i : i + step].reshape(shape) * update
        hidden = jnp.maximum(dot(normed(middle, -1), up_ref[...]), 0.0).astype(BF16)
        result = middle + dot(hidden, down_ref[...]) + outer_ref[i : i + step].reshape(shape)
        out_ref[i : i + step] = result.astype(BF16).reshape(step, width, chans)


def pair_output(product, x, gate, outer, w, up, down):
    devices, per, rows, width = product.shape
    chans = devices * per
    return pl.pallas_call(
        pair_output_kernel,
        out_shape=jax.ShapeDtypeStruct(x.shape, BF16),
        in_specs=[VMEM] * 7,
        out_specs=VMEM,
        scratch_shapes=[pltpu.VMEM((rows * chans, width), F32)],
        compiler_params=PARAMS,
        cost_estimate=cost(2 * x.size * (chans + 2 * up.shape[1]), x.size * 14),
        name="pair_output",
    )(product, x, gate, outer, w, up, down)


def outer_kernel(where_ref, *refs):
    groups, (w_ref, out_ref, right_scr, left_scr, w_scr, m_scr) = refs[:-6], refs[-6:]
    rows, width, chans = out_ref.shape
    total = 2 * sum(ref.shape[0] for ref in groups)
    depth = m_scr.shape[1] // total
    s = 0
    for ref in groups:
        for k in range(ref.shape[0]):
            both = ref[k, 2 * depth :].astype(F32)
            for far in range(2):
                at = s + far * (total // 2)
                side = ref[k, far * depth : (far + 1) * depth].astype(F32)
                right_scr[pl.ds(at, depth, stride=total), :] = side
                left_scr[pl.ds(at, rows, stride=total), :] = both
            s += 1
    right = jnp.transpose(right_scr[...]).astype(BF16)
    both = left_scr[...]
    shift = lax.bitwise_and(where_ref[1], 1) * depth
    first = pltpu.roll(both, width - shift, 1)[:, :depth]
    second = pltpu.roll(both, width - 2 * depth - shift, 1)[:, :depth]
    row = lax.broadcasted_iota(jnp.int32, first.shape, 0)
    left = jnp.where(row % total < total // 2, first, second).astype(BF16)
    w_scr[...] = w_ref[...].astype(F32)
    for d in range(depth):
        part = w_scr[pl.ds(d, depth, stride=depth), :].astype(BF16)
        m_scr[:, d * total : (d + 1) * total] = (
            dot(left, part).astype(BF16).reshape(rows, total, chans)
        )
    for i in range(0, rows, 2):
        pair = jnp.concatenate([m_scr[i], m_scr[i + 1]], axis=1)
        result = dot(right, pair) / total
        out_ref[i] = result[:, :chans]
        out_ref[i + 1] = result[:, chans:]


def outer_update(where, groups, w, rows, chans):
    total = 2 * sum(group.shape[0] for group in groups)
    width = groups[0].shape[2]
    depth = (groups[0].shape[1] - rows) // 2
    return pl.pallas_call(
        outer_kernel,
        out_shape=jax.ShapeDtypeStruct((rows, width, chans), F32),
        in_specs=[SMEM] + [VMEM] * (len(groups) + 1),
        out_specs=VMEM,
        scratch_shapes=[
            pltpu.VMEM((depth * total, width), F32),
            pltpu.VMEM((rows * total, width), F32),
            pltpu.VMEM((depth * depth, chans), F32),
            pltpu.VMEM((rows, depth * total, chans), BF16),
        ],
        compiler_params=PARAMS,
        cost_estimate=cost(2 * rows * width * depth * total * chans * 2, rows * width * chans * 4),
        name="outer_product_mean",
    )(where, *groups, w)


def swap(x, n_branch, n_rows, mask):
    count = n_branch * n_rows
    return lax.ppermute(x, AXES, [(d, d ^ mask) for d in range(count)])


def own_channels_device(
    n_branch,
    n_rows,
    homolog_features,
    pairwise_input,
    transition_expand_matrix,
    transition_contract_matrix,
    factor_pair_matrices,
    outer_output_weight,
    triangle_projection_weight,
    triangle_output_weight,
    pairwise_up_weight,
    pairwise_down_weight,
):
    rows, _, chans = pairwise_input.shape
    near = 8
    halves = n_rows // near
    places = near // 2
    per = chans // (n_branch * near)
    where = jnp.stack([lax.axis_index("branch"), lax.axis_index("rows")]).astype(jnp.int32)

    fresh, sides = msa(
        homolog_features,
        transition_expand_matrix,
        transition_contract_matrix,
        jnp.transpose(factor_pair_matrices),
        rows,
        pairwise_input.shape[1],
    )
    far_sides = swap(sides, n_branch, n_rows, near)
    pairwise_input, _ = lax.optimization_barrier((pairwise_input, sides))
    sent, tokens = right_operand(
        pairwise_input, triangle_projection_weight, n_branch, n_branch * n_rows, per
    )
    sent, far_sides = lax.optimization_barrier((sent, far_sides))
    received = lax.all_to_all(sent, AXES, 0, 0, tiled=True)

    other = swap(tokens, n_branch, n_rows, 1)
    pieces = beside(
        where,
        tokens,
        other,
        triangle_projection_weight,
        sides,
        far_sides,
        factor_pair_matrices.shape[1] // 2,
        n_branch,
        near,
    )
    moved = [
        piece if t == 0 else swap(piece, n_branch, n_rows, t // places * n_rows + t % places * 2)
        for t, piece in zip(TARGETS, pieces)
    ]
    mine = jnp.stack([piece[per * 2 * rows :] for piece in moved])
    groups = [mine, swap(mine, n_branch, n_rows, 1)]
    outer = outer_update(where, groups, outer_output_weight, rows, chans)
    gate_tokens, _ = lax.optimization_barrier((tokens, moved[0]))
    gate = output_gate(gate_tokens, triangle_projection_weight)

    product = triangle_product(where, received, moved, n_branch, near)
    members = [
        [b * n_rows + h * near + k for b in range(n_branch) for k in range(near)]
        for h in range(halves)
    ]
    returned = lax.all_to_all(product, AXES, 0, 0, axis_index_groups=members, tiled=True)
    pairwise_output = pair_output(
        returned,
        pairwise_input,
        gate,
        outer,
        triangle_output_weight,
        pairwise_up_weight,
        pairwise_down_weight,
    )
    return (fresh, pairwise_output)


def on_device(n_branch, n_rows, homolog_features, pairwise_input, *weights):
    rows, width, chans = pairwise_input.shape
    near = 8
    halves = n_rows // near
    fits = (
        homolog_features.shape[0] == 1
        and halves == 2
        and n_branch == 2
        and n_rows % near == 0
        and chans % (n_branch * near) == 0
        and rows == 16
        and width == 128
        and homolog_features.shape[1] == n_rows * rows == n_branch * width
        and 2 * weights[2].shape[1] == width
    )
    if fits:
        return own_channels_device(n_branch, n_rows, homolog_features, pairwise_input, *weights)
    return general_device(homolog_features, pairwise_input, *weights)


def solution(mesh):
    return jax.shard_map(
        functools.partial(on_device, mesh.shape["branch"], mesh.shape["rows"]),
        mesh=mesh,
        in_specs=(
            P(("branch", "rows"), None, None),
            P("rows", "branch", None),
            P(),
            P(),
            P(),
            P(),
            P(),
            P(),
            P(),
            P(),
        ),
        out_specs=(P(("branch", "rows"), None, None), P("rows", "branch", None)),
        check_vma=False,
    )
```

```python
import functools

import jax
import jax.numpy as jnp
from jax import lax
from jax.experimental import pallas as pl
from jax.experimental.pallas import tpu as pltpu
from jax.sharding import PartitionSpec as P

BF16 = jnp.bfloat16
F32 = jnp.float32
AXES = ("branch", "rows")
NT = (((1,), (1,)), ((), ()))
TN = (((0,), (0,)), ((), ()))
VMEM = pl.BlockSpec(memory_space=pltpu.VMEM)
SMEM = pl.BlockSpec(memory_space=pltpu.SMEM)
TARGETS = (0, 1, 4, 7, 3, 6, 2, 5)
HBM = pl.BlockSpec(memory_space=pltpu.HBM)
PARAMS = pltpu.CompilerParams(vmem_limit_bytes=48 * 1024 * 1024)

def standardize_features(values, dimension):
    average = jnp.mean(values, axis=dimension, keepdims=True)
    centered = values - average
    variance = jnp.mean(centered * centered, axis=dimension, keepdims=True)
    return centered * lax.rsqrt(variance + 1e-05)


def alignment_branch(
    homolog_features, transition_expand_matrix, transition_contract_matrix, factor_pair_matrices
):
    local_rows, sequence_length, channel_width = homolog_features.shape
    homolog_real_matrix = homolog_features.astype(jnp.float32)
    standardized_homologs = (
        standardize_features(homolog_real_matrix, -1)
        .astype(jnp.bfloat16)
        .reshape(local_rows * sequence_length, channel_width)
    )
    expanded_activations = jax.nn.relu(
        jnp.dot(standardized_homologs, transition_expand_matrix, preferred_element_type=jnp.float32)
    ).astype(jnp.bfloat16)
    refreshed_homolog_features = (
        homolog_real_matrix
        + jnp.dot(
            expanded_activations, transition_contract_matrix, preferred_element_type=jnp.float32
        ).reshape(homolog_features.shape)
    ).astype(jnp.bfloat16)
    standardized_for_factors = (
        standardize_features(refreshed_homolog_features.astype(jnp.float32), -1)
        .astype(jnp.bfloat16)
        .reshape(local_rows * sequence_length, channel_width)
    )
    projected = jnp.dot(
        standardized_for_factors, factor_pair_matrices, preferred_element_type=jnp.float32
    ).reshape(local_rows, sequence_length, -1)
    channels = projected.shape[-1] // 2
    left_side = projected[..., :channels].astype(jnp.bfloat16)
    right_side = jnp.swapaxes(projected[..., channels:].astype(jnp.bfloat16), 1, 2)
    left_pair = lax.all_gather(left_side, "branch", axis=0, tiled=True)
    left_gathered = lax.all_to_all(left_pair, "rows", split_axis=1, concat_axis=0, tiled=True)
    right_pair = lax.all_to_all(right_side, "branch", split_axis=2, concat_axis=0, tiled=True)
    right_gathered = lax.all_gather(right_pair, "rows", axis=0, tiled=True)
    return (refreshed_homolog_features, left_gathered, right_gathered)


def send_whole(tri_left, tri_right):
    return (
        lax.all_to_all(
            lax.all_to_all(tri_left, "branch", split_axis=0, concat_axis=2, tiled=True),
            "rows",
            split_axis=0,
            concat_axis=1,
            tiled=True,
        ),
        lax.all_to_all(
            lax.all_to_all(tri_right, "branch", split_axis=0, concat_axis=2, tiled=True),
            "rows",
            split_axis=0,
            concat_axis=1,
            tiled=True,
        ),
    )


def send_back(product):
    return lax.all_to_all(
        lax.all_to_all(product, "rows", split_axis=1, concat_axis=0, tiled=True),
        "branch",
        split_axis=2,
        concat_axis=0,
        tiled=True,
    )


def pair_branch(
    pairwise_input,
    triangle_projection_weight,
    triangle_output_weight,
    pairwise_up_weight,
    pairwise_down_weight,
):
    tile_rows, columns, chans = pairwise_input.shape
    pair_float = pairwise_input.astype(jnp.float32)
    pair_norm = standardize_features(pair_float, -1).astype(jnp.bfloat16)
    norm_flat = pair_norm.reshape(tile_rows * columns, chans)
    proj_flat = lax.dot_general(
        triangle_projection_weight,
        norm_flat,
        (((0,), (1,)), ((), ())),
        preferred_element_type=jnp.float32,
    )
    proj_tile = proj_flat[: 4 * chans].reshape(4 * chans, tile_rows, columns)
    gate_vals = jax.nn.sigmoid(proj_flat[4 * chans :])
    tri_left = (jax.nn.sigmoid(proj_tile[chans : 2 * chans]) * proj_tile[:chans]).astype(
        jnp.bfloat16
    )
    tri_right = (jax.nn.sigmoid(proj_tile[3 * chans :]) * proj_tile[2 * chans : 3 * chans]).astype(
        jnp.bfloat16
    )
    left_chan, right_chan = send_whole(tri_left, tri_right)
    product = jnp.einsum(
        "cik,cjk->cij", left_chan, right_chan, preferred_element_type=jnp.float32
    ).astype(jnp.bfloat16)
    product_tile = send_back(product)
    prod_norm = (
        standardize_features(product_tile.astype(jnp.float32), 0)
        .astype(jnp.bfloat16)
        .reshape(chans, tile_rows * columns)
    )
    tri_update = lax.dot_general(
        triangle_output_weight,
        prod_norm,
        (((0,), (0,)), ((), ())),
        preferred_element_type=jnp.float32,
    )
    gated_update = jnp.transpose(gate_vals * tri_update).reshape(tile_rows, columns, chans)
    pair_mid = pair_float + gated_update
    mid_norm = standardize_features(pair_mid, -1).astype(jnp.bfloat16)
    pair_hidden = jax.nn.relu(
        jnp.einsum("ijd,dh->ijh", mid_norm, pairwise_up_weight, preferred_element_type=jnp.float32)
    ).astype(jnp.bfloat16)
    return pair_mid + jnp.einsum(
        "ijh,hd->ijd", pair_hidden, pairwise_down_weight, preferred_element_type=jnp.float32
    )


def outer_product(left_gathered, right_gathered, outer_output_weight):
    total_rows, tile_rows, channels = left_gathered.shape
    columns = right_gathered.shape[2]
    span_cols = 128
    left_flat = left_gathered.reshape(total_rows, tile_rows * channels)
    pieces = []
    for offset in range(0, columns, span_cols):
        right_piece = right_gathered[:, :, offset : offset + span_cols].reshape(
            total_rows, channels * span_cols
        )
        outer_vals = lax.dot_general(
            left_flat, right_piece, (((0,), (0,)), ((), ())), preferred_element_type=jnp.float32
        )
        outer_vals = (
            (outer_vals / total_rows)
            .astype(jnp.bfloat16)
            .reshape(tile_rows, channels * channels, span_cols)
        )
        pieces.append(
            lax.dot_general(
                outer_output_weight,
                outer_vals,
                (((0,), (1,)), ((), ())),
                preferred_element_type=jnp.float32,
            )
        )
    outer_eij = jnp.concatenate(pieces, axis=2)
    return jnp.transpose(outer_eij, (1, 2, 0))


def general_device(
    homolog_features,
    pairwise_input,
    transition_expand_matrix,
    transition_contract_matrix,
    factor_pair_matrices,
    outer_output_weight,
    triangle_projection_weight,
    triangle_output_weight,
    pairwise_up_weight,
    pairwise_down_weight,
):
    refreshed_homolog_features, left_gathered, right_gathered = alignment_branch(
        homolog_features, transition_expand_matrix, transition_contract_matrix, factor_pair_matrices
    )
    pair_mid = pair_branch(
        pairwise_input,
        triangle_projection_weight,
        triangle_output_weight,
        pairwise_up_weight,
        pairwise_down_weight,
    )
    outer_update = outer_product(left_gathered, right_gathered, outer_output_weight)
    pairwise_output = (pair_mid + outer_update).astype(jnp.bfloat16)
    return (refreshed_homolog_features, pairwise_output)


def normed(values, axis):
    average = jnp.mean(values, axis=axis, keepdims=True)
    centered = values - average
    variance = jnp.mean(centered * centered, axis=axis, keepdims=True)
    return (centered * lax.rsqrt(variance + 1e-05)).astype(BF16)


def sigmoid(values):
    return 0.5 * jnp.tanh(0.5 * values) + 0.5


def dot(a, b, dims=(((1,), (0,)), ((), ()))):
    return lax.dot_general(a, b, dims, preferred_element_type=F32)


def cost(flops, nbytes, transcendentals=0):
    return pl.CostEstimate(flops=flops, bytes_accessed=nbytes, transcendentals=transcendentals)


def channel_order(w, sides, source, count):
    chans = w.shape[0]
    col = lax.broadcasted_iota(jnp.int32, (count, chans), 1)
    order = jnp.where(col == source, 1.0, 0.0).astype(BF16)
    return [dot(order, w[:, s * chans : (s + 1) * chans], NT).astype(BF16) for s in sides]


def gated_rows(values, gates, rows_ref, store):
    rows, width, chans = rows_ref.shape
    for i in range(0, rows, 2):
        tokens = rows_ref[i : i + 2].reshape(2 * width, chans)
        result = dot(values, tokens, NT) * sigmoid(dot(gates, tokens, NT))
        store(i, result[:, :width])
        store(i + 1, result[:, width:])


def right_kernel(
    n_branch, x_hbm, w_hbm, sent_hbm, tokens_hbm, x_ref, w_ref, sent_ref, tokens_ref, scr, sems
):
    rows, width, chans = x_ref.shape
    groups, per = sent_ref.shape[:2]
    near = groups // n_branch
    halves = sent_hbm.shape[0] // groups
    columns = w_hbm.at[:, pl.ds(2 * chans, 2 * chans)]
    copies = [
        pltpu.make_async_copy(columns, w_ref, sems.at[0]),
        pltpu.make_async_copy(x_hbm, x_ref, sems.at[1]),
    ]
    for copy in copies:
        copy.start()
    for copy in copies:
        copy.wait()
    values = jnp.transpose(w_ref[:, :chans])
    gates = jnp.transpose(w_ref[:, chans:])
    step = 4
    parts = []
    for i in range(0, rows, step):
        tokens = normed(x_ref[i : i + step].astype(F32), -1)
        tokens_ref[i : i + step] = tokens
        parts.append(tokens.reshape(step * width, chans))
    outs = [pltpu.make_async_copy(tokens_ref, tokens_hbm, sems.at[2])]
    outs[0].start()
    for i, tokens in zip(range(0, rows, step), parts):
        result = dot(values, tokens, NT) * sigmoid(dot(gates, tokens, NT))
        for k in range(step):
            scr[pl.ds(i + k, chans, stride=rows), :] = result[:, k * width : (k + 1) * width]
    span = 4
    for g in range(groups):
        for c in range(per):
            q = (g * per + c) * rows
            sent_ref[g, c] = scr[q : q + rows, :].astype(BF16)
        if g % span == span - 1:
            begin = g + 1 - span
            for h in range(halves):
                to = (begin // near * halves + h) * near + begin % near
                copy = pltpu.make_async_copy(
                    sent_ref.at[pl.ds(begin, span)],
                    sent_hbm.at[pl.ds(to, span)],
                    sems.at[2 + len(outs)],
                )
                copy.start()
                outs.append(copy)
    for copy in outs:
        copy.wait()


def right_operand(x, w, n_branch, devices, per):
    rows, width, chans = x.shape
    groups = chans // per
    return pl.pallas_call(
        functools.partial(right_kernel, n_branch),
        out_shape=[
            jax.ShapeDtypeStruct((devices, per, rows, width), BF16),
            jax.ShapeDtypeStruct(x.shape, BF16),
        ],
        in_specs=[HBM] * 2,
        out_specs=[HBM] * 2,
        scratch_shapes=[
            pltpu.VMEM(x.shape, BF16),
            pltpu.VMEM((chans, 2 * chans), BF16),
            pltpu.VMEM((groups, per, rows, width), BF16),
            pltpu.VMEM(x.shape, BF16),
            pltpu.VMEM((chans * rows, width), F32),
            pltpu.SemaphoreType.DMA((3 + devices // 4,)),
        ],
        cost_estimate=cost(2 * rows * width * chans * 2 * chans, 3 * rows * width * chans * 2),
        name="right_operand",
    )(x, w)


def msa_kernel(
    n_branch, rows, seq_hbm, up_hbm, down_hbm, factor_hbm, fresh_ref, sides_ref,
    seq_ref, up_ref, down_ref, factor_ref, sems
):
    pairs = [
        (seq_hbm, seq_ref),
        (up_hbm, up_ref),
        (down_hbm, down_ref),
        (factor_hbm, factor_ref),
    ]
    copies = [pltpu.make_async_copy(a, b, sems.at[k]) for k, (a, b) in enumerate(pairs)]
    for copy in copies:
        copy.start()
    copies[0].wait()
    x = seq_ref[0].astype(F32)
    tokens = normed(x, -1)
    copies[1].wait()
    hidden = jnp.maximum(dot(tokens, up_ref[...]), 0.0).astype(BF16)
    copies[2].wait()
    fresh = (x + dot(hidden, down_ref[...])).astype(BF16)
    fresh_ref[0] = fresh
    tokens = normed(fresh.astype(F32), -1)
    copies[3].wait()
    factor = factor_ref[...]
    depth = factor.shape[0] // 2
    left = dot(tokens, factor[:depth], NT).astype(BF16)
    right = dot(factor[depth:], tokens, NT).astype(BF16)
    width = sides_ref.shape[1]
    for b in range(n_branch):
        sides_ref[b * depth : (b + 1) * depth] = right[:, b * width : (b + 1) * width]
    tiles = left.reshape(-1, 2, rows, depth)
    blank = jnp.zeros((rows, width - 2 * depth), BF16)
    base = n_branch * depth
    for t in range(tiles.shape[0]):
        sides_ref[base + t * rows : base + (t + 1) * rows] = jnp.concatenate(
            [tiles[t, 0], tiles[t, 1], blank], axis=1
        )


def msa(seq, up, down, factor, rows, width):
    _, length, feats = seq.shape
    depth = factor.shape[0] // 2
    n_branch = length // width
    operands = (seq, up, down, factor)
    return pl.pallas_call(
        functools.partial(msa_kernel, n_branch, rows),
        out_shape=[
            jax.ShapeDtypeStruct(seq.shape, BF16),
            jax.ShapeDtypeStruct((n_branch * depth + length // 2, width), BF16),
        ],
        in_specs=[HBM] * 4,
        out_specs=[VMEM] * 2,
        scratch_shapes=[pltpu.VMEM(array.shape, BF16) for array in operands]
        + [pltpu.SemaphoreType.DMA((4,))],
        cost_estimate=cost(4 * length * feats * up.shape[1], 4 * feats * up.shape[1]),
        name="msa_transition",
    )(*operands)


def beside_kernel(
    n_branch, near, where_ref, x_ref, other_ref, w_ref, sides_ref, far_ref, *rest
):
    out_refs, scr = rest[:-1], rest[-1]
    rows, _, chans = x_ref.shape
    branch, row_at = where_ref[0], where_ref[1]
    core = lax.bitwise_and(row_at, 1)
    place = lax.shift_right_logical(lax.bitwise_and(row_at, near - 1), 1)
    half = row_at // near
    count = len(out_refs)
    places = count // n_branch
    per = chans // (n_branch * near)

    total = count * per
    q = lax.broadcasted_iota(jnp.int32, (total, chans), 0)
    t = q // per
    group = lax.bitwise_xor(t // places, branch) * near + (
        lax.bitwise_xor(t % places, place) * 2 + core
    )
    values, gates = channel_order(w_ref[...], (0, 1), group * per + q % per, total)

    def store_at(at):
        def store(i, block):
            scr[at, pl.ds(i, total, stride=rows), :] = block

        return store

    gated_rows(values, gates, x_ref, store_at(core))
    gated_rows(values, gates, other_ref, store_at(1 - core))
    depth = (out_refs[0].shape[0] - per * 2 * rows - rows) // 2
    base = per * 2 * rows
    for t, out_ref in zip(TARGETS, out_refs):
        for c in range(per):
            for k in range(2):
                start = (t * per + c) * rows
                out_ref[pl.ds((c * 2 + k) * rows, rows)] = scr[k, start : start + rows, :].astype(
                    BF16
                )
        b = lax.bitwise_xor(branch, t // places)
        p = lax.bitwise_xor(place, t % places)
        right = pl.ds(pl.multiple_of(b * depth, depth), depth)
        start = n_branch * depth + (half * places + p) * rows
        left = pl.ds(pl.multiple_of(start, rows), rows)
        out_ref[base : base + depth] = sides_ref[right]
        out_ref[base + depth : base + 2 * depth] = far_ref[right]
        out_ref[base + 2 * depth :] = jnp.concatenate(
            [sides_ref[left][:, : 2 * depth], far_ref[left][:, : 2 * depth]], axis=1
        )


def beside(where, x, other, w, sides, far_sides, depth, n_branch, near):
    rows, width, chans = x.shape
    count = n_branch * near // 2
    per = chans // (n_branch * near)
    piece = jax.ShapeDtypeStruct((per * 2 * rows + 2 * depth + rows, width), BF16)
    return pl.pallas_call(
        functools.partial(beside_kernel, n_branch, near),
        out_shape=[piece] * count,
        in_specs=[SMEM] + [VMEM] * 5,
        out_specs=[VMEM] * count,
        scratch_shapes=[pltpu.VMEM((2, count * per * rows, width), F32)],
        compiler_params=PARAMS,
        cost_estimate=cost(4 * x.size * 2 * chans, x.size * 8),
        name="left_operand",
    )(where, x, other, w, sides, far_sides)


def gate_kernel(x_ref, w_ref, out_ref):
    rows, width, chans = x_ref.shape
    tokens = x_ref[...].reshape(rows * width, chans)
    out_ref[...] = sigmoid(dot(tokens, w_ref[:, 4 * chans :])).reshape(rows, width, chans)


def output_gate(x, w):
    rows, width, chans = x.shape
    step = 4
    spec = pl.BlockSpec((step, width, chans), lambda i: (i, 0, 0))
    return pl.pallas_call(
        gate_kernel,
        grid=(rows // step,),
        out_shape=jax.ShapeDtypeStruct(x.shape, F32),
        in_specs=[spec, pl.BlockSpec(w.shape, lambda i: (0, 0))],
        out_specs=spec,
        compiler_params=PARAMS,
        cost_estimate=cost(2 * rows * width * chans * chans, rows * width * chans * 6),
        name="triangle_output_gate",
    )(x, w)


def product_kernel(n_branch, near, where_ref, in_ref, *rest):
    places = near // 2
    left_refs = dict(zip(TARGETS, rest))
    out_hbm, out_ref, sems = rest[n_branch * places :]
    devices, per, rows, width = in_ref.shape
    n_rows = devices // n_branch
    branch, row_at = where_ref[0], where_ref[1]
    place = lax.shift_right_logical(lax.bitwise_and(row_at, near - 1), 1)
    outs = []
    for c in range(per):
        span = slice(c * 2 * rows, (c + 1) * 2 * rows)
        left = jnp.concatenate(
            [
                jnp.concatenate([left_refs[s * places + p][span] for p in range(places)], axis=0)
                for s in range(n_branch)
            ],
            axis=1,
        )
        right = jnp.concatenate(
            [
                in_ref[pl.ds(lax.bitwise_xor(branch, s) * n_rows, n_rows), c].reshape(
                    n_rows * rows, width
                )
                for s in range(n_branch)
            ],
            axis=1,
        )
        product = dot(left, right, NT).astype(BF16)
        for p in range(places):
            at = lax.bitwise_xor(place, p) * 2
            part = product[p * 2 * rows : (p + 1) * 2 * rows]
            for b in range(n_branch):
                for k in range(2):
                    out_ref[n_branch * near - 1 - (b * near + at + k), c] = part[
                        k * rows : (k + 1) * rows, b * width : (b + 1) * width
                    ]
        if c % 2 == 1:
            half = pl.ds(c - 1, 2)
            copy = pltpu.make_async_copy(
                out_ref.at[:, half], out_hbm.at[:, half], sems.at[c // 2]
            )
            copy.start()
            outs.append(copy)
    for copy in outs:
        copy.wait()


def triangle_product(where, received, pieces, n_branch, near):
    devices, per, rows, width = received.shape
    shape = (n_branch * near, per, rows, width)
    return pl.pallas_call(
        functools.partial(product_kernel, n_branch, near),
        out_shape=jax.ShapeDtypeStruct(shape, BF16),
        in_specs=[SMEM] + [VMEM] * (1 + len(pieces)),
        out_specs=HBM,
        scratch_shapes=[pltpu.VMEM(shape, BF16), pltpu.SemaphoreType.DMA((per // 2,))],
        compiler_params=PARAMS,
        cost_estimate=cost(2 * near * rows * received.size, received.size * 4),
        name="triangle_product",
    )(where, received, *pieces)


def pair_output_kernel(
    p_ref, x_ref, gate_ref, outer_ref, w_ref, up_ref, down_ref, out_hbm, scr, out_ref, sems
):
    devices, per, rows, width = p_ref.shape
    chans = devices * per
    step = rows // 2
    shape = (step * width, chans)
    share = up_ref.shape[1] // 4

    def place(i):
        for g in range(devices):
            for c in range(per):
                tile = p_ref[devices - 1 - g, c].astype(F32)[i : i + step]
                scr[pl.ds(i * chans + g * per + c, step, stride=chans), :] = tile

    def triangle(i):
        parts = [
            normed(scr[(i + k) * chans : (i + k + 1) * chans, :], 0) for k in range(step)
        ]
        update = dot(jnp.concatenate(parts, axis=1), w_ref[...], TN)
        x = x_ref[i : i + step].astype(F32).reshape(shape)
        middle = x + gate_ref[i : i + step].reshape(shape) * update
        return middle, normed(middle, -1)

    def transition(i, middle, tokens):
        result = middle + outer_ref[i : i + step].reshape(shape)
        for h in range(0, up_ref.shape[1], share):
            hidden = dot(tokens, up_ref[:, h : h + share]).astype(BF16)
            result = result + dot(jnp.maximum(hidden, 0.0), down_ref[h : h + share])
        out_ref[i : i + step] = result.astype(BF16).reshape(step, width, chans)
        part = pl.ds(i, step)
        copy = pltpu.make_async_copy(out_ref.at[part], out_hbm.at[part], sems.at[i // step])
        copy.start()
        return copy

    middles = []
    for i in range(0, rows, step):
        place(i)
        middles.append(triangle(i))
    copies = [transition(i * step, *middle) for i, middle in enumerate(middles)]
    for copy in copies:
        copy.wait()


def pair_output(product, x, gate, outer, w, up, down):
    devices, per, rows, width = product.shape
    chans = devices * per
    return pl.pallas_call(
        pair_output_kernel,
        out_shape=jax.ShapeDtypeStruct(x.shape, BF16),
        in_specs=[VMEM] * 7,
        out_specs=HBM,
        scratch_shapes=[
            pltpu.VMEM((rows * chans, width), F32),
            pltpu.VMEM(x.shape, BF16),
            pltpu.SemaphoreType.DMA((2,)),
        ],
        compiler_params=PARAMS,
        cost_estimate=cost(2 * x.size * (chans + 2 * up.shape[1]), x.size * 14),
        name="pair_output",
    )(product, x, gate, outer, w, up, down)


def outer_kernel(where_ref, *refs):
    groups, (w_ref, out_ref, right_scr, left_scr, w_scr, m_scr) = refs[:-6], refs[-6:]
    rows, width, chans = out_ref.shape
    total = 2 * sum(ref.shape[0] for ref in groups)
    depth = m_scr.shape[1] // total
    s = 0
    for ref in groups:
        for k in range(ref.shape[0]):
            both = ref[k, 2 * depth :].astype(F32)
            for far in range(2):
                at = s + far * (total // 2)
                side = ref[k, far * depth : (far + 1) * depth].astype(F32)
                right_scr[pl.ds(at, depth, stride=total), :] = side
                left_scr[pl.ds(at, rows, stride=total), :] = both
            s += 1
    right = jnp.transpose(right_scr[...]).astype(BF16)
    both = left_scr[...]
    shift = lax.bitwise_and(where_ref[1], 1) * depth
    first = pltpu.roll(both, width - shift, 1)[:, :depth]
    second = pltpu.roll(both, width - 2 * depth - shift, 1)[:, :depth]
    row = lax.broadcasted_iota(jnp.int32, first.shape, 0)
    left = jnp.where(row % total < total // 2, first, second).astype(BF16)
    w_scr[...] = w_ref[...].astype(F32)
    for d in range(depth):
        part = w_scr[pl.ds(d, depth, stride=depth), :].astype(BF16)
        m_scr[:, d * total : (d + 1) * total] = (
            dot(left, part).astype(BF16).reshape(rows, total, chans)
        )
    for i in range(0, rows, 2):
        pair = jnp.concatenate([m_scr[i], m_scr[i + 1]], axis=1)
        result = dot(right, pair) / total
        out_ref[i] = result[:, :chans]
        out_ref[i + 1] = result[:, chans:]


def outer_update(where, groups, w, rows, chans):
    total = 2 * sum(group.shape[0] for group in groups)
    width = groups[0].shape[2]
    depth = (groups[0].shape[1] - rows) // 2
    return pl.pallas_call(
        outer_kernel,
        out_shape=jax.ShapeDtypeStruct((rows, width, chans), F32),
        in_specs=[SMEM] + [VMEM] * (len(groups) + 1),
        out_specs=VMEM,
        scratch_shapes=[
            pltpu.VMEM((depth * total, width), F32),
            pltpu.VMEM((rows * total, width), F32),
            pltpu.VMEM((depth * depth, chans), F32),
            pltpu.VMEM((rows, depth * total, chans), BF16),
        ],
        compiler_params=PARAMS,
        cost_estimate=cost(2 * rows * width * depth * total * chans * 2, rows * width * chans * 4),
        name="outer_product_mean",
    )(where, *groups, w)


def swap(x, n_branch, n_rows, mask):
    count = n_branch * n_rows
    return lax.ppermute(x, AXES, [(d, d ^ mask) for d in range(count)])


def own_channels_device(
    n_branch,
    n_rows,
    homolog_features,
    pairwise_input,
    transition_expand_matrix,
    transition_contract_matrix,
    factor_pair_matrices,
    outer_output_weight,
    triangle_projection_weight,
    triangle_output_weight,
    pairwise_up_weight,
    pairwise_down_weight,
):
    rows, _, chans = pairwise_input.shape
    near = 8
    halves = n_rows // near
    places = near // 2
    per = chans // (n_branch * near)
    where = jnp.stack([lax.axis_index("branch"), lax.axis_index("rows")]).astype(jnp.int32)

    fresh, sides = msa(
        homolog_features,
        transition_expand_matrix,
        transition_contract_matrix,
        jnp.transpose(factor_pair_matrices),
        rows,
        pairwise_input.shape[1],
    )
    far_sides = swap(sides, n_branch, n_rows, near)
    pairwise_input, _ = lax.optimization_barrier((pairwise_input, sides))
    sent, tokens = right_operand(
        pairwise_input, triangle_projection_weight, n_branch, n_branch * n_rows, per
    )
    sent, far_sides = lax.optimization_barrier((sent, far_sides))
    received = lax.all_to_all(sent, AXES, 0, 0, tiled=True)

    other = swap(tokens, n_branch, n_rows, 1)
    pieces = beside(
        where,
        tokens,
        other,
        triangle_projection_weight,
        sides,
        far_sides,
        factor_pair_matrices.shape[1] // 2,
        n_branch,
        near,
    )
    moved = [
        piece if t == 0 else swap(piece, n_branch, n_rows, t // places * n_rows + t % places * 2)
        for t, piece in zip(TARGETS, pieces)
    ]
    mine = jnp.stack([piece[per * 2 * rows :] for piece in moved])
    groups = [mine, swap(mine, n_branch, n_rows, 1)]
    outer = outer_update(where, groups, outer_output_weight, rows, chans)
    gate_tokens, _ = lax.optimization_barrier((tokens, moved[0]))
    gate = output_gate(gate_tokens, triangle_projection_weight)

    product = triangle_product(where, received, moved, n_branch, near)
    members = [
        [b * n_rows + h * near + k for b in range(n_branch) for k in range(near)][::-1]
        for h in range(halves)
    ]
    returned = lax.all_to_all(product, AXES, 0, 0, axis_index_groups=members, tiled=True)
    pairwise_output = pair_output(
        returned,
        pairwise_input,
        gate,
        outer,
        triangle_output_weight,
        pairwise_up_weight,
        pairwise_down_weight,
    )
    return (fresh, pairwise_output)


def on_device(n_branch, n_rows, homolog_features, pairwise_input, *weights):
    rows, width, chans = pairwise_input.shape
    near = 8
    halves = n_rows // near
    fits = (
        homolog_features.shape[0] == 1
        and halves == 2
        and n_branch == 2
        and n_rows % near == 0
        and chans % (n_branch * near) == 0
        and rows == 16
        and width == 128
        and homolog_features.shape[1] == n_rows * rows == n_branch * width
        and 2 * weights[2].shape[1] == width
    )
    if fits:
        return own_channels_device(n_branch, n_rows, homolog_features, pairwise_input, *weights)
    return general_device(homolog_features, pairwise_input, *weights)


def solution(mesh):
    return jax.shard_map(
        functools.partial(on_device, mesh.shape["branch"], mesh.shape["rows"]),
        mesh=mesh,
        in_specs=(
            P(("branch", "rows"), None, None),
            P("rows", "branch", None),
            P(),
            P(),
            P(),
            P(),
            P(),
            P(),
            P(),
            P(),
        ),
        out_specs=(P(("branch", "rows"), None, None), P("rows", "branch", None)),
        check_vma=False,
    )
```

```python
import functools

import jax
import jax.numpy as jnp
from jax import lax
from jax.experimental import pallas as pl
from jax.experimental.pallas import tpu as pltpu
from jax.sharding import PartitionSpec as P

BF16 = jnp.bfloat16
F32 = jnp.float32
AXES = ("branch", "rows")
NT = (((1,), (1,)), ((), ()))
TN = (((0,), (0,)), ((), ()))
VMEM = pl.BlockSpec(memory_space=pltpu.VMEM)
SMEM = pl.BlockSpec(memory_space=pltpu.SMEM)
TARGETS = (0, 4, 1, 2, 7, 3, 6, 5)
HBM = pl.BlockSpec(memory_space=pltpu.HBM)
PARAMS = pltpu.CompilerParams(vmem_limit_bytes=48 * 1024 * 1024)

def standardize_features(values, dimension):
    average = jnp.mean(values, axis=dimension, keepdims=True)
    centered = values - average
    variance = jnp.mean(centered * centered, axis=dimension, keepdims=True)
    return centered * lax.rsqrt(variance + 1e-05)


def alignment_branch(
    homolog_features, transition_expand_matrix, transition_contract_matrix, factor_pair_matrices
):
    local_rows, sequence_length, channel_width = homolog_features.shape
    homolog_real_matrix = homolog_features.astype(jnp.float32)
    standardized_homologs = (
        standardize_features(homolog_real_matrix, -1)
        .astype(jnp.bfloat16)
        .reshape(local_rows * sequence_length, channel_width)
    )
    expanded_activations = jax.nn.relu(
        jnp.dot(standardized_homologs, transition_expand_matrix, preferred_element_type=jnp.float32)
    ).astype(jnp.bfloat16)
    refreshed_homolog_features = (
        homolog_real_matrix
        + jnp.dot(
            expanded_activations, transition_contract_matrix, preferred_element_type=jnp.float32
        ).reshape(homolog_features.shape)
    ).astype(jnp.bfloat16)
    standardized_for_factors = (
        standardize_features(refreshed_homolog_features.astype(jnp.float32), -1)
        .astype(jnp.bfloat16)
        .reshape(local_rows * sequence_length, channel_width)
    )
    projected = jnp.dot(
        standardized_for_factors, factor_pair_matrices, preferred_element_type=jnp.float32
    ).reshape(local_rows, sequence_length, -1)
    channels = projected.shape[-1] // 2
    left_side = projected[..., :channels].astype(jnp.bfloat16)
    right_side = jnp.swapaxes(projected[..., channels:].astype(jnp.bfloat16), 1, 2)
    left_pair = lax.all_gather(left_side, "branch", axis=0, tiled=True)
    left_gathered = lax.all_to_all(left_pair, "rows", split_axis=1, concat_axis=0, tiled=True)
    right_pair = lax.all_to_all(right_side, "branch", split_axis=2, concat_axis=0, tiled=True)
    right_gathered = lax.all_gather(right_pair, "rows", axis=0, tiled=True)
    return (refreshed_homolog_features, left_gathered, right_gathered)


def send_whole(tri_left, tri_right):
    return (
        lax.all_to_all(
            lax.all_to_all(tri_left, "branch", split_axis=0, concat_axis=2, tiled=True),
            "rows",
            split_axis=0,
            concat_axis=1,
            tiled=True,
        ),
        lax.all_to_all(
            lax.all_to_all(tri_right, "branch", split_axis=0, concat_axis=2, tiled=True),
            "rows",
            split_axis=0,
            concat_axis=1,
            tiled=True,
        ),
    )


def send_back(product):
    return lax.all_to_all(
        lax.all_to_all(product, "rows", split_axis=1, concat_axis=0, tiled=True),
        "branch",
        split_axis=2,
        concat_axis=0,
        tiled=True,
    )


def pair_branch(
    pairwise_input,
    triangle_projection_weight,
    triangle_output_weight,
    pairwise_up_weight,
    pairwise_down_weight,
):
    tile_rows, columns, chans = pairwise_input.shape
    pair_float = pairwise_input.astype(jnp.float32)
    pair_norm = standardize_features(pair_float, -1).astype(jnp.bfloat16)
    norm_flat = pair_norm.reshape(tile_rows * columns, chans)
    proj_flat = lax.dot_general(
        triangle_projection_weight,
        norm_flat,
        (((0,), (1,)), ((), ())),
        preferred_element_type=jnp.float32,
    )
    proj_tile = proj_flat[: 4 * chans].reshape(4 * chans, tile_rows, columns)
    gate_vals = jax.nn.sigmoid(proj_flat[4 * chans :])
    tri_left = (jax.nn.sigmoid(proj_tile[chans : 2 * chans]) * proj_tile[:chans]).astype(
        jnp.bfloat16
    )
    tri_right = (jax.nn.sigmoid(proj_tile[3 * chans :]) * proj_tile[2 * chans : 3 * chans]).astype(
        jnp.bfloat16
    )
    left_chan, right_chan = send_whole(tri_left, tri_right)
    product = jnp.einsum(
        "cik,cjk->cij", left_chan, right_chan, preferred_element_type=jnp.float32
    ).astype(jnp.bfloat16)
    product_tile = send_back(product)
    prod_norm = (
        standardize_features(product_tile.astype(jnp.float32), 0)
        .astype(jnp.bfloat16)
        .reshape(chans, tile_rows * columns)
    )
    tri_update = lax.dot_general(
        triangle_output_weight,
        prod_norm,
        (((0,), (0,)), ((), ())),
        preferred_element_type=jnp.float32,
    )
    gated_update = jnp.transpose(gate_vals * tri_update).reshape(tile_rows, columns, chans)
    pair_mid = pair_float + gated_update
    mid_norm = standardize_features(pair_mid, -1).astype(jnp.bfloat16)
    pair_hidden = jax.nn.relu(
        jnp.einsum("ijd,dh->ijh", mid_norm, pairwise_up_weight, preferred_element_type=jnp.float32)
    ).astype(jnp.bfloat16)
    return pair_mid + jnp.einsum(
        "ijh,hd->ijd", pair_hidden, pairwise_down_weight, preferred_element_type=jnp.float32
    )


def outer_product(left_gathered, right_gathered, outer_output_weight):
    total_rows, tile_rows, channels = left_gathered.shape
    columns = right_gathered.shape[2]
    span_cols = 128
    left_flat = left_gathered.reshape(total_rows, tile_rows * channels)
    pieces = []
    for offset in range(0, columns, span_cols):
        right_piece = right_gathered[:, :, offset : offset + span_cols].reshape(
            total_rows, channels * span_cols
        )
        outer_vals = lax.dot_general(
            left_flat, right_piece, (((0,), (0,)), ((), ())), preferred_element_type=jnp.float32
        )
        outer_vals = (
            (outer_vals / total_rows)
            .astype(jnp.bfloat16)
            .reshape(tile_rows, channels * channels, span_cols)
        )
        pieces.append(
            lax.dot_general(
                outer_output_weight,
                outer_vals,
                (((0,), (1,)), ((), ())),
                preferred_element_type=jnp.float32,
            )
        )
    outer_eij = jnp.concatenate(pieces, axis=2)
    return jnp.transpose(outer_eij, (1, 2, 0))


def general_device(
    homolog_features,
    pairwise_input,
    transition_expand_matrix,
    transition_contract_matrix,
    factor_pair_matrices,
    outer_output_weight,
    triangle_projection_weight,
    triangle_output_weight,
    pairwise_up_weight,
    pairwise_down_weight,
):
    refreshed_homolog_features, left_gathered, right_gathered = alignment_branch(
        homolog_features, transition_expand_matrix, transition_contract_matrix, factor_pair_matrices
    )
    pair_mid = pair_branch(
        pairwise_input,
        triangle_projection_weight,
        triangle_output_weight,
        pairwise_up_weight,
        pairwise_down_weight,
    )
    outer_update = outer_product(left_gathered, right_gathered, outer_output_weight)
    pairwise_output = (pair_mid + outer_update).astype(jnp.bfloat16)
    return (refreshed_homolog_features, pairwise_output)


def normed(values, axis):
    average = jnp.mean(values, axis=axis, keepdims=True)
    centered = values - average
    variance = jnp.mean(centered * centered, axis=axis, keepdims=True)
    return (centered * lax.rsqrt(variance + 1e-05)).astype(BF16)


def sigmoid(values):
    return 0.5 * jnp.tanh(0.5 * values) + 0.5


def dot(a, b, dims=(((1,), (0,)), ((), ()))):
    return lax.dot_general(a, b, dims, preferred_element_type=F32)


def cost(flops, nbytes, transcendentals=0):
    return pl.CostEstimate(flops=flops, bytes_accessed=nbytes, transcendentals=transcendentals)


def channel_order(w, sides, source, count):
    chans = w.shape[0]
    col = lax.broadcasted_iota(jnp.int32, (count, chans), 1)
    order = jnp.where(col == source, 1.0, 0.0).astype(BF16)
    return [dot(order, w[:, s * chans : (s + 1) * chans], NT).astype(BF16) for s in sides]


def gated_rows(values, gates, rows_ref, store):
    rows, width, chans = rows_ref.shape
    for i in range(0, rows, 2):
        tokens = rows_ref[i : i + 2].reshape(2 * width, chans)
        result = dot(values, tokens, NT) * sigmoid(dot(gates, tokens, NT))
        store(i, result[:, :width])
        store(i + 1, result[:, width:])


def right_kernel(
    n_branch, x_hbm, w_hbm, sent_hbm, tokens_hbm, x_ref, w_ref, sent_ref, tokens_ref, scr, sems
):
    rows, width, chans = x_ref.shape
    groups, per = sent_ref.shape[:2]
    near = groups // n_branch
    halves = sent_hbm.shape[0] // groups
    columns = w_hbm.at[:, pl.ds(2 * chans, 2 * chans)]
    copies = [
        pltpu.make_async_copy(columns, w_ref, sems.at[0]),
        pltpu.make_async_copy(x_hbm, x_ref, sems.at[1]),
    ]
    for copy in copies:
        copy.start()
    for copy in copies:
        copy.wait()
    values = jnp.transpose(w_ref[:, :chans])
    gates = jnp.transpose(w_ref[:, chans:])
    step = 4
    parts = []
    for i in range(0, rows, step):
        tokens = normed(x_ref[i : i + step].astype(F32), -1)
        tokens_ref[i : i + step] = tokens
        parts.append(tokens.reshape(step * width, chans))
    outs = [pltpu.make_async_copy(tokens_ref, tokens_hbm, sems.at[2])]
    outs[0].start()
    for i, tokens in zip(range(0, rows, step), parts):
        result = dot(values, tokens, NT) * sigmoid(dot(gates, tokens, NT))
        for k in range(step):
            scr[pl.ds(i + k, chans, stride=rows), :] = result[:, k * width : (k + 1) * width]
    span = 4
    for g in range(groups):
        for c in range(per):
            q = (g * per + c) * rows
            sent_ref[g, c] = scr[q : q + rows, :].astype(BF16)
        if g % span == span - 1:
            begin = g + 1 - span
            for h in range(halves):
                to = (begin // near * halves + h) * near + begin % near
                copy = pltpu.make_async_copy(
                    sent_ref.at[pl.ds(begin, span)],
                    sent_hbm.at[pl.ds(to, span)],
                    sems.at[2 + len(outs)],
                )
                copy.start()
                outs.append(copy)
    for copy in outs:
        copy.wait()


def right_operand(x, w, n_branch, devices, per):
    rows, width, chans = x.shape
    groups = chans // per
    return pl.pallas_call(
        functools.partial(right_kernel, n_branch),
        out_shape=[
            jax.ShapeDtypeStruct((devices, per, rows, width), BF16),
            jax.ShapeDtypeStruct(x.shape, BF16),
        ],
        in_specs=[HBM] * 2,
        out_specs=[HBM] * 2,
        scratch_shapes=[
            pltpu.VMEM(x.shape, BF16),
            pltpu.VMEM((chans, 2 * chans), BF16),
            pltpu.VMEM((groups, per, rows, width), BF16),
            pltpu.VMEM(x.shape, BF16),
            pltpu.VMEM((chans * rows, width), F32),
            pltpu.SemaphoreType.DMA((3 + devices // 4,)),
        ],
        cost_estimate=cost(2 * rows * width * chans * 2 * chans, 3 * rows * width * chans * 2),
        name="right_operand",
    )(x, w)


def msa_kernel(
    n_branch, rows, seq_ref, far_ref, up_ref, down_ref, factor_ref, fresh_ref, *side_refs
):
    x = [ref[0].astype(F32) for ref in (seq_ref, far_ref)]
    tokens = [normed(v, -1) for v in x]
    hidden = [jnp.maximum(dot(t, up_ref[...]).astype(BF16), 0.0) for t in tokens]
    fresh = [(v + dot(h, down_ref[...])).astype(BF16) for v, h in zip(x, hidden)]
    fresh_ref[0] = fresh[0]
    factor = factor_ref[...]
    depth = factor.shape[0] // 2
    for row, sides_ref in zip(fresh, side_refs):
        tokens = normed(row.astype(F32), -1)
        left = dot(tokens, factor[:depth], NT).astype(BF16)
        right = dot(factor[depth:], tokens, NT).astype(BF16)
        width = sides_ref.shape[1]
        for b in range(n_branch):
            sides_ref[b * depth : (b + 1) * depth] = right[:, b * width : (b + 1) * width]
        tiles = left.reshape(-1, 2, rows, depth)
        blank = jnp.zeros((rows, width - 2 * depth), BF16)
        base = n_branch * depth
        for t in range(tiles.shape[0]):
            sides_ref[base + t * rows : base + (t + 1) * rows] = jnp.concatenate(
                [tiles[t, 0], tiles[t, 1], blank], axis=1
            )


def msa(seq, far, up, down, factor, rows, width):
    _, length, feats = seq.shape
    depth = factor.shape[0] // 2
    n_branch = length // width
    sides = jax.ShapeDtypeStruct((n_branch * depth + length // 2, width), BF16)
    return pl.pallas_call(
        functools.partial(msa_kernel, n_branch, rows),
        out_shape=[jax.ShapeDtypeStruct(seq.shape, BF16), sides, sides],
        in_specs=[VMEM] * 5,
        out_specs=[VMEM] * 3,
        compiler_params=PARAMS,
        cost_estimate=cost(8 * length * feats * up.shape[1], 4 * feats * up.shape[1]),
        name="msa_transition",
    )(seq, far, up, down, factor)


def beside_kernel(
    n_branch, near, where_ref, x_ref, other_ref, w_ref, sides_ref, far_ref, *rest
):
    out_refs, scr = rest[:-1], rest[-1]
    rows, _, chans = x_ref.shape
    branch, row_at = where_ref[0], where_ref[1]
    core = lax.bitwise_and(row_at, 1)
    place = lax.shift_right_logical(lax.bitwise_and(row_at, near - 1), 1)
    half = row_at // near
    count = len(out_refs)
    places = count // n_branch
    per = chans // (n_branch * near)

    total = count * per
    q = lax.broadcasted_iota(jnp.int32, (total, chans), 0)
    t = q // per
    group = lax.bitwise_xor(t // places, branch) * near + (
        lax.bitwise_xor(t % places, place) * 2 + core
    )
    values, gates = channel_order(w_ref[...], (0, 1), group * per + q % per, total)

    def store_at(at):
        def store(i, block):
            scr[at, pl.ds(i, total, stride=rows), :] = block

        return store

    gated_rows(values, gates, x_ref, store_at(core))
    gated_rows(values, gates, other_ref, store_at(1 - core))
    depth = (out_refs[0].shape[0] - per * 2 * rows - rows) // 2
    base = per * 2 * rows
    for t, out_ref in zip(TARGETS, out_refs):
        for c in range(per):
            for k in range(2):
                start = (t * per + c) * rows
                out_ref[pl.ds((c * 2 + k) * rows, rows)] = scr[k, start : start + rows, :].astype(
                    BF16
                )
        b = lax.bitwise_xor(branch, t // places)
        p = lax.bitwise_xor(place, t % places)
        right = pl.ds(pl.multiple_of(b * depth, depth), depth)
        start = n_branch * depth + (half * places + p) * rows
        left = pl.ds(pl.multiple_of(start, rows), rows)
        out_ref[base : base + depth] = sides_ref[right]
        out_ref[base + depth : base + 2 * depth] = far_ref[right]
        out_ref[base + 2 * depth :] = jnp.concatenate(
            [sides_ref[left][:, : 2 * depth], far_ref[left][:, : 2 * depth]], axis=1
        )


def beside(where, x, other, w, sides, far_sides, depth, n_branch, near):
    rows, width, chans = x.shape
    count = n_branch * near // 2
    per = chans // (n_branch * near)
    piece = jax.ShapeDtypeStruct((per * 2 * rows + 2 * depth + rows, width), BF16)
    return pl.pallas_call(
        functools.partial(beside_kernel, n_branch, near),
        out_shape=[piece] * count,
        in_specs=[SMEM] + [VMEM] * 5,
        out_specs=[VMEM] * count,
        scratch_shapes=[pltpu.VMEM((2, count * per * rows, width), F32)],
        compiler_params=PARAMS,
        cost_estimate=cost(2 * 10**10, x.size * 8),
        name="left_operand",
    )(where, x, other, w, sides, far_sides)


def gate_kernel(x_ref, w_ref, out_ref):
    rows, width, chans = x_ref.shape
    tokens = x_ref[...].reshape(rows * width, chans)
    out_ref[...] = sigmoid(dot(tokens, w_ref[:, 4 * chans :])).reshape(rows, width, chans)


def output_gate(x, w):
    rows, width, chans = x.shape
    step = 4
    spec = pl.BlockSpec((step, width, chans), lambda i: (i, 0, 0))
    return pl.pallas_call(
        gate_kernel,
        grid=(rows // step,),
        out_shape=jax.ShapeDtypeStruct(x.shape, F32),
        in_specs=[spec, pl.BlockSpec(w.shape, lambda i: (0, 0))],
        out_specs=spec,
        compiler_params=PARAMS,
        cost_estimate=cost(2 * rows * width * chans * chans, rows * width * chans * 6),
        name="triangle_output_gate",
    )(x, w)


def product_kernel(n_branch, near, where_ref, in_ref, *rest):
    places = near // 2
    left_refs = dict(zip(TARGETS, rest))
    out_hbm, out_ref, sems = rest[n_branch * places :]
    devices, per, rows, width = in_ref.shape
    n_rows = devices // n_branch
    branch, row_at = where_ref[0], where_ref[1]
    place = lax.shift_right_logical(lax.bitwise_and(row_at, near - 1), 1)
    outs = []
    for c in range(per):
        span = slice(c * 2 * rows, (c + 1) * 2 * rows)
        left = jnp.concatenate(
            [
                jnp.concatenate([left_refs[s * places + p][span] for p in range(places)], axis=0)
                for s in range(n_branch)
            ],
            axis=1,
        )
        right = jnp.concatenate(
            [
                in_ref[pl.ds(lax.bitwise_xor(branch, s) * n_rows, n_rows), c].reshape(
                    n_rows * rows, width
                )
                for s in range(n_branch)
            ],
            axis=1,
        )
        product = dot(left, right, NT).astype(BF16)
        for p in range(places):
            at = lax.bitwise_xor(place, p) * 2
            part = product[p * 2 * rows : (p + 1) * 2 * rows]
            for b in range(n_branch):
                for k in range(2):
                    out_ref[n_branch * near - 1 - (b * near + at + k), c] = part[
                        k * rows : (k + 1) * rows, b * width : (b + 1) * width
                    ]
        if c % 2 == 1:
            half = pl.ds(c - 1, 2)
            copy = pltpu.make_async_copy(
                out_ref.at[:, half], out_hbm.at[:, half], sems.at[c // 2]
            )
            copy.start()
            outs.append(copy)
    for copy in outs:
        copy.wait()


def triangle_product(where, received, pieces, n_branch, near):
    devices, per, rows, width = received.shape
    shape = (n_branch * near, per, rows, width)
    return pl.pallas_call(
        functools.partial(product_kernel, n_branch, near),
        out_shape=jax.ShapeDtypeStruct(shape, BF16),
        in_specs=[SMEM] + [VMEM] * (1 + len(pieces)),
        out_specs=HBM,
        scratch_shapes=[pltpu.VMEM(shape, BF16), pltpu.SemaphoreType.DMA((per // 2,))],
        compiler_params=PARAMS,
        cost_estimate=cost(2 * near * rows * received.size, received.size * 4),
        name="triangle_product",
    )(where, received, *pieces)


def pair_output_kernel(
    p_ref, x_ref, gate_ref, outer_ref, w_ref, up_ref, down_ref, out_hbm, scr, out_ref, sems
):
    devices, per, rows, width = p_ref.shape
    chans = devices * per
    step = rows // 2
    shape = (step * width, chans)
    share = up_ref.shape[1] // 4

    def place(i):
        for g in range(devices):
            for c in range(per):
                tile = p_ref[devices - 1 - g, c].astype(F32)[i : i + step]
                scr[pl.ds(i * chans + g * per + c, step, stride=chans), :] = tile

    def triangle(i):
        parts = [
            normed(scr[(i + k) * chans : (i + k + 1) * chans, :], 0) for k in range(step)
        ]
        update = dot(jnp.concatenate(parts, axis=1), w_ref[...], TN)
        x = x_ref[i : i + step].astype(F32).reshape(shape)
        middle = x + gate_ref[i : i + step].reshape(shape) * update
        return middle, normed(middle, -1)

    def transition(i, middle, tokens):
        result = middle + outer_ref[i : i + step].reshape(shape)
        for h in range(0, up_ref.shape[1], share):
            hidden = dot(tokens, up_ref[:, h : h + share]).astype(BF16)
            result = result + dot(jnp.maximum(hidden, 0.0), down_ref[h : h + share])
        out_ref[i : i + step] = result.astype(BF16).reshape(step, width, chans)
        part = pl.ds(i, step)
        copy = pltpu.make_async_copy(out_ref.at[part], out_hbm.at[part], sems.at[i // step])
        copy.start()
        return copy

    middles = []
    for i in range(0, rows, step):
        place(i)
        middles.append(triangle(i))
    copies = [transition(i * step, *middle) for i, middle in enumerate(middles)]
    for copy in copies:
        copy.wait()


def pair_output(product, x, gate, outer, w, up, down):
    devices, per, rows, width = product.shape
    chans = devices * per
    return pl.pallas_call(
        pair_output_kernel,
        out_shape=jax.ShapeDtypeStruct(x.shape, BF16),
        in_specs=[VMEM] * 7,
        out_specs=HBM,
        scratch_shapes=[
            pltpu.VMEM((rows * chans, width), F32),
            pltpu.VMEM(x.shape, BF16),
            pltpu.SemaphoreType.DMA((2,)),
        ],
        compiler_params=PARAMS,
        cost_estimate=cost(2 * x.size * (chans + 2 * up.shape[1]), x.size * 14),
        name="pair_output",
    )(product, x, gate, outer, w, up, down)


def outer_kernel(where_ref, *refs):
    groups, (w_ref, out_ref, right_scr, left_scr, w_scr, m_scr) = refs[:-6], refs[-6:]
    rows, width, chans = out_ref.shape
    total = 2 * sum(ref.shape[0] for ref in groups)
    depth = m_scr.shape[1] // total
    s = 0
    for ref in groups:
        for k in range(ref.shape[0]):
            both = ref[k, 2 * depth :].astype(F32)
            for far in range(2):
                at = s + far * (total // 2)
                side = ref[k, far * depth : (far + 1) * depth].astype(F32)
                right_scr[pl.ds(at, depth, stride=total), :] = side
                left_scr[pl.ds(at, rows, stride=total), :] = both
            s += 1
    right = jnp.transpose(right_scr[...]).astype(BF16)
    both = left_scr[...]
    shift = lax.bitwise_and(where_ref[1], 1) * depth
    first = pltpu.roll(both, width - shift, 1)[:, :depth]
    second = pltpu.roll(both, width - 2 * depth - shift, 1)[:, :depth]
    row = lax.broadcasted_iota(jnp.int32, first.shape, 0)
    left = jnp.where(row % total < total // 2, first, second).astype(BF16)
    w_scr[...] = w_ref[...].astype(F32)
    for d in range(depth):
        part = w_scr[pl.ds(d, depth, stride=depth), :].astype(BF16)
        m_scr[:, d * total : (d + 1) * total] = (
            dot(left, part).astype(BF16).reshape(rows, total, chans)
        )
    for i in range(0, rows, 2):
        pair = jnp.concatenate([m_scr[i], m_scr[i + 1]], axis=1)
        result = dot(right, pair) / total
        out_ref[i] = result[:, :chans]
        out_ref[i + 1] = result[:, chans:]


def outer_update(where, groups, w, rows, chans):
    total = 2 * sum(group.shape[0] for group in groups)
    width = groups[0].shape[2]
    depth = (groups[0].shape[1] - rows) // 2
    return pl.pallas_call(
        outer_kernel,
        out_shape=jax.ShapeDtypeStruct((rows, width, chans), F32),
        in_specs=[SMEM] + [VMEM] * (len(groups) + 1),
        out_specs=VMEM,
        scratch_shapes=[
            pltpu.VMEM((depth * total, width), F32),
            pltpu.VMEM((rows * total, width), F32),
            pltpu.VMEM((depth * depth, chans), F32),
            pltpu.VMEM((rows, depth * total, chans), BF16),
        ],
        compiler_params=PARAMS,
        cost_estimate=cost(2 * rows * width * depth * total * chans * 2, rows * width * chans * 4),
        name="outer_product_mean",
    )(where, *groups, w)


def swap(x, n_branch, n_rows, mask):
    count = n_branch * n_rows
    return lax.ppermute(x, AXES, [(d, d ^ mask) for d in range(count)])


def own_channels_device(
    n_branch,
    n_rows,
    homolog_features,
    pairwise_input,
    transition_expand_matrix,
    transition_contract_matrix,
    factor_pair_matrices,
    outer_output_weight,
    triangle_projection_weight,
    triangle_output_weight,
    pairwise_up_weight,
    pairwise_down_weight,
):
    rows, _, chans = pairwise_input.shape
    near = 8
    halves = n_rows // near
    places = near // 2
    per = chans // (n_branch * near)
    where = jnp.stack([lax.axis_index("branch"), lax.axis_index("rows")]).astype(jnp.int32)

    far_row = swap(homolog_features, n_branch, n_rows, near)
    sent, tokens = right_operand(
        pairwise_input, triangle_projection_weight, n_branch, n_branch * n_rows, per
    )
    received = lax.all_to_all(sent, AXES, 0, 0, tiled=True)

    other = swap(tokens, n_branch, n_rows, 1)
    fresh, sides, far_sides = msa(
        homolog_features,
        far_row,
        transition_expand_matrix,
        transition_contract_matrix,
        jnp.transpose(factor_pair_matrices),
        rows,
        pairwise_input.shape[1],
    )
    pieces = beside(
        where,
        tokens,
        other,
        triangle_projection_weight,
        sides,
        far_sides,
        factor_pair_matrices.shape[1] // 2,
        n_branch,
        near,
    )
    moved = [
        piece if t == 0 else swap(piece, n_branch, n_rows, t // places * n_rows + t % places * 2)
        for t, piece in zip(TARGETS, pieces)
    ]
    mine = jnp.stack([piece[per * 2 * rows :] for piece in moved])
    groups = [mine, swap(mine, n_branch, n_rows, 1)]
    outer = outer_update(where, groups, outer_output_weight, rows, chans)
    gate_tokens, _ = lax.optimization_barrier((tokens, moved[0]))
    gate = output_gate(gate_tokens, triangle_projection_weight)

    product = triangle_product(where, received, moved, n_branch, near)
    members = [
        [b * n_rows + h * near + k for b in range(n_branch) for k in range(near)][::-1]
        for h in range(halves)
    ]
    returned = lax.all_to_all(product, AXES, 0, 0, axis_index_groups=members, tiled=True)
    pairwise_output = pair_output(
        returned,
        pairwise_input,
        gate,
        outer,
        triangle_output_weight,
        pairwise_up_weight,
        pairwise_down_weight,
    )
    return (fresh, pairwise_output)


def on_device(n_branch, n_rows, homolog_features, pairwise_input, *weights):
    rows, width, chans = pairwise_input.shape
    near = 8
    halves = n_rows // near
    fits = (
        homolog_features.shape[0] == 1
        and halves == 2
        and n_branch == 2
        and n_rows % near == 0
        and chans % (n_branch * near) == 0
        and rows == 16
        and width == 128
        and homolog_features.shape[1] == n_rows * rows == n_branch * width
        and 2 * weights[2].shape[1] == width
    )
    if fits:
        return own_channels_device(n_branch, n_rows, homolog_features, pairwise_input, *weights)
    return general_device(homolog_features, pairwise_input, *weights)


def solution(mesh):
    return jax.shard_map(
        functools.partial(on_device, mesh.shape["branch"], mesh.shape["rows"]),
        mesh=mesh,
        in_specs=(
            P(("branch", "rows"), None, None),
            P("rows", "branch", None),
            P(),
            P(),
            P(),
            P(),
            P(),
            P(),
            P(),
            P(),
        ),
        out_specs=(P(("branch", "rows"), None, None), P("rows", "branch", None)),
        check_vma=False,
    )
```

```python
import functools

import jax
import jax.numpy as jnp
from jax import lax
from jax.experimental import pallas as pl
from jax.experimental.pallas import tpu as pltpu
from jax.sharding import PartitionSpec as P

BF16 = jnp.bfloat16
F32 = jnp.float32
AXES = ("branch", "rows")
NT = (((1,), (1,)), ((), ()))
TN = (((0,), (0,)), ((), ()))
VMEM = pl.BlockSpec(memory_space=pltpu.VMEM)
SMEM = pl.BlockSpec(memory_space=pltpu.SMEM)
TARGETS = (0, 4, 1, 2, 7, 3, 6, 5)
HBM = pl.BlockSpec(memory_space=pltpu.HBM)
PARAMS = pltpu.CompilerParams(vmem_limit_bytes=48 * 1024 * 1024)

def standardize_features(values, dimension):
    average = jnp.mean(values, axis=dimension, keepdims=True)
    centered = values - average
    variance = jnp.mean(centered * centered, axis=dimension, keepdims=True)
    return centered * lax.rsqrt(variance + 1e-05)


def alignment_branch(
    homolog_features, transition_expand_matrix, transition_contract_matrix, factor_pair_matrices
):
    local_rows, sequence_length, channel_width = homolog_features.shape
    homolog_real_matrix = homolog_features.astype(jnp.float32)
    standardized_homologs = (
        standardize_features(homolog_real_matrix, -1)
        .astype(jnp.bfloat16)
        .reshape(local_rows * sequence_length, channel_width)
    )
    expanded_activations = jax.nn.relu(
        jnp.dot(standardized_homologs, transition_expand_matrix, preferred_element_type=jnp.float32)
    ).astype(jnp.bfloat16)
    refreshed_homolog_features = (
        homolog_real_matrix
        + jnp.dot(
            expanded_activations, transition_contract_matrix, preferred_element_type=jnp.float32
        ).reshape(homolog_features.shape)
    ).astype(jnp.bfloat16)
    standardized_for_factors = (
        standardize_features(refreshed_homolog_features.astype(jnp.float32), -1)
        .astype(jnp.bfloat16)
        .reshape(local_rows * sequence_length, channel_width)
    )
    projected = jnp.dot(
        standardized_for_factors, factor_pair_matrices, preferred_element_type=jnp.float32
    ).reshape(local_rows, sequence_length, -1)
    channels = projected.shape[-1] // 2
    left_side = projected[..., :channels].astype(jnp.bfloat16)
    right_side = jnp.swapaxes(projected[..., channels:].astype(jnp.bfloat16), 1, 2)
    left_pair = lax.all_gather(left_side, "branch", axis=0, tiled=True)
    left_gathered = lax.all_to_all(left_pair, "rows", split_axis=1, concat_axis=0, tiled=True)
    right_pair = lax.all_to_all(right_side, "branch", split_axis=2, concat_axis=0, tiled=True)
    right_gathered = lax.all_gather(right_pair, "rows", axis=0, tiled=True)
    return (refreshed_homolog_features, left_gathered, right_gathered)


def send_whole(tri_left, tri_right):
    return (
        lax.all_to_all(
            lax.all_to_all(tri_left, "branch", split_axis=0, concat_axis=2, tiled=True),
            "rows",
            split_axis=0,
            concat_axis=1,
            tiled=True,
        ),
        lax.all_to_all(
            lax.all_to_all(tri_right, "branch", split_axis=0, concat_axis=2, tiled=True),
            "rows",
            split_axis=0,
            concat_axis=1,
            tiled=True,
        ),
    )


def send_back(product):
    return lax.all_to_all(
        lax.all_to_all(product, "rows", split_axis=1, concat_axis=0, tiled=True),
        "branch",
        split_axis=2,
        concat_axis=0,
        tiled=True,
    )


def pair_branch(
    pairwise_input,
    triangle_projection_weight,
    triangle_output_weight,
    pairwise_up_weight,
    pairwise_down_weight,
):
    tile_rows, columns, chans = pairwise_input.shape
    pair_float = pairwise_input.astype(jnp.float32)
    pair_norm = standardize_features(pair_float, -1).astype(jnp.bfloat16)
    norm_flat = pair_norm.reshape(tile_rows * columns, chans)
    proj_flat = lax.dot_general(
        triangle_projection_weight,
        norm_flat,
        (((0,), (1,)), ((), ())),
        preferred_element_type=jnp.float32,
    )
    proj_tile = proj_flat[: 4 * chans].reshape(4 * chans, tile_rows, columns)
    gate_vals = jax.nn.sigmoid(proj_flat[4 * chans :])
    tri_left = (jax.nn.sigmoid(proj_tile[chans : 2 * chans]) * proj_tile[:chans]).astype(
        jnp.bfloat16
    )
    tri_right = (jax.nn.sigmoid(proj_tile[3 * chans :]) * proj_tile[2 * chans : 3 * chans]).astype(
        jnp.bfloat16
    )
    left_chan, right_chan = send_whole(tri_left, tri_right)
    product = jnp.einsum(
        "cik,cjk->cij", left_chan, right_chan, preferred_element_type=jnp.float32
    ).astype(jnp.bfloat16)
    product_tile = send_back(product)
    prod_norm = (
        standardize_features(product_tile.astype(jnp.float32), 0)
        .astype(jnp.bfloat16)
        .reshape(chans, tile_rows * columns)
    )
    tri_update = lax.dot_general(
        triangle_output_weight,
        prod_norm,
        (((0,), (0,)), ((), ())),
        preferred_element_type=jnp.float32,
    )
    gated_update = jnp.transpose(gate_vals * tri_update).reshape(tile_rows, columns, chans)
    pair_mid = pair_float + gated_update
    mid_norm = standardize_features(pair_mid, -1).astype(jnp.bfloat16)
    pair_hidden = jax.nn.relu(
        jnp.einsum("ijd,dh->ijh", mid_norm, pairwise_up_weight, preferred_element_type=jnp.float32)
    ).astype(jnp.bfloat16)
    return pair_mid + jnp.einsum(
        "ijh,hd->ijd", pair_hidden, pairwise_down_weight, preferred_element_type=jnp.float32
    )


def outer_product(left_gathered, right_gathered, outer_output_weight):
    total_rows, tile_rows, channels = left_gathered.shape
    columns = right_gathered.shape[2]
    span_cols = 128
    left_flat = left_gathered.reshape(total_rows, tile_rows * channels)
    pieces = []
    for offset in range(0, columns, span_cols):
        right_piece = right_gathered[:, :, offset : offset + span_cols].reshape(
            total_rows, channels * span_cols
        )
        outer_vals = lax.dot_general(
            left_flat, right_piece, (((0,), (0,)), ((), ())), preferred_element_type=jnp.float32
        )
        outer_vals = (
            (outer_vals / total_rows)
            .astype(jnp.bfloat16)
            .reshape(tile_rows, channels * channels, span_cols)
        )
        pieces.append(
            lax.dot_general(
                outer_output_weight,
                outer_vals,
                (((0,), (1,)), ((), ())),
                preferred_element_type=jnp.float32,
            )
        )
    outer_eij = jnp.concatenate(pieces, axis=2)
    return jnp.transpose(outer_eij, (1, 2, 0))


def general_device(
    homolog_features,
    pairwise_input,
    transition_expand_matrix,
    transition_contract_matrix,
    factor_pair_matrices,
    outer_output_weight,
    triangle_projection_weight,
    triangle_output_weight,
    pairwise_up_weight,
    pairwise_down_weight,
):
    refreshed_homolog_features, left_gathered, right_gathered = alignment_branch(
        homolog_features, transition_expand_matrix, transition_contract_matrix, factor_pair_matrices
    )
    pair_mid = pair_branch(
        pairwise_input,
        triangle_projection_weight,
        triangle_output_weight,
        pairwise_up_weight,
        pairwise_down_weight,
    )
    outer_update = outer_product(left_gathered, right_gathered, outer_output_weight)
    pairwise_output = (pair_mid + outer_update).astype(jnp.bfloat16)
    return (refreshed_homolog_features, pairwise_output)


def normed(values, axis):
    average = jnp.mean(values, axis=axis, keepdims=True)
    centered = values - average
    variance = jnp.mean(centered * centered, axis=axis, keepdims=True)
    return (centered * lax.rsqrt(variance + 1e-05)).astype(BF16)


def sigmoid(values):
    return 0.5 * jnp.tanh(0.5 * values) + 0.5


def dot(a, b, dims=(((1,), (0,)), ((), ()))):
    return lax.dot_general(a, b, dims, preferred_element_type=F32)


def cost(flops, nbytes, transcendentals=0):
    return pl.CostEstimate(flops=flops, bytes_accessed=nbytes, transcendentals=transcendentals)


def channel_order(w, sides, source, count):
    chans = w.shape[0]
    col = lax.broadcasted_iota(jnp.int32, (count, chans), 1)
    order = jnp.where(col == source, 1.0, 0.0).astype(BF16)
    return [dot(order, w[:, s * chans : (s + 1) * chans], NT).astype(BF16) for s in sides]


def gated_rows(values, gates, rows_ref, store):
    rows, width, chans = rows_ref.shape
    for i in range(0, rows, 2):
        tokens = rows_ref[i : i + 2].reshape(2 * width, chans)
        result = dot(values, tokens, NT) * sigmoid(dot(gates, tokens, NT))
        store(i, result[:, :width])
        store(i + 1, result[:, width:])


def right_kernel(
    n_branch, x_hbm, w_hbm, sent_hbm, tokens_hbm, x_ref, w_ref, sent_ref, tokens_ref, scr, sems
):
    rows, width, chans = x_ref.shape
    groups, per = sent_ref.shape[:2]
    near = groups // n_branch
    halves = sent_hbm.shape[0] // groups
    columns = w_hbm.at[:, pl.ds(2 * chans, 2 * chans)]
    copies = [
        pltpu.make_async_copy(columns, w_ref, sems.at[0]),
        pltpu.make_async_copy(x_hbm, x_ref, sems.at[1]),
    ]
    for copy in copies:
        copy.start()
    for copy in copies:
        copy.wait()
    values = jnp.transpose(w_ref[:, :chans])
    gates = jnp.transpose(w_ref[:, chans:])
    step = 4
    parts = []
    for i in range(0, rows, step):
        tokens = normed(x_ref[i : i + step].astype(F32), -1)
        tokens_ref[i : i + step] = tokens
        parts.append(tokens.reshape(step * width, chans))
    outs = [pltpu.make_async_copy(tokens_ref, tokens_hbm, sems.at[2])]
    outs[0].start()
    for i, tokens in zip(range(0, rows, step), parts):
        result = dot(values, tokens, NT) * sigmoid(dot(gates, tokens, NT))
        for k in range(step):
            scr[pl.ds(i + k, chans, stride=rows), :] = result[:, k * width : (k + 1) * width]
    span = 4
    for g in range(groups):
        for c in range(per):
            q = (g * per + c) * rows
            sent_ref[g, c] = scr[q : q + rows, :].astype(BF16)
        if g % span == span - 1:
            begin = g + 1 - span
            for h in range(halves):
                to = (begin // near * halves + h) * near + begin % near
                copy = pltpu.make_async_copy(
                    sent_ref.at[pl.ds(begin, span)],
                    sent_hbm.at[pl.ds(to, span)],
                    sems.at[2 + len(outs)],
                )
                copy.start()
                outs.append(copy)
    for copy in outs:
        copy.wait()


def right_operand(x, w, n_branch, devices, per):
    rows, width, chans = x.shape
    groups = chans // per
    return pl.pallas_call(
        functools.partial(right_kernel, n_branch),
        out_shape=[
            jax.ShapeDtypeStruct((devices, per, rows, width), BF16),
            jax.ShapeDtypeStruct(x.shape, BF16),
        ],
        in_specs=[HBM] * 2,
        out_specs=[HBM] * 2,
        scratch_shapes=[
            pltpu.VMEM(x.shape, BF16),
            pltpu.VMEM((chans, 2 * chans), BF16),
            pltpu.VMEM((groups, per, rows, width), BF16),
            pltpu.VMEM(x.shape, BF16),
            pltpu.VMEM((chans * rows, width), F32),
            pltpu.SemaphoreType.DMA((3 + devices // 4,)),
        ],
        cost_estimate=cost(2 * rows * width * chans * 2 * chans, 3 * rows * width * chans * 2),
        name="right_operand",
    )(x, w)


def left_kernel(n_branch, near, where_ref, x_ref, other_ref, w_ref, out_ref, scr, norm_scr):
    rows, _, chans = x_ref.shape
    branch, row_at = where_ref[0], where_ref[1]
    core = lax.bitwise_and(row_at, 1)
    place = lax.shift_right_logical(lax.bitwise_and(row_at, near - 1), 1)
    count = out_ref.shape[0]
    places = count // n_branch
    per = chans // (n_branch * near)

    total = count * per
    q = lax.broadcasted_iota(jnp.int32, (total, chans), 0)
    t = q // per
    group = lax.bitwise_xor(t // places, branch) * near + (
        lax.bitwise_xor(t % places, place) * 2 + core
    )
    values, gates = channel_order(w_ref[...], (0, 1), group * per + q % per, total)

    def store_at(at):
        def store(i, block):
            scr[at, pl.ds(i, total, stride=rows), :] = block

        return store

    gated_rows(values, gates, x_ref, store_at(core))
    for i in range(0, rows, 4):
        norm_scr[i : i + 4] = normed(other_ref[i : i + 4].astype(F32), -1)
    gated_rows(values, gates, norm_scr, store_at(1 - core))
    for t in range(count):
        for c in range(per):
            for k in range(2):
                start = (t * per + c) * rows
                out_ref[t, pl.ds((c * 2 + k) * rows, rows)] = scr[
                    k, start : start + rows, :
                ].astype(BF16)


def left_operand(where, x, other, w, n_branch, near):
    rows, width, chans = x.shape
    count = n_branch * near // 2
    per = chans // (n_branch * near)
    return pl.pallas_call(
        functools.partial(left_kernel, n_branch, near),
        out_shape=jax.ShapeDtypeStruct((count, per * 2 * rows, width), BF16),
        in_specs=[SMEM] + [VMEM] * 3,
        out_specs=VMEM,
        scratch_shapes=[
            pltpu.VMEM((2, count * per * rows, width), F32),
            pltpu.VMEM(x.shape, BF16),
        ],
        compiler_params=PARAMS,
        cost_estimate=cost(4 * x.size * 2 * chans, x.size * 8),
        name="left_operand",
    )(where, x, other, w)


def message_kernel(
    n_branch, near, rows, where_ref, left_ref, seq_ref, far_ref, up_ref, down_ref, factor_ref,
    fresh_ref, *rest
):
    out_refs, (right_scr, left_scr) = rest[:-2], rest[-2:]
    count, size, width = left_ref.shape
    for t, out_ref in zip(TARGETS, out_refs):
        out_ref[:size] = left_ref[t]
    x = [ref[0].astype(F32) for ref in (seq_ref, far_ref)]
    tokens = [normed(v, -1) for v in x]
    hidden = [jnp.maximum(dot(t, up_ref[...]).astype(BF16), 0.0) for t in tokens]
    fresh = [(v + dot(h, down_ref[...])).astype(BF16) for v, h in zip(x, hidden)]
    fresh_ref[0] = fresh[0]
    factor = factor_ref[...]
    depth = factor.shape[0] // 2
    tokens = [normed(v.astype(F32), -1) for v in fresh]
    for k, row in enumerate(tokens):
        right = dot(factor[depth:], row, NT).astype(BF16)
        for b in range(n_branch):
            right_scr[b, k * depth : (k + 1) * depth] = right[:, b * width : (b + 1) * width]
    tiles = [dot(row, factor[:depth], NT).astype(BF16).reshape(-1, 2, rows, depth) for row in tokens]
    for t in range(left_scr.shape[0]):
        left_scr[t] = jnp.concatenate([tile[t, c] for tile in tiles for c in range(2)], axis=1)
    branch, row_at = where_ref[0], where_ref[1]
    place = lax.shift_right_logical(lax.bitwise_and(row_at, near - 1), 1)
    places = count // n_branch
    first = row_at // near * places
    for t, out_ref in zip(TARGETS, out_refs):
        out_ref[size : size + 2 * depth] = right_scr[lax.bitwise_xor(branch, t // places)]
        out_ref[size + 2 * depth :] = left_scr[first + lax.bitwise_xor(place, t % places)]


def messages(where, left, seq, far, up, down, factor, rows, n_branch, near):
    _, length, feats = seq.shape
    depth = factor.shape[0] // 2
    count, size, width = left.shape
    piece = jax.ShapeDtypeStruct((size + 2 * depth + rows, width), BF16)
    fresh, *pieces = pl.pallas_call(
        functools.partial(message_kernel, n_branch, near, rows),
        out_shape=[jax.ShapeDtypeStruct(seq.shape, BF16)] + [piece] * count,
        in_specs=[SMEM] + [VMEM] * 6,
        out_specs=[VMEM] * (1 + count),
        scratch_shapes=[
            pltpu.VMEM((n_branch, 2 * depth, width), BF16),
            pltpu.VMEM((length // rows // 2, rows, width), BF16),
        ],
        compiler_params=PARAMS,
        cost_estimate=cost(2 * 10**10, 4 * feats * up.shape[1]),
        name="msa_transition_and_messages",
    )(where, left, seq, far, up, down, factor)
    return fresh, pieces


def gate_kernel(x_ref, w_ref, out_ref):
    rows, width, chans = x_ref.shape
    tokens = x_ref[...].reshape(rows * width, chans)
    out_ref[...] = sigmoid(dot(tokens, w_ref[:, 4 * chans :])).reshape(rows, width, chans)


def output_gate(x, w):
    rows, width, chans = x.shape
    step = 4
    spec = pl.BlockSpec((step, width, chans), lambda i: (i, 0, 0))
    return pl.pallas_call(
        gate_kernel,
        grid=(rows // step,),
        out_shape=jax.ShapeDtypeStruct(x.shape, F32),
        in_specs=[spec, pl.BlockSpec(w.shape, lambda i: (0, 0))],
        out_specs=spec,
        compiler_params=PARAMS,
        cost_estimate=cost(2 * rows * width * chans * chans, rows * width * chans * 6),
        name="triangle_output_gate",
    )(x, w)


def product_kernel(n_branch, near, where_ref, in_ref, *rest):
    places = near // 2
    left_refs = dict(zip(TARGETS, rest))
    out_hbm, out_ref, sems = rest[n_branch * places :]
    devices, per, rows, width = in_ref.shape
    n_rows = devices // n_branch
    branch, row_at = where_ref[0], where_ref[1]
    place = lax.shift_right_logical(lax.bitwise_and(row_at, near - 1), 1)
    outs = []
    for c in range(per):
        span = slice(c * 2 * rows, (c + 1) * 2 * rows)
        left = jnp.concatenate(
            [
                jnp.concatenate([left_refs[s * places + p][span] for p in range(places)], axis=0)
                for s in range(n_branch)
            ],
            axis=1,
        )
        right = jnp.concatenate(
            [
                in_ref[pl.ds(lax.bitwise_xor(branch, s) * n_rows, n_rows), c].reshape(
                    n_rows * rows, width
                )
                for s in range(n_branch)
            ],
            axis=1,
        )
        product = dot(left, right, NT).astype(BF16)
        for p in range(places):
            at = lax.bitwise_xor(place, p) * 2
            part = product[p * 2 * rows : (p + 1) * 2 * rows]
            for b in range(n_branch):
                for k in range(2):
                    out_ref[n_branch * near - 1 - (b * near + at + k), c] = part[
                        k * rows : (k + 1) * rows, b * width : (b + 1) * width
                    ]
        if c % 2 == 1:
            half = pl.ds(c - 1, 2)
            copy = pltpu.make_async_copy(
                out_ref.at[:, half], out_hbm.at[:, half], sems.at[c // 2]
            )
            copy.start()
            outs.append(copy)
    for copy in outs:
        copy.wait()


def triangle_product(where, received, pieces, n_branch, near):
    devices, per, rows, width = received.shape
    shape = (n_branch * near, per, rows, width)
    return pl.pallas_call(
        functools.partial(product_kernel, n_branch, near),
        out_shape=jax.ShapeDtypeStruct(shape, BF16),
        in_specs=[SMEM] + [VMEM] * (1 + len(pieces)),
        out_specs=HBM,
        scratch_shapes=[pltpu.VMEM(shape, BF16), pltpu.SemaphoreType.DMA((per // 2,))],
        compiler_params=PARAMS,
        cost_estimate=cost(2 * near * rows * received.size, received.size * 4),
        name="triangle_product",
    )(where, received, *pieces)


def pair_output_kernel(
    p_ref, x_ref, gate_ref, outer_ref, w_ref, up_ref, down_ref, out_hbm, scr, out_ref, sems
):
    devices, per, rows, width = p_ref.shape
    chans = devices * per
    step = rows // 2
    shape = (step * width, chans)
    share = up_ref.shape[1] // 4

    def place(i):
        for g in range(devices):
            for c in range(per):
                tile = p_ref[devices - 1 - g, c].astype(F32)[i : i + step]
                scr[pl.ds(i * chans + g * per + c, step, stride=chans), :] = tile

    def triangle(i):
        parts = [
            normed(scr[(i + k) * chans : (i + k + 1) * chans, :], 0) for k in range(step)
        ]
        update = dot(jnp.concatenate(parts, axis=1), w_ref[...], TN)
        x = x_ref[i : i + step].astype(F32).reshape(shape)
        middle = x + gate_ref[i : i + step].reshape(shape) * update
        return middle, normed(middle, -1)

    def transition(i, middle, tokens):
        result = middle + outer_ref[i : i + step].reshape(shape)
        for h in range(0, up_ref.shape[1], share):
            hidden = dot(tokens, up_ref[:, h : h + share]).astype(BF16)
            result = result + dot(jnp.maximum(hidden, 0.0), down_ref[h : h + share])
        out_ref[i : i + step] = result.astype(BF16).reshape(step, width, chans)
        part = pl.ds(i, step)
        copy = pltpu.make_async_copy(out_ref.at[part], out_hbm.at[part], sems.at[i // step])
        copy.start()
        return copy

    middles = []
    for i in range(0, rows, step):
        place(i)
        middles.append(triangle(i))
    copies = [transition(i * step, *middle) for i, middle in enumerate(middles)]
    for copy in copies:
        copy.wait()


def pair_output(product, x, gate, outer, w, up, down):
    devices, per, rows, width = product.shape
    chans = devices * per
    return pl.pallas_call(
        pair_output_kernel,
        out_shape=jax.ShapeDtypeStruct(x.shape, BF16),
        in_specs=[VMEM] * 7,
        out_specs=HBM,
        scratch_shapes=[
            pltpu.VMEM((rows * chans, width), F32),
            pltpu.VMEM(x.shape, BF16),
            pltpu.SemaphoreType.DMA((2,)),
        ],
        compiler_params=PARAMS,
        cost_estimate=cost(2 * x.size * (chans + 2 * up.shape[1]), x.size * 14),
        name="pair_output",
    )(product, x, gate, outer, w, up, down)


def outer_kernel(where_ref, *refs):
    groups, (w_ref, out_ref, right_scr, left_scr, w_scr, m_scr) = refs[:-6], refs[-6:]
    rows, width, chans = out_ref.shape
    total = 2 * sum(ref.shape[0] for ref in groups)
    depth = m_scr.shape[1] // total
    s = 0
    for ref in groups:
        for k in range(ref.shape[0]):
            both = ref[k, 2 * depth :].astype(F32)
            for far in range(2):
                at = s + far * (total // 2)
                side = ref[k, far * depth : (far + 1) * depth].astype(F32)
                right_scr[pl.ds(at, depth, stride=total), :] = side
                left_scr[pl.ds(at, rows, stride=total), :] = both
            s += 1
    right = jnp.transpose(right_scr[...]).astype(BF16)
    both = left_scr[...]
    shift = lax.bitwise_and(where_ref[1], 1) * depth
    first = pltpu.roll(both, width - shift, 1)[:, :depth]
    second = pltpu.roll(both, width - 2 * depth - shift, 1)[:, :depth]
    row = lax.broadcasted_iota(jnp.int32, first.shape, 0)
    left = jnp.where(row % total < total // 2, first, second).astype(BF16)
    w_scr[...] = w_ref[...].astype(F32)
    for d in range(depth):
        part = w_scr[pl.ds(d, depth, stride=depth), :].astype(BF16)
        m_scr[:, d * total : (d + 1) * total] = (
            dot(left, part).astype(BF16).reshape(rows, total, chans)
        )
    for i in range(0, rows, 2):
        pair = jnp.concatenate([m_scr[i], m_scr[i + 1]], axis=1)
        result = dot(right, pair) / total
        out_ref[i] = result[:, :chans]
        out_ref[i + 1] = result[:, chans:]


def outer_update(where, groups, w, rows, chans):
    total = 2 * sum(group.shape[0] for group in groups)
    width = groups[0].shape[2]
    depth = (groups[0].shape[1] - rows) // 2
    return pl.pallas_call(
        outer_kernel,
        out_shape=jax.ShapeDtypeStruct((rows, width, chans), F32),
        in_specs=[SMEM] + [VMEM] * (len(groups) + 1),
        out_specs=VMEM,
        scratch_shapes=[
            pltpu.VMEM((depth * total, width), F32),
            pltpu.VMEM((rows * total, width), F32),
            pltpu.VMEM((depth * depth, chans), F32),
            pltpu.VMEM((rows, depth * total, chans), BF16),
        ],
        compiler_params=PARAMS,
        cost_estimate=cost(2 * rows * width * depth * total * chans * 2, rows * width * chans * 4),
        name="outer_product_mean",
    )(where, *groups, w)


def swap(x, n_branch, n_rows, mask):
    count = n_branch * n_rows
    return lax.ppermute(x, AXES, [(d, d ^ mask) for d in range(count)])


def own_channels_device(
    n_branch,
    n_rows,
    homolog_features,
    pairwise_input,
    transition_expand_matrix,
    transition_contract_matrix,
    factor_pair_matrices,
    outer_output_weight,
    triangle_projection_weight,
    triangle_output_weight,
    pairwise_up_weight,
    pairwise_down_weight,
):
    rows, _, chans = pairwise_input.shape
    near = 8
    halves = n_rows // near
    places = near // 2
    per = chans // (n_branch * near)
    where = jnp.stack([lax.axis_index("branch"), lax.axis_index("rows")]).astype(jnp.int32)

    far_row = swap(homolog_features, n_branch, n_rows, near)
    sent, tokens = right_operand(
        pairwise_input, triangle_projection_weight, n_branch, n_branch * n_rows, per
    )
    received = lax.all_to_all(sent, AXES, 0, 0, tiled=True)

    other = swap(pairwise_input, n_branch, n_rows, 1)
    left = left_operand(where, tokens, other, triangle_projection_weight, n_branch, near)
    fresh, pieces = messages(
        where,
        left,
        homolog_features,
        far_row,
        transition_expand_matrix,
        transition_contract_matrix,
        jnp.transpose(factor_pair_matrices),
        rows,
        n_branch,
        near,
    )
    moved = [
        piece if t == 0 else swap(piece, n_branch, n_rows, t // places * n_rows + t % places * 2)
        for t, piece in zip(TARGETS, pieces)
    ]
    mine = jnp.stack([piece[per * 2 * rows :] for piece in moved])
    groups = [mine, swap(mine, n_branch, n_rows, 1)]
    outer = outer_update(where, groups, outer_output_weight, rows, chans)
    gate_tokens, _ = lax.optimization_barrier((tokens, moved[0]))
    gate = output_gate(gate_tokens, triangle_projection_weight)

    product = triangle_product(where, received, moved, n_branch, near)
    members = [
        [b * n_rows + h * near + k for b in range(n_branch) for k in range(near)][::-1]
        for h in range(halves)
    ]
    returned = lax.all_to_all(product, AXES, 0, 0, axis_index_groups=members, tiled=True)
    pairwise_output = pair_output(
        returned,
        pairwise_input,
        gate,
        outer,
        triangle_output_weight,
        pairwise_up_weight,
        pairwise_down_weight,
    )
    return (fresh, pairwise_output)


def on_device(n_branch, n_rows, homolog_features, pairwise_input, *weights):
    rows, width, chans = pairwise_input.shape
    near = 8
    halves = n_rows // near
    fits = (
        homolog_features.shape[0] == 1
        and halves == 2
        and n_branch == 2
        and n_rows % near == 0
        and chans % (n_branch * near) == 0
        and rows == 16
        and width == 128
        and homolog_features.shape[1] == n_rows * rows == n_branch * width
        and 2 * weights[2].shape[1] == width
    )
    if fits:
        return own_channels_device(n_branch, n_rows, homolog_features, pairwise_input, *weights)
    return general_device(homolog_features, pairwise_input, *weights)


def solution(mesh):
    return jax.shard_map(
        functools.partial(on_device, mesh.shape["branch"], mesh.shape["rows"]),
        mesh=mesh,
        in_specs=(
            P(("branch", "rows"), None, None),
            P("rows", "branch", None),
            P(),
            P(),
            P(),
            P(),
            P(),
            P(),
            P(),
            P(),
        ),
        out_specs=(P(("branch", "rows"), None, None), P("rows", "branch", None)),
        check_vma=False,
    )
```

```python
import functools

import jax
import jax.numpy as jnp
from jax import lax
from jax.experimental import pallas as pl
from jax.experimental.pallas import tpu as pltpu
from jax.sharding import PartitionSpec as P

BF16 = jnp.bfloat16
F32 = jnp.float32
AXES = ("branch", "rows")
NT = (((1,), (1,)), ((), ()))
TN = (((0,), (0,)), ((), ()))
VMEM = pl.BlockSpec(memory_space=pltpu.VMEM)
SMEM = pl.BlockSpec(memory_space=pltpu.SMEM)
TARGETS = (0, 4, 1, 2, 7, 3, 6, 5)
HBM = pl.BlockSpec(memory_space=pltpu.HBM)
PARAMS = pltpu.CompilerParams(vmem_limit_bytes=48 * 1024 * 1024)

def standardize_features(values, dimension):
    average = jnp.mean(values, axis=dimension, keepdims=True)
    centered = values - average
    variance = jnp.mean(centered * centered, axis=dimension, keepdims=True)
    return centered * lax.rsqrt(variance + 1e-05)


def alignment_branch(
    homolog_features, transition_expand_matrix, transition_contract_matrix, factor_pair_matrices
):
    local_rows, sequence_length, channel_width = homolog_features.shape
    homolog_real_matrix = homolog_features.astype(jnp.float32)
    standardized_homologs = (
        standardize_features(homolog_real_matrix, -1)
        .astype(jnp.bfloat16)
        .reshape(local_rows * sequence_length, channel_width)
    )
    expanded_activations = jax.nn.relu(
        jnp.dot(standardized_homologs, transition_expand_matrix, preferred_element_type=jnp.float32)
    ).astype(jnp.bfloat16)
    refreshed_homolog_features = (
        homolog_real_matrix
        + jnp.dot(
            expanded_activations, transition_contract_matrix, preferred_element_type=jnp.float32
        ).reshape(homolog_features.shape)
    ).astype(jnp.bfloat16)
    standardized_for_factors = (
        standardize_features(refreshed_homolog_features.astype(jnp.float32), -1)
        .astype(jnp.bfloat16)
        .reshape(local_rows * sequence_length, channel_width)
    )
    projected = jnp.dot(
        standardized_for_factors, factor_pair_matrices, preferred_element_type=jnp.float32
    ).reshape(local_rows, sequence_length, -1)
    channels = projected.shape[-1] // 2
    left_side = projected[..., :channels].astype(jnp.bfloat16)
    right_side = jnp.swapaxes(projected[..., channels:].astype(jnp.bfloat16), 1, 2)
    left_pair = lax.all_gather(left_side, "branch", axis=0, tiled=True)
    left_gathered = lax.all_to_all(left_pair, "rows", split_axis=1, concat_axis=0, tiled=True)
    right_pair = lax.all_to_all(right_side, "branch", split_axis=2, concat_axis=0, tiled=True)
    right_gathered = lax.all_gather(right_pair, "rows", axis=0, tiled=True)
    return (refreshed_homolog_features, left_gathered, right_gathered)


def send_whole(tri_left, tri_right):
    return (
        lax.all_to_all(
            lax.all_to_all(tri_left, "branch", split_axis=0, concat_axis=2, tiled=True),
            "rows",
            split_axis=0,
            concat_axis=1,
            tiled=True,
        ),
        lax.all_to_all(
            lax.all_to_all(tri_right, "branch", split_axis=0, concat_axis=2, tiled=True),
            "rows",
            split_axis=0,
            concat_axis=1,
            tiled=True,
        ),
    )


def send_back(product):
    return lax.all_to_all(
        lax.all_to_all(product, "rows", split_axis=1, concat_axis=0, tiled=True),
        "branch",
        split_axis=2,
        concat_axis=0,
        tiled=True,
    )


def pair_branch(
    pairwise_input,
    triangle_projection_weight,
    triangle_output_weight,
    pairwise_up_weight,
    pairwise_down_weight,
):
    tile_rows, columns, chans = pairwise_input.shape
    pair_float = pairwise_input.astype(jnp.float32)
    pair_norm = standardize_features(pair_float, -1).astype(jnp.bfloat16)
    norm_flat = pair_norm.reshape(tile_rows * columns, chans)
    proj_flat = lax.dot_general(
        triangle_projection_weight,
        norm_flat,
        (((0,), (1,)), ((), ())),
        preferred_element_type=jnp.float32,
    )
    proj_tile = proj_flat[: 4 * chans].reshape(4 * chans, tile_rows, columns)
    gate_vals = jax.nn.sigmoid(proj_flat[4 * chans :])
    tri_left = (jax.nn.sigmoid(proj_tile[chans : 2 * chans]) * proj_tile[:chans]).astype(
        jnp.bfloat16
    )
    tri_right = (jax.nn.sigmoid(proj_tile[3 * chans :]) * proj_tile[2 * chans : 3 * chans]).astype(
        jnp.bfloat16
    )
    left_chan, right_chan = send_whole(tri_left, tri_right)
    product = jnp.einsum(
        "cik,cjk->cij", left_chan, right_chan, preferred_element_type=jnp.float32
    ).astype(jnp.bfloat16)
    product_tile = send_back(product)
    prod_norm = (
        standardize_features(product_tile.astype(jnp.float32), 0)
        .astype(jnp.bfloat16)
        .reshape(chans, tile_rows * columns)
    )
    tri_update = lax.dot_general(
        triangle_output_weight,
        prod_norm,
        (((0,), (0,)), ((), ())),
        preferred_element_type=jnp.float32,
    )
    gated_update = jnp.transpose(gate_vals * tri_update).reshape(tile_rows, columns, chans)
    pair_mid = pair_float + gated_update
    mid_norm = standardize_features(pair_mid, -1).astype(jnp.bfloat16)
    pair_hidden = jax.nn.relu(
        jnp.einsum("ijd,dh->ijh", mid_norm, pairwise_up_weight, preferred_element_type=jnp.float32)
    ).astype(jnp.bfloat16)
    return pair_mid + jnp.einsum(
        "ijh,hd->ijd", pair_hidden, pairwise_down_weight, preferred_element_type=jnp.float32
    )


def outer_product(left_gathered, right_gathered, outer_output_weight):
    total_rows, tile_rows, channels = left_gathered.shape
    columns = right_gathered.shape[2]
    span_cols = 128
    left_flat = left_gathered.reshape(total_rows, tile_rows * channels)
    pieces = []
    for offset in range(0, columns, span_cols):
        right_piece = right_gathered[:, :, offset : offset + span_cols].reshape(
            total_rows, channels * span_cols
        )
        outer_vals = lax.dot_general(
            left_flat, right_piece, (((0,), (0,)), ((), ())), preferred_element_type=jnp.float32
        )
        outer_vals = (
            (outer_vals / total_rows)
            .astype(jnp.bfloat16)
            .reshape(tile_rows, channels * channels, span_cols)
        )
        pieces.append(
            lax.dot_general(
                outer_output_weight,
                outer_vals,
                (((0,), (1,)), ((), ())),
                preferred_element_type=jnp.float32,
            )
        )
    outer_eij = jnp.concatenate(pieces, axis=2)
    return jnp.transpose(outer_eij, (1, 2, 0))


def general_device(
    homolog_features,
    pairwise_input,
    transition_expand_matrix,
    transition_contract_matrix,
    factor_pair_matrices,
    outer_output_weight,
    triangle_projection_weight,
    triangle_output_weight,
    pairwise_up_weight,
    pairwise_down_weight,
):
    refreshed_homolog_features, left_gathered, right_gathered = alignment_branch(
        homolog_features, transition_expand_matrix, transition_contract_matrix, factor_pair_matrices
    )
    pair_mid = pair_branch(
        pairwise_input,
        triangle_projection_weight,
        triangle_output_weight,
        pairwise_up_weight,
        pairwise_down_weight,
    )
    outer_update = outer_product(left_gathered, right_gathered, outer_output_weight)
    pairwise_output = (pair_mid + outer_update).astype(jnp.bfloat16)
    return (refreshed_homolog_features, pairwise_output)


def normed(values, axis):
    average = jnp.mean(values, axis=axis, keepdims=True)
    centered = values - average
    variance = jnp.mean(centered * centered, axis=axis, keepdims=True)
    return (centered * lax.rsqrt(variance + 1e-05)).astype(BF16)


def sigmoid(values):
    return 0.5 * jnp.tanh(0.5 * values) + 0.5


def dot(a, b, dims=(((1,), (0,)), ((), ()))):
    return lax.dot_general(a, b, dims, preferred_element_type=F32)


def cost(flops, nbytes, transcendentals=0):
    return pl.CostEstimate(flops=flops, bytes_accessed=nbytes, transcendentals=transcendentals)


def channel_order(w, sides, source, count):
    chans = w.shape[0]
    col = lax.broadcasted_iota(jnp.int32, (count, chans), 1)
    order = jnp.where(col == source, 1.0, 0.0).astype(BF16)
    return [dot(order, w[:, s * chans : (s + 1) * chans], NT).astype(BF16) for s in sides]


def gated_rows(values, gates, rows_ref, store):
    rows, width, chans = rows_ref.shape
    for i in range(0, rows, 2):
        tokens = rows_ref[i : i + 2].reshape(2 * width, chans)
        result = dot(values, tokens, NT) * sigmoid(dot(gates, tokens, NT))
        store(i, result[:, :width])
        store(i + 1, result[:, width:])


def right_kernel(
    n_branch, x_hbm, w_hbm, sent_hbm, tokens_hbm, x_ref, w_ref, sent_ref, tokens_ref, scr, sems
):
    rows, width, chans = x_ref.shape
    groups, per = sent_ref.shape[:2]
    near = groups // n_branch
    halves = sent_hbm.shape[0] // groups
    columns = w_hbm.at[:, pl.ds(2 * chans, 2 * chans)]
    copies = [
        pltpu.make_async_copy(columns, w_ref, sems.at[0]),
        pltpu.make_async_copy(x_hbm, x_ref, sems.at[1]),
    ]
    for copy in copies:
        copy.start()
    for copy in copies:
        copy.wait()
    values = jnp.transpose(w_ref[:, :chans])
    gates = jnp.transpose(w_ref[:, chans:])
    step = 4
    parts = []
    for i in range(0, rows, step):
        tokens = normed(x_ref[i : i + step].astype(F32), -1)
        tokens_ref[i : i + step] = tokens
        parts.append(tokens.reshape(step * width, chans))
    outs = [pltpu.make_async_copy(tokens_ref, tokens_hbm, sems.at[2])]
    outs[0].start()
    for i, tokens in zip(range(0, rows, step), parts):
        result = dot(values, tokens, NT) * sigmoid(dot(gates, tokens, NT))
        for k in range(step):
            scr[pl.ds(i + k, chans, stride=rows), :] = result[:, k * width : (k + 1) * width]
    span = 4
    for g in range(groups):
        for c in range(per):
            q = (g * per + c) * rows
            sent_ref[g, c] = scr[q : q + rows, :].astype(BF16)
        if g % span == span - 1:
            begin = g + 1 - span
            for h in range(halves):
                to = (begin // near * halves + h) * near + begin % near
                copy = pltpu.make_async_copy(
                    sent_ref.at[pl.ds(begin, span)],
                    sent_hbm.at[pl.ds(to, span)],
                    sems.at[2 + len(outs)],
                )
                copy.start()
                outs.append(copy)
    for copy in outs:
        copy.wait()


def right_operand(x, w, n_branch, devices, per):
    rows, width, chans = x.shape
    groups = chans // per
    return pl.pallas_call(
        functools.partial(right_kernel, n_branch),
        out_shape=[
            jax.ShapeDtypeStruct((devices, per, rows, width), BF16),
            jax.ShapeDtypeStruct(x.shape, BF16),
        ],
        in_specs=[HBM] * 2,
        out_specs=[HBM] * 2,
        scratch_shapes=[
            pltpu.VMEM(x.shape, BF16),
            pltpu.VMEM((chans, 2 * chans), BF16),
            pltpu.VMEM((groups, per, rows, width), BF16),
            pltpu.VMEM(x.shape, BF16),
            pltpu.VMEM((chans * rows, width), F32),
            pltpu.SemaphoreType.DMA((3 + devices // 4,)),
        ],
        cost_estimate=cost(2 * rows * width * chans * 2 * chans, 3 * rows * width * chans * 2),
        name="right_operand",
    )(x, w)


def left_kernel(n_branch, near, where_ref, x_ref, other_ref, w_ref, out_ref, scr, norm_scr):
    rows, _, chans = x_ref.shape
    branch, row_at = where_ref[0], where_ref[1]
    core = lax.bitwise_and(row_at, 1)
    place = lax.shift_right_logical(lax.bitwise_and(row_at, near - 1), 1)
    count = out_ref.shape[0]
    places = count // n_branch
    per = chans // (n_branch * near)

    total = count * per
    q = lax.broadcasted_iota(jnp.int32, (total, chans), 0)
    t = q // per
    group = lax.bitwise_xor(t // places, branch) * near + (
        lax.bitwise_xor(t % places, place) * 2 + core
    )
    values, gates = channel_order(w_ref[...], (0, 1), group * per + q % per, total)

    def store_at(at):
        def store(i, block):
            scr[at, pl.ds(i, total, stride=rows), :] = block

        return store

    gated_rows(values, gates, x_ref, store_at(core))
    for i in range(0, rows, 4):
        norm_scr[i : i + 4] = normed(other_ref[i : i + 4].astype(F32), -1)
    gated_rows(values, gates, norm_scr, store_at(1 - core))
    for t in range(count):
        for c in range(per):
            for k in range(2):
                start = (t * per + c) * rows
                out_ref[t, pl.ds((c * 2 + k) * rows, rows)] = scr[
                    k, start : start + rows, :
                ].astype(BF16)


def left_operand(where, x, other, w, n_branch, near):
    rows, width, chans = x.shape
    count = n_branch * near // 2
    per = chans // (n_branch * near)
    return pl.pallas_call(
        functools.partial(left_kernel, n_branch, near),
        out_shape=jax.ShapeDtypeStruct((count, per * 2 * rows, width), BF16),
        in_specs=[SMEM] + [VMEM] * 3,
        out_specs=VMEM,
        scratch_shapes=[
            pltpu.VMEM((2, count * per * rows, width), F32),
            pltpu.VMEM(x.shape, BF16),
        ],
        compiler_params=PARAMS,
        cost_estimate=cost(4 * x.size * 2 * chans, x.size * 8),
        name="left_operand",
    )(where, x, other, w)


def message_kernel(
    n_branch, near, rows, where_ref, left_ref, seq_ref, far_ref, up_ref, down_ref, factor_ref,
    fresh_ref, *rest
):
    out_refs, (right_scr, left_scr) = rest[:-2], rest[-2:]
    count, size, width = left_ref.shape
    for t, out_ref in zip(TARGETS, out_refs):
        out_ref[:size] = left_ref[t]
    x = [ref[0].astype(F32) for ref in (seq_ref, far_ref)]
    tokens = [normed(v, -1) for v in x]
    hidden = [jnp.maximum(dot(t, up_ref[...]).astype(BF16), 0.0) for t in tokens]
    fresh = [(v + dot(h, down_ref[...])).astype(BF16) for v, h in zip(x, hidden)]
    fresh_ref[0] = fresh[0]
    factor = factor_ref[...]
    depth = factor.shape[0] // 2
    tokens = [normed(v.astype(F32), -1) for v in fresh]
    for k, row in enumerate(tokens):
        right = dot(factor[depth:], row, NT).astype(BF16)
        for b in range(n_branch):
            right_scr[b, k * depth : (k + 1) * depth] = right[:, b * width : (b + 1) * width]
    tiles = [dot(row, factor[:depth], NT).astype(BF16).reshape(-1, 2, rows, depth) for row in tokens]
    for t in range(left_scr.shape[0]):
        left_scr[t] = jnp.concatenate([tile[t, c] for tile in tiles for c in range(2)], axis=1)
    branch, row_at = where_ref[0], where_ref[1]
    place = lax.shift_right_logical(lax.bitwise_and(row_at, near - 1), 1)
    places = count // n_branch
    first = row_at // near * places
    for t, out_ref in zip(TARGETS, out_refs):
        out_ref[size : size + 2 * depth] = right_scr[lax.bitwise_xor(branch, t // places)]
        out_ref[size + 2 * depth :] = left_scr[first + lax.bitwise_xor(place, t % places)]


def messages(where, left, seq, far, up, down, factor, rows, n_branch, near):
    _, length, feats = seq.shape
    depth = factor.shape[0] // 2
    count, size, width = left.shape
    piece = jax.ShapeDtypeStruct((size + 2 * depth + rows, width), BF16)
    fresh, *pieces = pl.pallas_call(
        functools.partial(message_kernel, n_branch, near, rows),
        out_shape=[jax.ShapeDtypeStruct(seq.shape, BF16)] + [piece] * count,
        in_specs=[SMEM] + [VMEM] * 6,
        out_specs=[VMEM] * (1 + count),
        scratch_shapes=[
            pltpu.VMEM((n_branch, 2 * depth, width), BF16),
            pltpu.VMEM((length // rows // 2, rows, width), BF16),
        ],
        compiler_params=PARAMS,
        cost_estimate=cost(2 * 10**10, 4 * feats * up.shape[1]),
        name="msa_transition_and_messages",
    )(where, left, seq, far, up, down, factor)
    return fresh, pieces


def gate_kernel(x_ref, w_ref, out_ref):
    rows, width, chans = x_ref.shape
    tokens = x_ref[...].reshape(rows * width, chans)
    out_ref[...] = sigmoid(dot(tokens, w_ref[:, 4 * chans :])).reshape(rows, width, chans)


def output_gate(x, w):
    rows, width, chans = x.shape
    step = 4
    spec = pl.BlockSpec((step, width, chans), lambda i: (i, 0, 0))
    return pl.pallas_call(
        gate_kernel,
        grid=(rows // step,),
        out_shape=jax.ShapeDtypeStruct(x.shape, F32),
        in_specs=[spec, pl.BlockSpec(w.shape, lambda i: (0, 0))],
        out_specs=spec,
        compiler_params=PARAMS,
        cost_estimate=cost(2 * rows * width * chans * chans, rows * width * chans * 6),
        name="triangle_output_gate",
    )(x, w)


def product_kernel(n_branch, near, where_ref, in_ref, *rest):
    places = near // 2
    left_refs = dict(zip(TARGETS, rest))
    out_hbm, out_ref, sems = rest[n_branch * places :]
    devices, per, rows, width = in_ref.shape
    n_rows = devices // n_branch
    branch, row_at = where_ref[0], where_ref[1]
    place = lax.shift_right_logical(lax.bitwise_and(row_at, near - 1), 1)
    outs = []
    for c in range(per):
        span = slice(c * 2 * rows, (c + 1) * 2 * rows)
        left = jnp.concatenate(
            [
                jnp.concatenate([left_refs[s * places + p][span] for p in range(places)], axis=0)
                for s in range(n_branch)
            ],
            axis=1,
        )
        right = jnp.concatenate(
            [
                in_ref[pl.ds(lax.bitwise_xor(branch, s) * n_rows, n_rows), c].reshape(
                    n_rows * rows, width
                )
                for s in range(n_branch)
            ],
            axis=1,
        )
        product = dot(left, right, NT).astype(BF16)
        for p in range(places):
            at = lax.bitwise_xor(place, p) * 2
            part = product[p * 2 * rows : (p + 1) * 2 * rows]
            for b in range(n_branch):
                for k in range(2):
                    out_ref[n_branch * near - 1 - (b * near + at + k), c] = part[
                        k * rows : (k + 1) * rows, b * width : (b + 1) * width
                    ]
        if c % 2 == 1:
            half = pl.ds(c - 1, 2)
            copy = pltpu.make_async_copy(
                out_ref.at[:, half], out_hbm.at[:, half], sems.at[c // 2]
            )
            copy.start()
            outs.append(copy)
    for copy in outs:
        copy.wait()


def triangle_product(where, received, pieces, n_branch, near):
    devices, per, rows, width = received.shape
    shape = (n_branch * near, per, rows, width)
    return pl.pallas_call(
        functools.partial(product_kernel, n_branch, near),
        out_shape=jax.ShapeDtypeStruct(shape, BF16),
        in_specs=[SMEM] + [VMEM] * (1 + len(pieces)),
        out_specs=HBM,
        scratch_shapes=[pltpu.VMEM(shape, BF16), pltpu.SemaphoreType.DMA((per // 2,))],
        compiler_params=PARAMS,
        cost_estimate=cost(2 * near * rows * received.size, received.size * 4),
        name="triangle_product",
    )(where, received, *pieces)


def pair_output_kernel(
    p_ref, x_ref, gate_ref, outer_ref, w_ref, up_ref, down_ref, out_hbm, scr, out_ref, sems
):
    devices, per, rows, width = p_ref.shape
    chans = devices * per
    step = rows // 2
    shape = (step * width, chans)
    share = up_ref.shape[1] // 4

    for g in range(devices):
        for c in range(per):
            k = (g * per + c) * rows
            scr[k : k + rows, :] = p_ref[devices - 1 - g, c].astype(F32)

    def triangle(i):
        parts = [
            normed(scr[pl.ds(i + k, chans, stride=rows), :], 0) for k in range(step)
        ]
        update = dot(jnp.concatenate(parts, axis=1), w_ref[...], TN)
        x = x_ref[i : i + step].astype(F32).reshape(shape)
        middle = x + gate_ref[i : i + step].reshape(shape) * update
        return middle, normed(middle, -1)

    def transition(i, middle, tokens):
        result = middle + outer_ref[i : i + step].reshape(shape)
        for h in range(0, up_ref.shape[1], share):
            hidden = dot(tokens, up_ref[:, h : h + share]).astype(BF16)
            result = result + dot(jnp.maximum(hidden, 0.0), down_ref[h : h + share])
        out_ref[i : i + step] = result.astype(BF16).reshape(step, width, chans)
        part = pl.ds(i, step)
        copy = pltpu.make_async_copy(out_ref.at[part], out_hbm.at[part], sems.at[i // step])
        copy.start()
        return copy

    middles = [triangle(i) for i in range(0, rows, step)]
    copies = [transition(i * step, *middle) for i, middle in enumerate(middles)]
    for copy in copies:
        copy.wait()


def pair_output(product, x, gate, outer, w, up, down):
    devices, per, rows, width = product.shape
    chans = devices * per
    return pl.pallas_call(
        pair_output_kernel,
        out_shape=jax.ShapeDtypeStruct(x.shape, BF16),
        in_specs=[VMEM] * 7,
        out_specs=HBM,
        scratch_shapes=[
            pltpu.VMEM((rows * chans, width), F32),
            pltpu.VMEM(x.shape, BF16),
            pltpu.SemaphoreType.DMA((2,)),
        ],
        compiler_params=PARAMS,
        cost_estimate=cost(2 * x.size * (chans + 2 * up.shape[1]), x.size * 14),
        name="pair_output",
    )(product, x, gate, outer, w, up, down)


def outer_kernel(where_ref, *refs):
    groups, (w_ref, out_ref, right_scr, left_scr, w_scr, m_scr) = refs[:-6], refs[-6:]
    rows, width, chans = out_ref.shape
    total = 2 * sum(ref.shape[0] for ref in groups)
    depth = m_scr.shape[1] // total
    s = 0
    for ref in groups:
        for k in range(ref.shape[0]):
            both = ref[k, 2 * depth :].astype(F32)
            for far in range(2):
                at = s + far * (total // 2)
                side = ref[k, far * depth : (far + 1) * depth].astype(F32)
                right_scr[pl.ds(at, depth, stride=total), :] = side
                left_scr[pl.ds(at, rows, stride=total), :] = both
            s += 1
    right = jnp.transpose(right_scr[...]).astype(BF16)
    both = left_scr[...]
    shift = lax.bitwise_and(where_ref[1], 1) * depth
    first = pltpu.roll(both, width - shift, 1)[:, :depth]
    second = pltpu.roll(both, width - 2 * depth - shift, 1)[:, :depth]
    row = lax.broadcasted_iota(jnp.int32, first.shape, 0)
    left = jnp.where(row % total < total // 2, first, second).astype(BF16)
    w_scr[...] = w_ref[...].astype(F32)
    for d in range(depth):
        part = w_scr[pl.ds(d, depth, stride=depth), :].astype(BF16)
        m_scr[:, d * total : (d + 1) * total] = (
            dot(left, part).astype(BF16).reshape(rows, total, chans)
        )
    for i in range(0, rows, 2):
        pair = jnp.concatenate([m_scr[i], m_scr[i + 1]], axis=1)
        result = dot(right, pair) / total
        out_ref[i] = result[:, :chans]
        out_ref[i + 1] = result[:, chans:]


def outer_update(where, groups, w, rows, chans):
    total = 2 * sum(group.shape[0] for group in groups)
    width = groups[0].shape[2]
    depth = (groups[0].shape[1] - rows) // 2
    return pl.pallas_call(
        outer_kernel,
        out_shape=jax.ShapeDtypeStruct((rows, width, chans), F32),
        in_specs=[SMEM] + [VMEM] * (len(groups) + 1),
        out_specs=VMEM,
        scratch_shapes=[
            pltpu.VMEM((depth * total, width), F32),
            pltpu.VMEM((rows * total, width), F32),
            pltpu.VMEM((depth * depth, chans), F32),
            pltpu.VMEM((rows, depth * total, chans), BF16),
        ],
        compiler_params=PARAMS,
        cost_estimate=cost(2 * rows * width * depth * total * chans * 2, rows * width * chans * 4),
        name="outer_product_mean",
    )(where, *groups, w)


def swap(x, n_branch, n_rows, mask):
    count = n_branch * n_rows
    return lax.ppermute(x, AXES, [(d, d ^ mask) for d in range(count)])


def own_channels_device(
    n_branch,
    n_rows,
    homolog_features,
    pairwise_input,
    transition_expand_matrix,
    transition_contract_matrix,
    factor_pair_matrices,
    outer_output_weight,
    triangle_projection_weight,
    triangle_output_weight,
    pairwise_up_weight,
    pairwise_down_weight,
):
    rows, _, chans = pairwise_input.shape
    near = 8
    halves = n_rows // near
    places = near // 2
    per = chans // (n_branch * near)
    where = jnp.stack([lax.axis_index("branch"), lax.axis_index("rows")]).astype(jnp.int32)

    far_row = swap(homolog_features, n_branch, n_rows, near)
    sent, tokens = right_operand(
        pairwise_input, triangle_projection_weight, n_branch, n_branch * n_rows, per
    )
    received = lax.all_to_all(sent, AXES, 0, 0, tiled=True)

    other = swap(pairwise_input, n_branch, n_rows, 1)
    left = left_operand(where, tokens, other, triangle_projection_weight, n_branch, near)
    fresh, pieces = messages(
        where,
        left,
        homolog_features,
        far_row,
        transition_expand_matrix,
        transition_contract_matrix,
        jnp.transpose(factor_pair_matrices),
        rows,
        n_branch,
        near,
    )
    moved = [
        piece if t == 0 else swap(piece, n_branch, n_rows, t // places * n_rows + t % places * 2)
        for t, piece in zip(TARGETS, pieces)
    ]
    mine = jnp.stack([piece[per * 2 * rows :] for piece in moved])
    groups = [mine, swap(mine, n_branch, n_rows, 1)]
    outer = outer_update(where, groups, outer_output_weight, rows, chans)
    gate_tokens, _ = lax.optimization_barrier((tokens, moved[0]))
    gate = output_gate(gate_tokens, triangle_projection_weight)

    product = triangle_product(where, received, moved, n_branch, near)
    members = [
        [b * n_rows + h * near + k for b in range(n_branch) for k in range(near)][::-1]
        for h in range(halves)
    ]
    returned = lax.all_to_all(product, AXES, 0, 0, axis_index_groups=members, tiled=True)
    pairwise_output = pair_output(
        returned,
        pairwise_input,
        gate,
        outer,
        triangle_output_weight,
        pairwise_up_weight,
        pairwise_down_weight,
    )
    return (fresh, pairwise_output)


def on_device(n_branch, n_rows, homolog_features, pairwise_input, *weights):
    rows, width, chans = pairwise_input.shape
    near = 8
    halves = n_rows // near
    fits = (
        homolog_features.shape[0] == 1
        and halves == 2
        and n_branch == 2
        and n_rows % near == 0
        and chans % (n_branch * near) == 0
        and rows == 16
        and width == 128
        and homolog_features.shape[1] == n_rows * rows == n_branch * width
        and 2 * weights[2].shape[1] == width
    )
    if fits:
        return own_channels_device(n_branch, n_rows, homolog_features, pairwise_input, *weights)
    return general_device(homolog_features, pairwise_input, *weights)


def solution(mesh):
    return jax.shard_map(
        functools.partial(on_device, mesh.shape["branch"], mesh.shape["rows"]),
        mesh=mesh,
        in_specs=(
            P(("branch", "rows"), None, None),
            P("rows", "branch", None),
            P(),
            P(),
            P(),
            P(),
            P(),
            P(),
            P(),
            P(),
        ),
        out_specs=(P(("branch", "rows"), None, None), P("rows", "branch", None)),
        check_vma=False,
    )
```

```python
import functools

import jax
import jax.numpy as jnp
from jax import lax
from jax.experimental import pallas as pl
from jax.experimental.pallas import tpu as pltpu
from jax.sharding import PartitionSpec as P

BF16 = jnp.bfloat16
F32 = jnp.float32
AXES = ("branch", "rows")
NT = (((1,), (1,)), ((), ()))
TN = (((0,), (0,)), ((), ()))
VMEM = pl.BlockSpec(memory_space=pltpu.VMEM)
SMEM = pl.BlockSpec(memory_space=pltpu.SMEM)
TARGETS = (0, 4, 1, 2, 7, 3, 6, 5)
HBM = pl.BlockSpec(memory_space=pltpu.HBM)
PARAMS = pltpu.CompilerParams(vmem_limit_bytes=48 * 1024 * 1024)

def standardize_features(values, dimension):
    average = jnp.mean(values, axis=dimension, keepdims=True)
    centered = values - average
    variance = jnp.mean(centered * centered, axis=dimension, keepdims=True)
    return centered * lax.rsqrt(variance + 1e-05)


def alignment_branch(
    homolog_features, transition_expand_matrix, transition_contract_matrix, factor_pair_matrices
):
    local_rows, sequence_length, channel_width = homolog_features.shape
    homolog_real_matrix = homolog_features.astype(jnp.float32)
    standardized_homologs = (
        standardize_features(homolog_real_matrix, -1)
        .astype(jnp.bfloat16)
        .reshape(local_rows * sequence_length, channel_width)
    )
    expanded_activations = jax.nn.relu(
        jnp.dot(standardized_homologs, transition_expand_matrix, preferred_element_type=jnp.float32)
    ).astype(jnp.bfloat16)
    refreshed_homolog_features = (
        homolog_real_matrix
        + jnp.dot(
            expanded_activations, transition_contract_matrix, preferred_element_type=jnp.float32
        ).reshape(homolog_features.shape)
    ).astype(jnp.bfloat16)
    standardized_for_factors = (
        standardize_features(refreshed_homolog_features.astype(jnp.float32), -1)
        .astype(jnp.bfloat16)
        .reshape(local_rows * sequence_length, channel_width)
    )
    projected = jnp.dot(
        standardized_for_factors, factor_pair_matrices, preferred_element_type=jnp.float32
    ).reshape(local_rows, sequence_length, -1)
    channels = projected.shape[-1] // 2
    left_side = projected[..., :channels].astype(jnp.bfloat16)
    right_side = jnp.swapaxes(projected[..., channels:].astype(jnp.bfloat16), 1, 2)
    left_pair = lax.all_gather(left_side, "branch", axis=0, tiled=True)
    left_gathered = lax.all_to_all(left_pair, "rows", split_axis=1, concat_axis=0, tiled=True)
    right_pair = lax.all_to_all(right_side, "branch", split_axis=2, concat_axis=0, tiled=True)
    right_gathered = lax.all_gather(right_pair, "rows", axis=0, tiled=True)
    return (refreshed_homolog_features, left_gathered, right_gathered)


def send_whole(tri_left, tri_right):
    return (
        lax.all_to_all(
            lax.all_to_all(tri_left, "branch", split_axis=0, concat_axis=2, tiled=True),
            "rows",
            split_axis=0,
            concat_axis=1,
            tiled=True,
        ),
        lax.all_to_all(
            lax.all_to_all(tri_right, "branch", split_axis=0, concat_axis=2, tiled=True),
            "rows",
            split_axis=0,
            concat_axis=1,
            tiled=True,
        ),
    )


def send_back(product):
    return lax.all_to_all(
        lax.all_to_all(product, "rows", split_axis=1, concat_axis=0, tiled=True),
        "branch",
        split_axis=2,
        concat_axis=0,
        tiled=True,
    )


def pair_branch(
    pairwise_input,
    triangle_projection_weight,
    triangle_output_weight,
    pairwise_up_weight,
    pairwise_down_weight,
):
    tile_rows, columns, chans = pairwise_input.shape
    pair_float = pairwise_input.astype(jnp.float32)
    pair_norm = standardize_features(pair_float, -1).astype(jnp.bfloat16)
    norm_flat = pair_norm.reshape(tile_rows * columns, chans)
    proj_flat = lax.dot_general(
        triangle_projection_weight,
        norm_flat,
        (((0,), (1,)), ((), ())),
        preferred_element_type=jnp.float32,
    )
    proj_tile = proj_flat[: 4 * chans].reshape(4 * chans, tile_rows, columns)
    gate_vals = jax.nn.sigmoid(proj_flat[4 * chans :])
    tri_left = (jax.nn.sigmoid(proj_tile[chans : 2 * chans]) * proj_tile[:chans]).astype(
        jnp.bfloat16
    )
    tri_right = (jax.nn.sigmoid(proj_tile[3 * chans :]) * proj_tile[2 * chans : 3 * chans]).astype(
        jnp.bfloat16
    )
    left_chan, right_chan = send_whole(tri_left, tri_right)
    product = jnp.einsum(
        "cik,cjk->cij", left_chan, right_chan, preferred_element_type=jnp.float32
    ).astype(jnp.bfloat16)
    product_tile = send_back(product)
    prod_norm = (
        standardize_features(product_tile.astype(jnp.float32), 0)
        .astype(jnp.bfloat16)
        .reshape(chans, tile_rows * columns)
    )
    tri_update = lax.dot_general(
        triangle_output_weight,
        prod_norm,
        (((0,), (0,)), ((), ())),
        preferred_element_type=jnp.float32,
    )
    gated_update = jnp.transpose(gate_vals * tri_update).reshape(tile_rows, columns, chans)
    pair_mid = pair_float + gated_update
    mid_norm = standardize_features(pair_mid, -1).astype(jnp.bfloat16)
    pair_hidden = jax.nn.relu(
        jnp.einsum("ijd,dh->ijh", mid_norm, pairwise_up_weight, preferred_element_type=jnp.float32)
    ).astype(jnp.bfloat16)
    return pair_mid + jnp.einsum(
        "ijh,hd->ijd", pair_hidden, pairwise_down_weight, preferred_element_type=jnp.float32
    )


def outer_product(left_gathered, right_gathered, outer_output_weight):
    total_rows, tile_rows, channels = left_gathered.shape
    columns = right_gathered.shape[2]
    span_cols = 128
    left_flat = left_gathered.reshape(total_rows, tile_rows * channels)
    pieces = []
    for offset in range(0, columns, span_cols):
        right_piece = right_gathered[:, :, offset : offset + span_cols].reshape(
            total_rows, channels * span_cols
        )
        outer_vals = lax.dot_general(
            left_flat, right_piece, (((0,), (0,)), ((), ())), preferred_element_type=jnp.float32
        )
        outer_vals = (
            (outer_vals / total_rows)
            .astype(jnp.bfloat16)
            .reshape(tile_rows, channels * channels, span_cols)
        )
        pieces.append(
            lax.dot_general(
                outer_output_weight,
                outer_vals,
                (((0,), (1,)), ((), ())),
                preferred_element_type=jnp.float32,
            )
        )
    outer_eij = jnp.concatenate(pieces, axis=2)
    return jnp.transpose(outer_eij, (1, 2, 0))


def general_device(
    homolog_features,
    pairwise_input,
    transition_expand_matrix,
    transition_contract_matrix,
    factor_pair_matrices,
    outer_output_weight,
    triangle_projection_weight,
    triangle_output_weight,
    pairwise_up_weight,
    pairwise_down_weight,
):
    refreshed_homolog_features, left_gathered, right_gathered = alignment_branch(
        homolog_features, transition_expand_matrix, transition_contract_matrix, factor_pair_matrices
    )
    pair_mid = pair_branch(
        pairwise_input,
        triangle_projection_weight,
        triangle_output_weight,
        pairwise_up_weight,
        pairwise_down_weight,
    )
    outer_update = outer_product(left_gathered, right_gathered, outer_output_weight)
    pairwise_output = (pair_mid + outer_update).astype(jnp.bfloat16)
    return (refreshed_homolog_features, pairwise_output)


def normed(values, axis):
    average = jnp.mean(values, axis=axis, keepdims=True)
    centered = values - average
    variance = jnp.mean(centered * centered, axis=axis, keepdims=True)
    return (centered * lax.rsqrt(variance + 1e-05)).astype(BF16)


def sigmoid(values):
    return 0.5 * jnp.tanh(0.5 * values) + 0.5


def dot(a, b, dims=(((1,), (0,)), ((), ()))):
    return lax.dot_general(a, b, dims, preferred_element_type=F32)


def cost(flops, nbytes, transcendentals=0):
    return pl.CostEstimate(flops=flops, bytes_accessed=nbytes, transcendentals=transcendentals)


def channel_order(w, sides, source, count):
    chans = w.shape[0]
    col = lax.broadcasted_iota(jnp.int32, (count, chans), 1)
    order = jnp.where(col == source, 1.0, 0.0).astype(BF16)
    return [dot(order, w[:, s * chans : (s + 1) * chans], NT).astype(BF16) for s in sides]


def gated_rows(values, gates, rows_ref, store):
    rows, width, chans = rows_ref.shape
    for i in range(0, rows, 2):
        tokens = rows_ref[i : i + 2].reshape(2 * width, chans)
        result = dot(values, tokens, NT) * sigmoid(dot(gates, tokens, NT))
        store(i, result[:, :width])
        store(i + 1, result[:, width:])


def right_kernel(
    n_branch, x_hbm, w_hbm, sent_hbm, tokens_hbm, x_ref, w_ref, sent_ref, tokens_ref, scr, sems
):
    rows, width, chans = x_ref.shape
    groups, per = sent_ref.shape[:2]
    near = groups // n_branch
    halves = sent_hbm.shape[0] // groups
    columns = w_hbm.at[:, pl.ds(2 * chans, 2 * chans)]
    copies = [
        pltpu.make_async_copy(columns, w_ref, sems.at[0]),
        pltpu.make_async_copy(x_hbm, x_ref, sems.at[1]),
    ]
    for copy in copies:
        copy.start()
    for copy in copies:
        copy.wait()
    values = jnp.transpose(w_ref[:, :chans])
    gates = jnp.transpose(w_ref[:, chans:])
    step = 4
    parts = []
    for i in range(0, rows, step):
        tokens = normed(x_ref[i : i + step].astype(F32), -1)
        tokens_ref[i : i + step] = tokens
        parts.append(tokens.reshape(step * width, chans))
    outs = [pltpu.make_async_copy(tokens_ref, tokens_hbm, sems.at[2])]
    outs[0].start()
    for i, tokens in zip(range(0, rows, step), parts):
        result = dot(values, tokens, NT) * sigmoid(dot(gates, tokens, NT))
        for k in range(step):
            scr[pl.ds(i + k, chans, stride=rows), :] = result[:, k * width : (k + 1) * width]
    span = 4
    for g in range(groups):
        for c in range(per):
            q = (g * per + c) * rows
            sent_ref[g, c] = scr[q : q + rows, :].astype(BF16)
        if g % span == span - 1:
            begin = g + 1 - span
            for h in range(halves):
                to = (begin // near * halves + h) * near + begin % near
                copy = pltpu.make_async_copy(
                    sent_ref.at[pl.ds(begin, span)],
                    sent_hbm.at[pl.ds(to, span)],
                    sems.at[2 + len(outs)],
                )
                copy.start()
                outs.append(copy)
    for copy in outs:
        copy.wait()


def right_operand(x, w, n_branch, devices, per):
    rows, width, chans = x.shape
    groups = chans // per
    return pl.pallas_call(
        functools.partial(right_kernel, n_branch),
        out_shape=[
            jax.ShapeDtypeStruct((devices, per, rows, width), BF16),
            jax.ShapeDtypeStruct(x.shape, BF16),
        ],
        in_specs=[HBM] * 2,
        out_specs=[HBM] * 2,
        scratch_shapes=[
            pltpu.VMEM(x.shape, BF16),
            pltpu.VMEM((chans, 2 * chans), BF16),
            pltpu.VMEM((groups, per, rows, width), BF16),
            pltpu.VMEM(x.shape, BF16),
            pltpu.VMEM(((chans + 1) * rows, width), F32),
            pltpu.SemaphoreType.DMA((3 + devices // 4,)),
        ],
        cost_estimate=cost(2 * rows * width * chans * 2 * chans, 3 * rows * width * chans * 2),
        name="right_operand",
    )(x, w)


def left_kernel(n_branch, near, where_ref, x_ref, other_ref, w_ref, out_ref, scr, norm_scr):
    rows, _, chans = x_ref.shape
    branch, row_at = where_ref[0], where_ref[1]
    core = lax.bitwise_and(row_at, 1)
    place = lax.shift_right_logical(lax.bitwise_and(row_at, near - 1), 1)
    count = out_ref.shape[0]
    places = count // n_branch
    per = chans // (n_branch * near)

    total = count * per
    q = lax.broadcasted_iota(jnp.int32, (total, chans), 0)
    t = q // per
    group = lax.bitwise_xor(t // places, branch) * near + (
        lax.bitwise_xor(t % places, place) * 2 + core
    )
    values, gates = channel_order(w_ref[...], (0, 1), group * per + q % per, total)

    def store_at(at):
        def store(i, block):
            scr[at, pl.ds(i, total, stride=rows), :] = block

        return store

    gated_rows(values, gates, x_ref, store_at(core))
    for i in range(0, rows, 4):
        norm_scr[i : i + 4] = normed(other_ref[i : i + 4].astype(F32), -1)
    gated_rows(values, gates, norm_scr, store_at(1 - core))
    for t in range(count):
        for c in range(per):
            for k in range(2):
                start = (t * per + c) * rows
                out_ref[t, pl.ds((c * 2 + k) * rows, rows)] = scr[
                    k, start : start + rows, :
                ].astype(BF16)


def left_operand(where, x, other, w, n_branch, near):
    rows, width, chans = x.shape
    count = n_branch * near // 2
    per = chans // (n_branch * near)
    return pl.pallas_call(
        functools.partial(left_kernel, n_branch, near),
        out_shape=jax.ShapeDtypeStruct((count, per * 2 * rows, width), BF16),
        in_specs=[SMEM] + [VMEM] * 3,
        out_specs=VMEM,
        scratch_shapes=[
            pltpu.VMEM((2, (count * per + 1) * rows, width), F32),
            pltpu.VMEM(x.shape, BF16),
        ],
        compiler_params=PARAMS,
        cost_estimate=cost(4 * x.size * 2 * chans, x.size * 8),
        name="left_operand",
    )(where, x, other, w)


def message_kernel(
    n_branch, near, rows, where_ref, left_ref, seq_ref, far_ref, up_ref, down_ref, factor_ref,
    fresh_ref, *rest
):
    out_refs, (right_scr, left_scr) = rest[:-2], rest[-2:]
    count, size, width = left_ref.shape
    for t, out_ref in zip(TARGETS, out_refs):
        out_ref[:size] = left_ref[t]
    x = [ref[0].astype(F32) for ref in (seq_ref, far_ref)]
    tokens = [normed(v, -1) for v in x]
    hidden = [jnp.maximum(dot(t, up_ref[...]).astype(BF16), 0.0) for t in tokens]
    fresh = [(v + dot(h, down_ref[...])).astype(BF16) for v, h in zip(x, hidden)]
    fresh_ref[0] = fresh[0]
    factor = factor_ref[...]
    depth = factor.shape[0] // 2
    tokens = [normed(v.astype(F32), -1) for v in fresh]
    for k, row in enumerate(tokens):
        right = dot(factor[depth:], row, NT).astype(BF16)
        for b in range(n_branch):
            right_scr[b, k * depth : (k + 1) * depth] = right[:, b * width : (b + 1) * width]
    tiles = [dot(row, factor[:depth], NT).astype(BF16).reshape(-1, 2, rows, depth) for row in tokens]
    for t in range(left_scr.shape[0]):
        left_scr[t] = jnp.concatenate([tile[t, c] for tile in tiles for c in range(2)], axis=1)
    branch, row_at = where_ref[0], where_ref[1]
    place = lax.shift_right_logical(lax.bitwise_and(row_at, near - 1), 1)
    places = count // n_branch
    first = row_at // near * places
    for t, out_ref in zip(TARGETS, out_refs):
        out_ref[size : size + 2 * depth] = right_scr[lax.bitwise_xor(branch, t // places)]
        out_ref[size + 2 * depth :] = left_scr[first + lax.bitwise_xor(place, t % places)]


def messages(where, left, seq, far, up, down, factor, rows, n_branch, near):
    _, length, feats = seq.shape
    depth = factor.shape[0] // 2
    count, size, width = left.shape
    piece = jax.ShapeDtypeStruct((size + 2 * depth + rows, width), BF16)
    fresh, *pieces = pl.pallas_call(
        functools.partial(message_kernel, n_branch, near, rows),
        out_shape=[jax.ShapeDtypeStruct(seq.shape, BF16)] + [piece] * count,
        in_specs=[SMEM] + [VMEM] * 6,
        out_specs=[VMEM] * (1 + count),
        scratch_shapes=[
            pltpu.VMEM((n_branch, 2 * depth, width), BF16),
            pltpu.VMEM((length // rows // 2, rows, width), BF16),
        ],
        compiler_params=PARAMS,
        cost_estimate=cost(2 * 10**10, 4 * feats * up.shape[1]),
        name="msa_transition_and_messages",
    )(where, left, seq, far, up, down, factor)
    return fresh, pieces


def gate_kernel(x_ref, w_ref, out_ref):
    rows, width, chans = x_ref.shape
    tokens = x_ref[...].reshape(rows * width, chans)
    out_ref[...] = sigmoid(dot(tokens, w_ref[:, 4 * chans :])).reshape(rows, width, chans)


def output_gate(x, w):
    rows, width, chans = x.shape
    step = 4
    spec = pl.BlockSpec((step, width, chans), lambda i: (i, 0, 0))
    return pl.pallas_call(
        gate_kernel,
        grid=(rows // step,),
        out_shape=jax.ShapeDtypeStruct(x.shape, F32),
        in_specs=[spec, pl.BlockSpec(w.shape, lambda i: (0, 0))],
        out_specs=spec,
        compiler_params=PARAMS,
        cost_estimate=cost(2 * rows * width * chans * chans, rows * width * chans * 6),
        name="triangle_output_gate",
    )(x, w)


def product_kernel(n_branch, near, where_ref, in_ref, *rest):
    places = near // 2
    left_refs = dict(zip(TARGETS, rest))
    out_hbm, out_ref, sems = rest[n_branch * places :]
    devices, per, rows, width = in_ref.shape
    n_rows = devices // n_branch
    branch, row_at = where_ref[0], where_ref[1]
    place = lax.shift_right_logical(lax.bitwise_and(row_at, near - 1), 1)
    outs = []
    for c in range(per):
        span = slice(c * 2 * rows, (c + 1) * 2 * rows)
        left = jnp.concatenate(
            [
                jnp.concatenate([left_refs[s * places + p][span] for p in range(places)], axis=0)
                for s in range(n_branch)
            ],
            axis=1,
        )
        right = jnp.concatenate(
            [
                in_ref[pl.ds(lax.bitwise_xor(branch, s) * n_rows, n_rows), c].reshape(
                    n_rows * rows, width
                )
                for s in range(n_branch)
            ],
            axis=1,
        )
        product = dot(left, right, NT).astype(BF16)
        for p in range(places):
            at = lax.bitwise_xor(place, p) * 2
            part = product[p * 2 * rows : (p + 1) * 2 * rows]
            for b in range(n_branch):
                for k in range(2):
                    out_ref[n_branch * near - 1 - (b * near + at + k), c] = part[
                        k * rows : (k + 1) * rows, b * width : (b + 1) * width
                    ]
        if c % 2 == 1:
            half = pl.ds(c - 1, 2)
            copy = pltpu.make_async_copy(
                out_ref.at[:, half], out_hbm.at[:, half], sems.at[c // 2]
            )
            copy.start()
            outs.append(copy)
    for copy in outs:
        copy.wait()


def triangle_product(where, received, pieces, n_branch, near):
    devices, per, rows, width = received.shape
    shape = (n_branch * near, per, rows, width)
    return pl.pallas_call(
        functools.partial(product_kernel, n_branch, near),
        out_shape=jax.ShapeDtypeStruct(shape, BF16),
        in_specs=[SMEM] + [VMEM] * (1 + len(pieces)),
        out_specs=HBM,
        scratch_shapes=[pltpu.VMEM(shape, BF16), pltpu.SemaphoreType.DMA((per // 2,))],
        compiler_params=PARAMS,
        cost_estimate=cost(2 * near * rows * received.size, received.size * 4),
        name="triangle_product",
    )(where, received, *pieces)


def pair_output_kernel(
    p_ref, x_ref, gate_ref, outer_ref, w_ref, up_ref, down_ref, out_hbm, scr, out_ref, sems
):
    devices, per, rows, width = p_ref.shape
    chans = devices * per
    step = rows // 2
    shape = (step * width, chans)
    share = up_ref.shape[1] // 4

    for g in range(devices):
        for c in range(per):
            k = (g * per + c) * rows
            scr[k : k + rows, :] = p_ref[devices - 1 - g, c].astype(F32)

    def triangle(i):
        parts = [
            normed(scr[pl.ds(i + k, chans, stride=rows), :], 0) for k in range(step)
        ]
        update = dot(jnp.concatenate(parts, axis=1), w_ref[...], TN)
        x = x_ref[i : i + step].astype(F32).reshape(shape)
        middle = x + gate_ref[i : i + step].reshape(shape) * update
        return middle, normed(middle, -1)

    def transition(i, middle, tokens):
        result = middle + outer_ref[i : i + step].reshape(shape)
        for h in range(0, up_ref.shape[1], share):
            hidden = dot(tokens, up_ref[:, h : h + share]).astype(BF16)
            result = result + dot(jnp.maximum(hidden, 0.0), down_ref[h : h + share])
        out_ref[i : i + step] = result.astype(BF16).reshape(step, width, chans)
        part = pl.ds(i, step)
        copy = pltpu.make_async_copy(out_ref.at[part], out_hbm.at[part], sems.at[i // step])
        copy.start()
        return copy

    middles = [triangle(i) for i in range(0, rows, step)]
    copies = [transition(i * step, *middle) for i, middle in enumerate(middles)]
    for copy in copies:
        copy.wait()


def pair_output(product, x, gate, outer, w, up, down):
    devices, per, rows, width = product.shape
    chans = devices * per
    return pl.pallas_call(
        pair_output_kernel,
        out_shape=jax.ShapeDtypeStruct(x.shape, BF16),
        in_specs=[VMEM] * 7,
        out_specs=HBM,
        scratch_shapes=[
            pltpu.VMEM((rows * (chans + 1), width), F32),
            pltpu.VMEM(x.shape, BF16),
            pltpu.SemaphoreType.DMA((2,)),
        ],
        compiler_params=PARAMS,
        cost_estimate=cost(2 * x.size * (chans + 2 * up.shape[1]), x.size * 14),
        name="pair_output",
    )(product, x, gate, outer, w, up, down)


def outer_kernel(where_ref, *refs):
    groups, (w_ref, out_ref, right_scr, left_scr, w_scr, m_scr) = refs[:-6], refs[-6:]
    rows, width, chans = out_ref.shape
    total = 2 * sum(ref.shape[0] for ref in groups)
    depth = m_scr.shape[1] // total
    s = 0
    for ref in groups:
        for k in range(ref.shape[0]):
            both = ref[k, 2 * depth :].astype(F32)
            for far in range(2):
                at = s + far * (total // 2)
                side = ref[k, far * depth : (far + 1) * depth].astype(F32)
                right_scr[pl.ds(at, depth, stride=total), :] = side
                left_scr[pl.ds(at, rows, stride=total), :] = both
            s += 1
    right = jnp.transpose(right_scr[: depth * total]).astype(BF16)
    both = left_scr[: rows * total]
    shift = lax.bitwise_and(where_ref[1], 1) * depth
    first = pltpu.roll(both, width - shift, 1)[:, :depth]
    second = pltpu.roll(both, width - 2 * depth - shift, 1)[:, :depth]
    row = lax.broadcasted_iota(jnp.int32, first.shape, 0)
    left = jnp.where(row % total < total // 2, first, second).astype(BF16)
    w_scr[: depth * depth] = w_ref[...].astype(F32)
    for d in range(depth):
        part = w_scr[pl.ds(d, depth, stride=depth), :].astype(BF16)
        m_scr[:, d * total : (d + 1) * total] = (
            dot(left, part).astype(BF16).reshape(rows, total, chans)
        )
    for i in range(0, rows, 2):
        pair = jnp.concatenate([m_scr[i], m_scr[i + 1]], axis=1)
        result = dot(right, pair) / total
        out_ref[i] = result[:, :chans]
        out_ref[i + 1] = result[:, chans:]


def outer_update(where, groups, w, rows, chans):
    total = 2 * sum(group.shape[0] for group in groups)
    width = groups[0].shape[2]
    depth = (groups[0].shape[1] - rows) // 2
    return pl.pallas_call(
        outer_kernel,
        out_shape=jax.ShapeDtypeStruct((rows, width, chans), F32),
        in_specs=[SMEM] + [VMEM] * (len(groups) + 1),
        out_specs=VMEM,
        scratch_shapes=[
            pltpu.VMEM(((depth + 1) * total, width), F32),
            pltpu.VMEM(((rows + 1) * total, width), F32),
            pltpu.VMEM((depth * (depth + 1), chans), F32),
            pltpu.VMEM((rows, depth * total, chans), BF16),
        ],
        compiler_params=PARAMS,
        cost_estimate=cost(2 * rows * width * depth * total * chans * 2, rows * width * chans * 4),
        name="outer_product_mean",
    )(where, *groups, w)


def swap(x, n_branch, n_rows, mask):
    count = n_branch * n_rows
    return lax.ppermute(x, AXES, [(d, d ^ mask) for d in range(count)])


def own_channels_device(
    n_branch,
    n_rows,
    homolog_features,
    pairwise_input,
    transition_expand_matrix,
    transition_contract_matrix,
    factor_pair_matrices,
    outer_output_weight,
    triangle_projection_weight,
    triangle_output_weight,
    pairwise_up_weight,
    pairwise_down_weight,
):
    rows, _, chans = pairwise_input.shape
    near = 8
    halves = n_rows // near
    places = near // 2
    per = chans // (n_branch * near)
    where = jnp.stack([lax.axis_index("branch"), lax.axis_index("rows")]).astype(jnp.int32)

    far_row = swap(homolog_features, n_branch, n_rows, near)
    sent, tokens = right_operand(
        pairwise_input, triangle_projection_weight, n_branch, n_branch * n_rows, per
    )
    received = lax.all_to_all(sent, AXES, 0, 0, tiled=True)

    other = swap(pairwise_input, n_branch, n_rows, 1)
    left = left_operand(where, tokens, other, triangle_projection_weight, n_branch, near)
    fresh, pieces = messages(
        where,
        left,
        homolog_features,
        far_row,
        transition_expand_matrix,
        transition_contract_matrix,
        jnp.transpose(factor_pair_matrices),
        rows,
        n_branch,
        near,
    )
    moved = [
        piece if t == 0 else swap(piece, n_branch, n_rows, t // places * n_rows + t % places * 2)
        for t, piece in zip(TARGETS, pieces)
    ]
    mine = jnp.stack([piece[per * 2 * rows :] for piece in moved])
    groups = [mine, swap(mine, n_branch, n_rows, 1)]
    outer = outer_update(where, groups, outer_output_weight, rows, chans)
    gate_tokens, _ = lax.optimization_barrier((tokens, moved[0]))
    gate = output_gate(gate_tokens, triangle_projection_weight)

    product = triangle_product(where, received, moved, n_branch, near)
    members = [
        [b * n_rows + h * near + k for b in range(n_branch) for k in range(near)][::-1]
        for h in range(halves)
    ]
    returned = lax.all_to_all(product, AXES, 0, 0, axis_index_groups=members, tiled=True)
    pairwise_output = pair_output(
        returned,
        pairwise_input,
        gate,
        outer,
        triangle_output_weight,
        pairwise_up_weight,
        pairwise_down_weight,
    )
    return (fresh, pairwise_output)


def on_device(n_branch, n_rows, homolog_features, pairwise_input, *weights):
    rows, width, chans = pairwise_input.shape
    near = 8
    halves = n_rows // near
    fits = (
        homolog_features.shape[0] == 1
        and halves == 2
        and n_branch == 2
        and n_rows % near == 0
        and chans % (n_branch * near) == 0
        and rows == 16
        and width == 128
        and homolog_features.shape[1] == n_rows * rows == n_branch * width
        and 2 * weights[2].shape[1] == width
    )
    if fits:
        return own_channels_device(n_branch, n_rows, homolog_features, pairwise_input, *weights)
    return general_device(homolog_features, pairwise_input, *weights)


def solution(mesh):
    return jax.shard_map(
        functools.partial(on_device, mesh.shape["branch"], mesh.shape["rows"]),
        mesh=mesh,
        in_specs=(
            P(("branch", "rows"), None, None),
            P("rows", "branch", None),
            P(),
            P(),
            P(),
            P(),
            P(),
            P(),
            P(),
            P(),
        ),
        out_specs=(P(("branch", "rows"), None, None), P("rows", "branch", None)),
        check_vma=False,
    )
```

```python
import functools

import jax
import jax.numpy as jnp
from jax import lax
from jax.experimental import pallas as pl
from jax.experimental.pallas import tpu as pltpu
from jax.sharding import PartitionSpec as P

BF16 = jnp.bfloat16
F32 = jnp.float32
AXES = ("branch", "rows")
NT = (((1,), (1,)), ((), ()))
TN = (((0,), (0,)), ((), ()))
VMEM = pl.BlockSpec(memory_space=pltpu.VMEM)
SMEM = pl.BlockSpec(memory_space=pltpu.SMEM)
TARGETS = (0, 4, 1, 2, 7, 3, 6, 5)
HBM = pl.BlockSpec(memory_space=pltpu.HBM)
PARAMS = pltpu.CompilerParams(vmem_limit_bytes=48 * 1024 * 1024)

def standardize_features(values, dimension):
    average = jnp.mean(values, axis=dimension, keepdims=True)
    centered = values - average
    variance = jnp.mean(centered * centered, axis=dimension, keepdims=True)
    return centered * lax.rsqrt(variance + 1e-05)


def alignment_branch(
    homolog_features, transition_expand_matrix, transition_contract_matrix, factor_pair_matrices
):
    local_rows, sequence_length, channel_width = homolog_features.shape
    homolog_real_matrix = homolog_features.astype(jnp.float32)
    standardized_homologs = (
        standardize_features(homolog_real_matrix, -1)
        .astype(jnp.bfloat16)
        .reshape(local_rows * sequence_length, channel_width)
    )
    expanded_activations = jax.nn.relu(
        jnp.dot(standardized_homologs, transition_expand_matrix, preferred_element_type=jnp.float32)
    ).astype(jnp.bfloat16)
    refreshed_homolog_features = (
        homolog_real_matrix
        + jnp.dot(
            expanded_activations, transition_contract_matrix, preferred_element_type=jnp.float32
        ).reshape(homolog_features.shape)
    ).astype(jnp.bfloat16)
    standardized_for_factors = (
        standardize_features(refreshed_homolog_features.astype(jnp.float32), -1)
        .astype(jnp.bfloat16)
        .reshape(local_rows * sequence_length, channel_width)
    )
    projected = jnp.dot(
        standardized_for_factors, factor_pair_matrices, preferred_element_type=jnp.float32
    ).reshape(local_rows, sequence_length, -1)
    channels = projected.shape[-1] // 2
    left_side = projected[..., :channels].astype(jnp.bfloat16)
    right_side = jnp.swapaxes(projected[..., channels:].astype(jnp.bfloat16), 1, 2)
    left_pair = lax.all_gather(left_side, "branch", axis=0, tiled=True)
    left_gathered = lax.all_to_all(left_pair, "rows", split_axis=1, concat_axis=0, tiled=True)
    right_pair = lax.all_to_all(right_side, "branch", split_axis=2, concat_axis=0, tiled=True)
    right_gathered = lax.all_gather(right_pair, "rows", axis=0, tiled=True)
    return (refreshed_homolog_features, left_gathered, right_gathered)


def send_whole(tri_left, tri_right):
    return (
        lax.all_to_all(
            lax.all_to_all(tri_left, "branch", split_axis=0, concat_axis=2, tiled=True),
            "rows",
            split_axis=0,
            concat_axis=1,
            tiled=True,
        ),
        lax.all_to_all(
            lax.all_to_all(tri_right, "branch", split_axis=0, concat_axis=2, tiled=True),
            "rows",
            split_axis=0,
            concat_axis=1,
            tiled=True,
        ),
    )


def send_back(product):
    return lax.all_to_all(
        lax.all_to_all(product, "rows", split_axis=1, concat_axis=0, tiled=True),
        "branch",
        split_axis=2,
        concat_axis=0,
        tiled=True,
    )


def pair_branch(
    pairwise_input,
    triangle_projection_weight,
    triangle_output_weight,
    pairwise_up_weight,
    pairwise_down_weight,
):
    tile_rows, columns, chans = pairwise_input.shape
    pair_float = pairwise_input.astype(jnp.float32)
    pair_norm = standardize_features(pair_float, -1).astype(jnp.bfloat16)
    norm_flat = pair_norm.reshape(tile_rows * columns, chans)
    proj_flat = lax.dot_general(
        triangle_projection_weight,
        norm_flat,
        (((0,), (1,)), ((), ())),
        preferred_element_type=jnp.float32,
    )
    proj_tile = proj_flat[: 4 * chans].reshape(4 * chans, tile_rows, columns)
    gate_vals = jax.nn.sigmoid(proj_flat[4 * chans :])
    tri_left = (jax.nn.sigmoid(proj_tile[chans : 2 * chans]) * proj_tile[:chans]).astype(
        jnp.bfloat16
    )
    tri_right = (jax.nn.sigmoid(proj_tile[3 * chans :]) * proj_tile[2 * chans : 3 * chans]).astype(
        jnp.bfloat16
    )
    left_chan, right_chan = send_whole(tri_left, tri_right)
    product = jnp.einsum(
        "cik,cjk->cij", left_chan, right_chan, preferred_element_type=jnp.float32
    ).astype(jnp.bfloat16)
    product_tile = send_back(product)
    prod_norm = (
        standardize_features(product_tile.astype(jnp.float32), 0)
        .astype(jnp.bfloat16)
        .reshape(chans, tile_rows * columns)
    )
    tri_update = lax.dot_general(
        triangle_output_weight,
        prod_norm,
        (((0,), (0,)), ((), ())),
        preferred_element_type=jnp.float32,
    )
    gated_update = jnp.transpose(gate_vals * tri_update).reshape(tile_rows, columns, chans)
    pair_mid = pair_float + gated_update
    mid_norm = standardize_features(pair_mid, -1).astype(jnp.bfloat16)
    pair_hidden = jax.nn.relu(
        jnp.einsum("ijd,dh->ijh", mid_norm, pairwise_up_weight, preferred_element_type=jnp.float32)
    ).astype(jnp.bfloat16)
    return pair_mid + jnp.einsum(
        "ijh,hd->ijd", pair_hidden, pairwise_down_weight, preferred_element_type=jnp.float32
    )


def outer_product(left_gathered, right_gathered, outer_output_weight):
    total_rows, tile_rows, channels = left_gathered.shape
    columns = right_gathered.shape[2]
    span_cols = 128
    left_flat = left_gathered.reshape(total_rows, tile_rows * channels)
    pieces = []
    for offset in range(0, columns, span_cols):
        right_piece = right_gathered[:, :, offset : offset + span_cols].reshape(
            total_rows, channels * span_cols
        )
        outer_vals = lax.dot_general(
            left_flat, right_piece, (((0,), (0,)), ((), ())), preferred_element_type=jnp.float32
        )
        outer_vals = (
            (outer_vals / total_rows)
            .astype(jnp.bfloat16)
            .reshape(tile_rows, channels * channels, span_cols)
        )
        pieces.append(
            lax.dot_general(
                outer_output_weight,
                outer_vals,
                (((0,), (1,)), ((), ())),
                preferred_element_type=jnp.float32,
            )
        )
    outer_eij = jnp.concatenate(pieces, axis=2)
    return jnp.transpose(outer_eij, (1, 2, 0))


def general_device(
    homolog_features,
    pairwise_input,
    transition_expand_matrix,
    transition_contract_matrix,
    factor_pair_matrices,
    outer_output_weight,
    triangle_projection_weight,
    triangle_output_weight,
    pairwise_up_weight,
    pairwise_down_weight,
):
    refreshed_homolog_features, left_gathered, right_gathered = alignment_branch(
        homolog_features, transition_expand_matrix, transition_contract_matrix, factor_pair_matrices
    )
    pair_mid = pair_branch(
        pairwise_input,
        triangle_projection_weight,
        triangle_output_weight,
        pairwise_up_weight,
        pairwise_down_weight,
    )
    outer_update = outer_product(left_gathered, right_gathered, outer_output_weight)
    pairwise_output = (pair_mid + outer_update).astype(jnp.bfloat16)
    return (refreshed_homolog_features, pairwise_output)


def normed(values, axis):
    average = jnp.mean(values, axis=axis, keepdims=True)
    centered = values - average
    variance = jnp.mean(centered * centered, axis=axis, keepdims=True)
    return (centered * lax.rsqrt(variance + 1e-05)).astype(BF16)


def sigmoid(values):
    return 0.5 * jnp.tanh(0.5 * values) + 0.5


def dot(a, b, dims=(((1,), (0,)), ((), ()))):
    return lax.dot_general(a, b, dims, preferred_element_type=F32)


def cost(flops, nbytes, transcendentals=0):
    return pl.CostEstimate(flops=flops, bytes_accessed=nbytes, transcendentals=transcendentals)


def channel_order(w, sides, source, count):
    chans = w.shape[0]
    col = lax.broadcasted_iota(jnp.int32, (count, chans), 1)
    order = jnp.where(col == source, 1.0, 0.0).astype(BF16)
    return [dot(order, w[:, s * chans : (s + 1) * chans], NT).astype(BF16) for s in sides]


def gated_rows(values, gates, rows_ref, store):
    rows, width, chans = rows_ref.shape
    for i in range(0, rows, 2):
        tokens = rows_ref[i : i + 2].reshape(2 * width, chans)
        result = dot(values, tokens, NT) * sigmoid(dot(gates, tokens, NT))
        store(i, result[:, :width])
        store(i + 1, result[:, width:])


def right_kernel(
    n_branch, x_hbm, w_hbm, sent_hbm, x_ref, w_ref, sent_ref, scr, sems
):
    rows, width, chans = x_ref.shape
    groups, per = sent_ref.shape[:2]
    near = groups // n_branch
    halves = sent_hbm.shape[0] // groups
    columns = w_hbm.at[:, pl.ds(2 * chans, 2 * chans)]
    copies = [
        pltpu.make_async_copy(columns, w_ref, sems.at[0]),
        pltpu.make_async_copy(x_hbm, x_ref, sems.at[1]),
    ]
    for copy in copies:
        copy.start()
    for copy in copies:
        copy.wait()
    values = jnp.transpose(w_ref[:, :chans])
    gates = jnp.transpose(w_ref[:, chans:])
    step = 4
    parts = []
    for i in range(0, rows, step):
        tokens = normed(x_ref[i : i + step].astype(F32), -1)
        parts.append(tokens.reshape(step * width, chans))
    outs = []
    for i, tokens in zip(range(0, rows, step), parts):
        result = dot(values, tokens, NT) * sigmoid(dot(gates, tokens, NT))
        for k in range(step):
            scr[pl.ds(i + k, chans, stride=rows), :] = result[:, k * width : (k + 1) * width]
    span = 4
    for g in range(groups):
        for c in range(per):
            q = (g * per + c) * rows
            sent_ref[g, c] = scr[q : q + rows, :].astype(BF16)
        if g % span == span - 1:
            begin = g + 1 - span
            for h in range(halves):
                to = (begin // near * halves + h) * near + begin % near
                copy = pltpu.make_async_copy(
                    sent_ref.at[pl.ds(begin, span)],
                    sent_hbm.at[pl.ds(to, span)],
                    sems.at[2 + len(outs)],
                )
                copy.start()
                outs.append(copy)
    for copy in outs:
        copy.wait()


def right_operand(x, w, n_branch, devices, per):
    rows, width, chans = x.shape
    groups = chans // per
    return pl.pallas_call(
        functools.partial(right_kernel, n_branch),
        out_shape=jax.ShapeDtypeStruct((devices, per, rows, width), BF16),
        in_specs=[HBM] * 2,
        out_specs=HBM,
        scratch_shapes=[
            pltpu.VMEM(x.shape, BF16),
            pltpu.VMEM((chans, 2 * chans), BF16),
            pltpu.VMEM((groups, per, rows, width), BF16),
            pltpu.VMEM(((chans + 1) * rows, width), F32),
            pltpu.SemaphoreType.DMA((3 + devices // 4,)),
        ],
        cost_estimate=cost(2 * rows * width * chans * 2 * chans, 3 * rows * width * chans * 2),
        name="right_operand",
    )(x, w)


def left_kernel(n_branch, near, where_ref, x_ref, other_ref, w_ref, out_ref, scr, norm_scr):
    rows, _, chans = x_ref.shape
    branch, row_at = where_ref[0], where_ref[1]
    core = lax.bitwise_and(row_at, 1)
    place = lax.shift_right_logical(lax.bitwise_and(row_at, near - 1), 1)
    count = out_ref.shape[0]
    places = count // n_branch
    per = chans // (n_branch * near)

    total = count * per
    q = lax.broadcasted_iota(jnp.int32, (total, chans), 0)
    t = q // per
    group = lax.bitwise_xor(t // places, branch) * near + (
        lax.bitwise_xor(t % places, place) * 2 + core
    )
    values, gates = channel_order(w_ref[...], (0, 1), group * per + q % per, total)

    def store_at(at):
        def store(i, block):
            scr[at, pl.ds(i, total, stride=rows), :] = block

        return store

    for k, ref, at in ((0, x_ref, core), (1, other_ref, 1 - core)):
        for i in range(0, rows, 4):
            norm_scr[k, i : i + 4] = normed(ref[i : i + 4].astype(F32), -1)
        gated_rows(values, gates, norm_scr.at[k], store_at(at))
    for t in range(count):
        for c in range(per):
            for k in range(2):
                start = (t * per + c) * rows
                out_ref[t, pl.ds((c * 2 + k) * rows, rows)] = scr[
                    k, start : start + rows, :
                ].astype(BF16)


def left_operand(where, x, other, w, n_branch, near):
    rows, width, chans = x.shape
    count = n_branch * near // 2
    per = chans // (n_branch * near)
    return pl.pallas_call(
        functools.partial(left_kernel, n_branch, near),
        out_shape=jax.ShapeDtypeStruct((count, per * 2 * rows, width), BF16),
        in_specs=[SMEM] + [VMEM] * 3,
        out_specs=VMEM,
        scratch_shapes=[
            pltpu.VMEM((2, (count * per + 1) * rows, width), F32),
            pltpu.VMEM((2,) + x.shape, BF16),
        ],
        compiler_params=PARAMS,
        cost_estimate=cost(4 * x.size * 2 * chans, x.size * 8),
        name="left_operand",
    )(where, x, other, w)


def message_kernel(
    n_branch, near, rows, where_ref, left_ref, seq_ref, far_ref, up_ref, down_ref, factor_ref,
    fresh_ref, *rest
):
    out_refs, (right_scr, left_scr) = rest[:-2], rest[-2:]
    count, size, width = left_ref.shape
    for t, out_ref in zip(TARGETS, out_refs):
        out_ref[:size] = left_ref[t]
    x = [ref[0].astype(F32) for ref in (seq_ref, far_ref)]
    tokens = [normed(v, -1) for v in x]
    hidden = [jnp.maximum(dot(t, up_ref[...]).astype(BF16), 0.0) for t in tokens]
    fresh = [(v + dot(h, down_ref[...])).astype(BF16) for v, h in zip(x, hidden)]
    fresh_ref[0] = fresh[0]
    factor = factor_ref[...]
    depth = factor.shape[0] // 2
    tokens = [normed(v.astype(F32), -1) for v in fresh]
    for k, row in enumerate(tokens):
        right = dot(factor[depth:], row, NT).astype(BF16)
        for b in range(n_branch):
            right_scr[b, k * depth : (k + 1) * depth] = right[:, b * width : (b + 1) * width]
    tiles = [dot(row, factor[:depth], NT).astype(BF16).reshape(-1, 2, rows, depth) for row in tokens]
    for t in range(left_scr.shape[0]):
        left_scr[t] = jnp.concatenate([tile[t, c] for tile in tiles for c in range(2)], axis=1)
    branch, row_at = where_ref[0], where_ref[1]
    place = lax.shift_right_logical(lax.bitwise_and(row_at, near - 1), 1)
    places = count // n_branch
    first = row_at // near * places
    for t, out_ref in zip(TARGETS, out_refs):
        out_ref[size : size + 2 * depth] = right_scr[lax.bitwise_xor(branch, t // places)]
        out_ref[size + 2 * depth :] = left_scr[first + lax.bitwise_xor(place, t % places)]


def messages(where, left, seq, far, up, down, factor, rows, n_branch, near):
    _, length, feats = seq.shape
    depth = factor.shape[0] // 2
    count, size, width = left.shape
    piece = jax.ShapeDtypeStruct((size + 2 * depth + rows, width), BF16)
    fresh, *pieces = pl.pallas_call(
        functools.partial(message_kernel, n_branch, near, rows),
        out_shape=[jax.ShapeDtypeStruct(seq.shape, BF16)] + [piece] * count,
        in_specs=[SMEM] + [VMEM] * 6,
        out_specs=[VMEM] * (1 + count),
        scratch_shapes=[
            pltpu.VMEM((n_branch, 2 * depth, width), BF16),
            pltpu.VMEM((length // rows // 2, rows, width), BF16),
        ],
        compiler_params=PARAMS,
        cost_estimate=cost(2 * 10**10, 4 * feats * up.shape[1]),
        name="msa_transition_and_messages",
    )(where, left, seq, far, up, down, factor)
    return fresh, pieces


def gate_kernel(x_ref, w_ref, out_ref):
    rows, width, chans = x_ref.shape
    tokens = normed(x_ref[...].astype(F32).reshape(rows * width, chans), -1)
    out_ref[...] = sigmoid(dot(tokens, w_ref[:, 4 * chans :])).reshape(rows, width, chans)


def output_gate(x, w):
    rows, width, chans = x.shape
    step = 4
    spec = pl.BlockSpec((step, width, chans), lambda i: (i, 0, 0))
    return pl.pallas_call(
        gate_kernel,
        grid=(rows // step,),
        out_shape=jax.ShapeDtypeStruct(x.shape, F32),
        in_specs=[spec, pl.BlockSpec(w.shape, lambda i: (0, 0))],
        out_specs=spec,
        compiler_params=PARAMS,
        cost_estimate=cost(2 * rows * width * chans * chans, rows * width * chans * 6),
        name="triangle_output_gate",
    )(x, w)


def product_kernel(n_branch, near, where_ref, in_ref, *rest):
    places = near // 2
    left_refs = dict(zip(TARGETS, rest))
    out_hbm, out_ref, sems = rest[n_branch * places :]
    devices, per, rows, width = in_ref.shape
    n_rows = devices // n_branch
    branch, row_at = where_ref[0], where_ref[1]
    place = lax.shift_right_logical(lax.bitwise_and(row_at, near - 1), 1)
    outs = []
    for c in range(per):
        span = slice(c * 2 * rows, (c + 1) * 2 * rows)
        left = jnp.concatenate(
            [
                jnp.concatenate([left_refs[s * places + p][span] for p in range(places)], axis=0)
                for s in range(n_branch)
            ],
            axis=1,
        )
        right = jnp.concatenate(
            [
                in_ref[pl.ds(lax.bitwise_xor(branch, s) * n_rows, n_rows), c].reshape(
                    n_rows * rows, width
                )
                for s in range(n_branch)
            ],
            axis=1,
        )
        product = dot(left, right, NT).astype(BF16)
        for p in range(places):
            at = lax.bitwise_xor(place, p) * 2
            part = product[p * 2 * rows : (p + 1) * 2 * rows]
            for b in range(n_branch):
                for k in range(2):
                    out_ref[n_branch * near - 1 - (b * near + at + k), c] = part[
                        k * rows : (k + 1) * rows, b * width : (b + 1) * width
                    ]
        if c % 2 == 1:
            half = pl.ds(c - 1, 2)
            copy = pltpu.make_async_copy(
                out_ref.at[:, half], out_hbm.at[:, half], sems.at[c // 2]
            )
            copy.start()
            outs.append(copy)
    for copy in outs:
        copy.wait()


def triangle_product(where, received, pieces, n_branch, near):
    devices, per, rows, width = received.shape
    shape = (n_branch * near, per, rows, width)
    return pl.pallas_call(
        functools.partial(product_kernel, n_branch, near),
        out_shape=jax.ShapeDtypeStruct(shape, BF16),
        in_specs=[SMEM] + [VMEM] * (1 + len(pieces)),
        out_specs=HBM,
        scratch_shapes=[pltpu.VMEM(shape, BF16), pltpu.SemaphoreType.DMA((per // 2,))],
        compiler_params=PARAMS,
        cost_estimate=cost(2 * near * rows * received.size, received.size * 4),
        name="triangle_product",
    )(where, received, *pieces)


def pair_output_kernel(
    p_ref, x_ref, gate_ref, outer_ref, w_ref, up_ref, down_ref, out_hbm, scr, out_ref, sems
):
    devices, per, rows, width = p_ref.shape
    chans = devices * per
    step = rows // 2
    shape = (step * width, chans)
    share = up_ref.shape[1] // 4

    for g in range(devices):
        for c in range(per):
            k = (g * per + c) * rows
            scr[k : k + rows, :] = p_ref[devices - 1 - g, c].astype(F32)

    def triangle(i):
        parts = [
            normed(scr[pl.ds(i + k, chans, stride=rows), :], 0) for k in range(step)
        ]
        update = dot(jnp.concatenate(parts, axis=1), w_ref[...], TN)
        x = x_ref[i : i + step].astype(F32).reshape(shape)
        middle = x + gate_ref[i : i + step].reshape(shape) * update
        return middle, normed(middle, -1)

    def transition(i, middle, tokens):
        result = middle + outer_ref[i : i + step].reshape(shape)
        for h in range(0, up_ref.shape[1], share):
            hidden = dot(tokens, up_ref[:, h : h + share]).astype(BF16)
            result = result + dot(jnp.maximum(hidden, 0.0), down_ref[h : h + share])
        out_ref[i : i + step] = result.astype(BF16).reshape(step, width, chans)
        part = pl.ds(i, step)
        copy = pltpu.make_async_copy(out_ref.at[part], out_hbm.at[part], sems.at[i // step])
        copy.start()
        return copy

    middles = [triangle(i) for i in range(0, rows, step)]
    copies = [transition(i * step, *middle) for i, middle in enumerate(middles)]
    for copy in copies:
        copy.wait()


def pair_output(product, x, gate, outer, w, up, down):
    devices, per, rows, width = product.shape
    chans = devices * per
    return pl.pallas_call(
        pair_output_kernel,
        out_shape=jax.ShapeDtypeStruct(x.shape, BF16),
        in_specs=[VMEM] * 7,
        out_specs=HBM,
        scratch_shapes=[
            pltpu.VMEM((rows * (chans + 1), width), F32),
            pltpu.VMEM(x.shape, BF16),
            pltpu.SemaphoreType.DMA((2,)),
        ],
        compiler_params=PARAMS,
        cost_estimate=cost(2 * x.size * (chans + 2 * up.shape[1]), x.size * 14),
        name="pair_output",
    )(product, x, gate, outer, w, up, down)


def outer_kernel(where_ref, *refs):
    groups, (w_ref, out_ref, right_scr, left_scr, w_scr, m_scr) = refs[:-6], refs[-6:]
    rows, width, chans = out_ref.shape
    total = 2 * sum(ref.shape[0] for ref in groups)
    depth = m_scr.shape[1] // total
    s = 0
    for ref in groups:
        for k in range(ref.shape[0]):
            both = ref[k, 2 * depth :].astype(F32)
            for far in range(2):
                at = s + far * (total // 2)
                side = ref[k, far * depth : (far + 1) * depth].astype(F32)
                right_scr[pl.ds(at, depth, stride=total), :] = side
                left_scr[pl.ds(at, rows, stride=total), :] = both
            s += 1
    right = jnp.transpose(right_scr[: depth * total]).astype(BF16)
    both = left_scr[: rows * total]
    shift = lax.bitwise_and(where_ref[1], 1) * depth
    first = pltpu.roll(both, width - shift, 1)[:, :depth]
    second = pltpu.roll(both, width - 2 * depth - shift, 1)[:, :depth]
    row = lax.broadcasted_iota(jnp.int32, first.shape, 0)
    left = jnp.where(row % total < total // 2, first, second).astype(BF16)
    w_scr[: depth * depth] = w_ref[...].astype(F32)
    for d in range(depth):
        part = w_scr[pl.ds(d, depth, stride=depth), :].astype(BF16)
        m_scr[:, d * total : (d + 1) * total] = (
            dot(left, part).astype(BF16).reshape(rows, total, chans)
        )
    for i in range(0, rows, 2):
        pair = jnp.concatenate([m_scr[i], m_scr[i + 1]], axis=1)
        result = dot(right, pair) / total
        out_ref[i] = result[:, :chans]
        out_ref[i + 1] = result[:, chans:]


def outer_update(where, groups, w, rows, chans):
    total = 2 * sum(group.shape[0] for group in groups)
    width = groups[0].shape[2]
    depth = (groups[0].shape[1] - rows) // 2
    return pl.pallas_call(
        outer_kernel,
        out_shape=jax.ShapeDtypeStruct((rows, width, chans), F32),
        in_specs=[SMEM] + [VMEM] * (len(groups) + 1),
        out_specs=VMEM,
        scratch_shapes=[
            pltpu.VMEM(((depth + 1) * total, width), F32),
            pltpu.VMEM(((rows + 1) * total, width), F32),
            pltpu.VMEM((depth * (depth + 1), chans), F32),
            pltpu.VMEM((rows, depth * total, chans), BF16),
        ],
        compiler_params=PARAMS,
        cost_estimate=cost(2 * rows * width * depth * total * chans * 2, rows * width * chans * 4),
        name="outer_product_mean",
    )(where, *groups, w)


def swap(x, n_branch, n_rows, mask):
    count = n_branch * n_rows
    return lax.ppermute(x, AXES, [(d, d ^ mask) for d in range(count)])


def own_channels_device(
    n_branch,
    n_rows,
    homolog_features,
    pairwise_input,
    transition_expand_matrix,
    transition_contract_matrix,
    factor_pair_matrices,
    outer_output_weight,
    triangle_projection_weight,
    triangle_output_weight,
    pairwise_up_weight,
    pairwise_down_weight,
):
    rows, _, chans = pairwise_input.shape
    near = 8
    halves = n_rows // near
    places = near // 2
    per = chans // (n_branch * near)
    where = jnp.stack([lax.axis_index("branch"), lax.axis_index("rows")]).astype(jnp.int32)

    far_row = swap(homolog_features, n_branch, n_rows, near)
    sent = right_operand(
        pairwise_input, triangle_projection_weight, n_branch, n_branch * n_rows, per
    )
    received = lax.all_to_all(sent, AXES, 0, 0, tiled=True)

    other = swap(pairwise_input, n_branch, n_rows, 1)
    left = left_operand(where, pairwise_input, other, triangle_projection_weight, n_branch, near)
    fresh, pieces = messages(
        where,
        left,
        homolog_features,
        far_row,
        transition_expand_matrix,
        transition_contract_matrix,
        jnp.transpose(factor_pair_matrices),
        rows,
        n_branch,
        near,
    )
    moved = [
        piece if t == 0 else swap(piece, n_branch, n_rows, t // places * n_rows + t % places * 2)
        for t, piece in zip(TARGETS, pieces)
    ]
    mine = jnp.stack([piece[per * 2 * rows :] for piece in moved])
    groups = [mine, swap(mine, n_branch, n_rows, 1)]
    outer = outer_update(where, groups, outer_output_weight, rows, chans)
    gate_tile, _ = lax.optimization_barrier((pairwise_input, moved[0]))
    gate = output_gate(gate_tile, triangle_projection_weight)

    product = triangle_product(where, received, moved, n_branch, near)
    members = [
        [b * n_rows + h * near + k for b in range(n_branch) for k in range(near)][::-1]
        for h in range(halves)
    ]
    returned = lax.all_to_all(product, AXES, 0, 0, axis_index_groups=members, tiled=True)
    pairwise_output = pair_output(
        returned,
        pairwise_input,
        gate,
        outer,
        triangle_output_weight,
        pairwise_up_weight,
        pairwise_down_weight,
    )
    return (fresh, pairwise_output)


def on_device(n_branch, n_rows, homolog_features, pairwise_input, *weights):
    rows, width, chans = pairwise_input.shape
    near = 8
    halves = n_rows // near
    fits = (
        homolog_features.shape[0] == 1
        and halves == 2
        and n_branch == 2
        and n_rows % near == 0
        and chans % (n_branch * near) == 0
        and rows == 16
        and width == 128
        and homolog_features.shape[1] == n_rows * rows == n_branch * width
        and 2 * weights[2].shape[1] == width
    )
    if fits:
        return own_channels_device(n_branch, n_rows, homolog_features, pairwise_input, *weights)
    return general_device(homolog_features, pairwise_input, *weights)


def solution(mesh):
    return jax.shard_map(
        functools.partial(on_device, mesh.shape["branch"], mesh.shape["rows"]),
        mesh=mesh,
        in_specs=(
            P(("branch", "rows"), None, None),
            P("rows", "branch", None),
            P(),
            P(),
            P(),
            P(),
            P(),
            P(),
            P(),
            P(),
        ),
        out_specs=(P(("branch", "rows"), None, None), P("rows", "branch", None)),
        check_vma=False,
    )
```

```python
import functools

import jax
import jax.numpy as jnp
from jax import lax
from jax.experimental import pallas as pl
from jax.experimental.pallas import tpu as pltpu
from jax.sharding import PartitionSpec as P

BF16 = jnp.bfloat16
F32 = jnp.float32
AXES = ("branch", "rows")
NT = (((1,), (1,)), ((), ()))
TN = (((0,), (0,)), ((), ()))
VMEM = pl.BlockSpec(memory_space=pltpu.VMEM)
SMEM = pl.BlockSpec(memory_space=pltpu.SMEM)
TARGETS = (0, 4, 1, 2, 7, 3, 6, 5)
HBM = pl.BlockSpec(memory_space=pltpu.HBM)
PARAMS = pltpu.CompilerParams(vmem_limit_bytes=48 * 1024 * 1024)

def standardize_features(values, dimension):
    average = jnp.mean(values, axis=dimension, keepdims=True)
    centered = values - average
    variance = jnp.mean(centered * centered, axis=dimension, keepdims=True)
    return centered * lax.rsqrt(variance + 1e-05)


def alignment_branch(
    homolog_features, transition_expand_matrix, transition_contract_matrix, factor_pair_matrices
):
    local_rows, sequence_length, channel_width = homolog_features.shape
    homolog_real_matrix = homolog_features.astype(jnp.float32)
    standardized_homologs = (
        standardize_features(homolog_real_matrix, -1)
        .astype(jnp.bfloat16)
        .reshape(local_rows * sequence_length, channel_width)
    )
    expanded_activations = jax.nn.relu(
        jnp.dot(standardized_homologs, transition_expand_matrix, preferred_element_type=jnp.float32)
    ).astype(jnp.bfloat16)
    refreshed_homolog_features = (
        homolog_real_matrix
        + jnp.dot(
            expanded_activations, transition_contract_matrix, preferred_element_type=jnp.float32
        ).reshape(homolog_features.shape)
    ).astype(jnp.bfloat16)
    standardized_for_factors = (
        standardize_features(refreshed_homolog_features.astype(jnp.float32), -1)
        .astype(jnp.bfloat16)
        .reshape(local_rows * sequence_length, channel_width)
    )
    projected = jnp.dot(
        standardized_for_factors, factor_pair_matrices, preferred_element_type=jnp.float32
    ).reshape(local_rows, sequence_length, -1)
    channels = projected.shape[-1] // 2
    left_side = projected[..., :channels].astype(jnp.bfloat16)
    right_side = jnp.swapaxes(projected[..., channels:].astype(jnp.bfloat16), 1, 2)
    left_pair = lax.all_gather(left_side, "branch", axis=0, tiled=True)
    left_gathered = lax.all_to_all(left_pair, "rows", split_axis=1, concat_axis=0, tiled=True)
    right_pair = lax.all_to_all(right_side, "branch", split_axis=2, concat_axis=0, tiled=True)
    right_gathered = lax.all_gather(right_pair, "rows", axis=0, tiled=True)
    return (refreshed_homolog_features, left_gathered, right_gathered)


def send_whole(tri_left, tri_right):
    return (
        lax.all_to_all(
            lax.all_to_all(tri_left, "branch", split_axis=0, concat_axis=2, tiled=True),
            "rows",
            split_axis=0,
            concat_axis=1,
            tiled=True,
        ),
        lax.all_to_all(
            lax.all_to_all(tri_right, "branch", split_axis=0, concat_axis=2, tiled=True),
            "rows",
            split_axis=0,
            concat_axis=1,
            tiled=True,
        ),
    )


def send_back(product):
    return lax.all_to_all(
        lax.all_to_all(product, "rows", split_axis=1, concat_axis=0, tiled=True),
        "branch",
        split_axis=2,
        concat_axis=0,
        tiled=True,
    )


def pair_branch(
    pairwise_input,
    triangle_projection_weight,
    triangle_output_weight,
    pairwise_up_weight,
    pairwise_down_weight,
):
    tile_rows, columns, chans = pairwise_input.shape
    pair_float = pairwise_input.astype(jnp.float32)
    pair_norm = standardize_features(pair_float, -1).astype(jnp.bfloat16)
    norm_flat = pair_norm.reshape(tile_rows * columns, chans)
    proj_flat = lax.dot_general(
        triangle_projection_weight,
        norm_flat,
        (((0,), (1,)), ((), ())),
        preferred_element_type=jnp.float32,
    )
    proj_tile = proj_flat[: 4 * chans].reshape(4 * chans, tile_rows, columns)
    gate_vals = jax.nn.sigmoid(proj_flat[4 * chans :])
    tri_left = (jax.nn.sigmoid(proj_tile[chans : 2 * chans]) * proj_tile[:chans]).astype(
        jnp.bfloat16
    )
    tri_right = (jax.nn.sigmoid(proj_tile[3 * chans :]) * proj_tile[2 * chans : 3 * chans]).astype(
        jnp.bfloat16
    )
    left_chan, right_chan = send_whole(tri_left, tri_right)
    product = jnp.einsum(
        "cik,cjk->cij", left_chan, right_chan, preferred_element_type=jnp.float32
    ).astype(jnp.bfloat16)
    product_tile = send_back(product)
    prod_norm = (
        standardize_features(product_tile.astype(jnp.float32), 0)
        .astype(jnp.bfloat16)
        .reshape(chans, tile_rows * columns)
    )
    tri_update = lax.dot_general(
        triangle_output_weight,
        prod_norm,
        (((0,), (0,)), ((), ())),
        preferred_element_type=jnp.float32,
    )
    gated_update = jnp.transpose(gate_vals * tri_update).reshape(tile_rows, columns, chans)
    pair_mid = pair_float + gated_update
    mid_norm = standardize_features(pair_mid, -1).astype(jnp.bfloat16)
    pair_hidden = jax.nn.relu(
        jnp.einsum("ijd,dh->ijh", mid_norm, pairwise_up_weight, preferred_element_type=jnp.float32)
    ).astype(jnp.bfloat16)
    return pair_mid + jnp.einsum(
        "ijh,hd->ijd", pair_hidden, pairwise_down_weight, preferred_element_type=jnp.float32
    )


def outer_product(left_gathered, right_gathered, outer_output_weight):
    total_rows, tile_rows, channels = left_gathered.shape
    columns = right_gathered.shape[2]
    span_cols = 128
    left_flat = left_gathered.reshape(total_rows, tile_rows * channels)
    pieces = []
    for offset in range(0, columns, span_cols):
        right_piece = right_gathered[:, :, offset : offset + span_cols].reshape(
            total_rows, channels * span_cols
        )
        outer_vals = lax.dot_general(
            left_flat, right_piece, (((0,), (0,)), ((), ())), preferred_element_type=jnp.float32
        )
        outer_vals = (
            (outer_vals / total_rows)
            .astype(jnp.bfloat16)
            .reshape(tile_rows, channels * channels, span_cols)
        )
        pieces.append(
            lax.dot_general(
                outer_output_weight,
                outer_vals,
                (((0,), (1,)), ((), ())),
                preferred_element_type=jnp.float32,
            )
        )
    outer_eij = jnp.concatenate(pieces, axis=2)
    return jnp.transpose(outer_eij, (1, 2, 0))


def general_device(
    homolog_features,
    pairwise_input,
    transition_expand_matrix,
    transition_contract_matrix,
    factor_pair_matrices,
    outer_output_weight,
    triangle_projection_weight,
    triangle_output_weight,
    pairwise_up_weight,
    pairwise_down_weight,
):
    refreshed_homolog_features, left_gathered, right_gathered = alignment_branch(
        homolog_features, transition_expand_matrix, transition_contract_matrix, factor_pair_matrices
    )
    pair_mid = pair_branch(
        pairwise_input,
        triangle_projection_weight,
        triangle_output_weight,
        pairwise_up_weight,
        pairwise_down_weight,
    )
    outer_update = outer_product(left_gathered, right_gathered, outer_output_weight)
    pairwise_output = (pair_mid + outer_update).astype(jnp.bfloat16)
    return (refreshed_homolog_features, pairwise_output)


def normed(values, axis):
    average = jnp.mean(values, axis=axis, keepdims=True)
    centered = values - average
    variance = jnp.mean(centered * centered, axis=axis, keepdims=True)
    return (centered * lax.rsqrt(variance + 1e-05)).astype(BF16)


def sigmoid(values):
    return 0.5 * jnp.tanh(0.5 * values) + 0.5


def dot(a, b, dims=(((1,), (0,)), ((), ()))):
    return lax.dot_general(a, b, dims, preferred_element_type=F32)


def cost(flops, nbytes, transcendentals=0):
    return pl.CostEstimate(flops=flops, bytes_accessed=nbytes, transcendentals=transcendentals)


def channel_order(w, sides, source, count):
    chans = w.shape[0]
    col = lax.broadcasted_iota(jnp.int32, (count, chans), 1)
    order = jnp.where(col == source, 1.0, 0.0).astype(BF16)
    return [dot(order, w[:, s * chans : (s + 1) * chans], NT).astype(BF16) for s in sides]


def gated_rows(values, gates, rows_ref, store):
    rows, width, chans = rows_ref.shape
    for i in range(0, rows, 2):
        tokens = rows_ref[i : i + 2].reshape(2 * width, chans)
        result = dot(values, tokens, NT) * sigmoid(dot(gates, tokens, NT))
        store(i, result[:, :width])
        store(i + 1, result[:, width:])


def right_kernel(
    n_branch, x_hbm, w_hbm, sent_hbm, x_ref, w_ref, sent_ref, scr, sems
):
    rows, width, chans = x_ref.shape
    groups, per = sent_ref.shape[:2]
    near = groups // n_branch
    halves = sent_hbm.shape[0] // groups
    columns = w_hbm.at[:, pl.ds(2 * chans, 2 * chans)]
    copies = [
        pltpu.make_async_copy(columns, w_ref, sems.at[0]),
        pltpu.make_async_copy(x_hbm, x_ref, sems.at[1]),
    ]
    for copy in copies:
        copy.start()
    for copy in copies:
        copy.wait()
    values = jnp.transpose(w_ref[:, :chans])
    gates = jnp.transpose(w_ref[:, chans:])
    step = 4
    parts = []
    for i in range(0, rows, step):
        tokens = normed(x_ref[i : i + step].astype(F32), -1)
        parts.append(tokens.reshape(step * width, chans))
    outs = []
    for i, tokens in zip(range(0, rows, step), parts):
        result = dot(values, tokens, NT) * sigmoid(dot(gates, tokens, NT))
        for k in range(step):
            scr[pl.ds(i + k, chans, stride=rows), :] = result[:, k * width : (k + 1) * width]
    span = 4
    for g in range(groups):
        for c in range(per):
            q = (g * per + c) * rows
            sent_ref[g, c] = scr[q : q + rows, :].astype(BF16)
        if g % span == span - 1:
            begin = g + 1 - span
            for h in range(halves):
                to = (begin // near * halves + h) * near + begin % near
                copy = pltpu.make_async_copy(
                    sent_ref.at[pl.ds(begin, span)],
                    sent_hbm.at[pl.ds(to, span)],
                    sems.at[2 + len(outs)],
                )
                copy.start()
                outs.append(copy)
    for copy in outs:
        copy.wait()


def right_operand(x, w, n_branch, devices, per):
    rows, width, chans = x.shape
    groups = chans // per
    return pl.pallas_call(
        functools.partial(right_kernel, n_branch),
        out_shape=jax.ShapeDtypeStruct((devices, per, rows, width), BF16),
        in_specs=[HBM] * 2,
        out_specs=HBM,
        scratch_shapes=[
            pltpu.VMEM(x.shape, BF16),
            pltpu.VMEM((chans, 2 * chans), BF16),
            pltpu.VMEM((groups, per, rows, width), BF16),
            pltpu.VMEM(((chans + 1) * rows, width), F32),
            pltpu.SemaphoreType.DMA((3 + devices // 4,)),
        ],
        cost_estimate=cost(2 * rows * width * chans * 2 * chans, 3 * rows * width * chans * 2),
        name="right_operand",
    )(x, w)


def left_kernel(n_branch, near, where_ref, x_ref, other_ref, w_ref, out_ref, scr, norm_scr):
    rows, _, chans = x_ref.shape
    branch, row_at = where_ref[0], where_ref[1]
    core = lax.bitwise_and(row_at, 1)
    place = lax.shift_right_logical(lax.bitwise_and(row_at, near - 1), 1)
    count = out_ref.shape[0]
    places = count // n_branch
    per = chans // (n_branch * near)

    total = count * per
    q = lax.broadcasted_iota(jnp.int32, (total, chans), 0)
    t = q // per
    group = lax.bitwise_xor(t // places, branch) * near + (
        lax.bitwise_xor(t % places, place) * 2 + core
    )
    values, gates = channel_order(w_ref[...], (0, 1), group * per + q % per, total)

    def store_at(at):
        def store(i, block):
            scr[at, pl.ds(i, total, stride=rows), :] = block

        return store

    for k, ref, at in ((0, x_ref, core), (1, other_ref, 1 - core)):
        for i in range(0, rows, 4):
            norm_scr[k, i : i + 4] = normed(ref[i : i + 4].astype(F32), -1)
        gated_rows(values, gates, norm_scr.at[k], store_at(at))
    for t in range(count):
        for c in range(per):
            for k in range(2):
                start = (t * per + c) * rows
                out_ref[t, pl.ds((c * 2 + k) * rows, rows)] = scr[
                    k, start : start + rows, :
                ].astype(BF16)


def left_operand(where, x, other, w, n_branch, near):
    rows, width, chans = x.shape
    count = n_branch * near // 2
    per = chans // (n_branch * near)
    return pl.pallas_call(
        functools.partial(left_kernel, n_branch, near),
        out_shape=jax.ShapeDtypeStruct((count, per * 2 * rows, width), BF16),
        in_specs=[SMEM] + [VMEM] * 3,
        out_specs=VMEM,
        scratch_shapes=[
            pltpu.VMEM((2, (count * per + 1) * rows, width), F32),
            pltpu.VMEM((2,) + x.shape, BF16),
        ],
        compiler_params=PARAMS,
        cost_estimate=cost(4 * x.size * 2 * chans, x.size * 8),
        name="left_operand",
    )(where, x, other, w)


def message_kernel(
    n_branch, near, rows, where_ref, left_ref, seq_ref, far_ref, up_ref, down_ref, factor_ref,
    fresh_ref, *rest
):
    out_refs, (right_scr, left_scr) = rest[:-2], rest[-2:]
    count, size, width = left_ref.shape
    for t, out_ref in zip(TARGETS, out_refs):
        out_ref[:size] = left_ref[t]
    x = [ref[0].astype(F32) for ref in (seq_ref, far_ref)]
    tokens = [normed(v, -1) for v in x]
    hidden = [jnp.maximum(dot(t, up_ref[...]).astype(BF16), 0.0) for t in tokens]
    fresh = [(v + dot(h, down_ref[...])).astype(BF16) for v, h in zip(x, hidden)]
    fresh_ref[0] = fresh[0]
    factor = factor_ref[...]
    depth = factor.shape[0] // 2
    tokens = [normed(v.astype(F32), -1) for v in fresh]
    for k, row in enumerate(tokens):
        right = dot(factor[depth:], row, NT).astype(BF16)
        for b in range(n_branch):
            right_scr[b, k * depth : (k + 1) * depth] = right[:, b * width : (b + 1) * width]
    tiles = [dot(row, factor[:depth], NT).astype(BF16).reshape(-1, 2, rows, depth) for row in tokens]
    for t in range(left_scr.shape[0]):
        left_scr[t] = jnp.concatenate([tile[t, c] for tile in tiles for c in range(2)], axis=1)
    branch, row_at = where_ref[0], where_ref[1]
    place = lax.shift_right_logical(lax.bitwise_and(row_at, near - 1), 1)
    places = count // n_branch
    first = row_at // near * places
    for t, out_ref in zip(TARGETS, out_refs):
        out_ref[size : size + 2 * depth] = right_scr[lax.bitwise_xor(branch, t // places)]
        out_ref[size + 2 * depth :] = left_scr[first + lax.bitwise_xor(place, t % places)]


def messages(where, left, seq, far, up, down, factor, rows, n_branch, near):
    _, length, feats = seq.shape
    depth = factor.shape[0] // 2
    count, size, width = left.shape
    piece = jax.ShapeDtypeStruct((size + 2 * depth + rows, width), BF16)
    fresh, *pieces = pl.pallas_call(
        functools.partial(message_kernel, n_branch, near, rows),
        out_shape=[jax.ShapeDtypeStruct(seq.shape, BF16)] + [piece] * count,
        in_specs=[SMEM] + [VMEM] * 6,
        out_specs=[VMEM] * (1 + count),
        scratch_shapes=[
            pltpu.VMEM((n_branch, 2 * depth, width), BF16),
            pltpu.VMEM((length // rows // 2, rows, width), BF16),
        ],
        compiler_params=PARAMS,
        cost_estimate=cost(2 * 10**10, 4 * feats * up.shape[1]),
        name="msa_transition_and_messages",
    )(where, left, seq, far, up, down, factor)
    return fresh, pieces


def gate_kernel(x_ref, w_ref, out_ref):
    rows, width, chans = x_ref.shape
    tokens = normed(x_ref[...].astype(F32).reshape(rows * width, chans), -1)
    out_ref[...] = sigmoid(dot(tokens, w_ref[:, 4 * chans :])).reshape(rows, width, chans)


def output_gate(x, w):
    rows, width, chans = x.shape
    step = 4
    spec = pl.BlockSpec((step, width, chans), lambda i: (i, 0, 0))
    return pl.pallas_call(
        gate_kernel,
        grid=(rows // step,),
        out_shape=jax.ShapeDtypeStruct(x.shape, F32),
        in_specs=[spec, pl.BlockSpec(w.shape, lambda i: (0, 0))],
        out_specs=spec,
        compiler_params=PARAMS,
        cost_estimate=cost(2 * rows * width * chans * chans, rows * width * chans * 6),
        name="triangle_output_gate",
    )(x, w)


def product_kernel(n_branch, near, where_ref, in_ref, *rest):
    places = near // 2
    left_refs = dict(zip(TARGETS, rest))
    out_hbm, out_ref, sems = rest[n_branch * places :]
    devices, per, rows, width = in_ref.shape
    n_rows = devices // n_branch
    branch, row_at = where_ref[0], where_ref[1]
    place = lax.shift_right_logical(lax.bitwise_and(row_at, near - 1), 1)
    outs = []
    ends = (0, per // 2, per * 3 // 4, per)
    for c in range(per):
        span = slice(c * 2 * rows, (c + 1) * 2 * rows)
        left = jnp.concatenate(
            [
                jnp.concatenate([left_refs[s * places + p][span] for p in range(places)], axis=0)
                for s in range(n_branch)
            ],
            axis=1,
        )
        right = jnp.concatenate(
            [
                in_ref[pl.ds(lax.bitwise_xor(branch, s) * n_rows, n_rows), c].reshape(
                    n_rows * rows, width
                )
                for s in range(n_branch)
            ],
            axis=1,
        )
        product = dot(left, right, NT).astype(BF16)
        for p in range(places):
            at = lax.bitwise_xor(place, p) * 2
            part = product[p * 2 * rows : (p + 1) * 2 * rows]
            for b in range(n_branch):
                for k in range(2):
                    out_ref[n_branch * near - 1 - (b * near + at + k), c] = part[
                        k * rows : (k + 1) * rows, b * width : (b + 1) * width
                    ]
        if c + 1 in ends:
            done = pl.ds(ends[len(outs)], c + 1 - ends[len(outs)])
            copy = pltpu.make_async_copy(
                out_ref.at[:, done], out_hbm.at[:, done], sems.at[len(outs)]
            )
            copy.start()
            outs.append(copy)
    for copy in outs:
        copy.wait()


def triangle_product(where, received, pieces, n_branch, near):
    devices, per, rows, width = received.shape
    shape = (n_branch * near, per, rows, width)
    return pl.pallas_call(
        functools.partial(product_kernel, n_branch, near),
        out_shape=jax.ShapeDtypeStruct(shape, BF16),
        in_specs=[SMEM] + [VMEM] * (1 + len(pieces)),
        out_specs=HBM,
        scratch_shapes=[pltpu.VMEM(shape, BF16), pltpu.SemaphoreType.DMA((per // 2,))],
        compiler_params=PARAMS,
        cost_estimate=cost(2 * near * rows * received.size, received.size * 4),
        name="triangle_product",
    )(where, received, *pieces)


def pair_output_kernel(
    p_ref, x_ref, gate_ref, outer_ref, w_ref, up_ref, down_ref, out_hbm, scr, out_ref, sems
):
    devices, per, rows, width = p_ref.shape
    chans = devices * per
    step = rows // 2
    shape = (step * width, chans)
    share = up_ref.shape[1] // 4

    for g in range(devices):
        for c in range(per):
            k = (g * per + c) * rows
            scr[k : k + rows, :] = p_ref[devices - 1 - g, c].astype(F32)

    def triangle(i):
        parts = [
            normed(scr[pl.ds(i + k, chans, stride=rows), :], 0) for k in range(step)
        ]
        update = dot(jnp.concatenate(parts, axis=1), w_ref[...], TN)
        x = x_ref[i : i + step].astype(F32).reshape(shape)
        middle = x + gate_ref[i : i + step].reshape(shape) * update
        return middle, normed(middle, -1)

    def transition(i, middle, tokens):
        result = middle + outer_ref[i : i + step].reshape(shape)
        for h in range(0, up_ref.shape[1], share):
            hidden = dot(tokens, up_ref[:, h : h + share]).astype(BF16)
            result = result + dot(jnp.maximum(hidden, 0.0), down_ref[h : h + share])
        out_ref[i : i + step] = result.astype(BF16).reshape(step, width, chans)
        part = pl.ds(i, step)
        copy = pltpu.make_async_copy(out_ref.at[part], out_hbm.at[part], sems.at[i // step])
        copy.start()
        return copy

    middles = [triangle(i) for i in range(0, rows, step)]
    copies = [transition(i * step, *middle) for i, middle in enumerate(middles)]
    for copy in copies:
        copy.wait()


def pair_output(product, x, gate, outer, w, up, down):
    devices, per, rows, width = product.shape
    chans = devices * per
    return pl.pallas_call(
        pair_output_kernel,
        out_shape=jax.ShapeDtypeStruct(x.shape, BF16),
        in_specs=[VMEM] * 7,
        out_specs=HBM,
        scratch_shapes=[
            pltpu.VMEM((rows * (chans + 1), width), F32),
            pltpu.VMEM(x.shape, BF16),
            pltpu.SemaphoreType.DMA((2,)),
        ],
        compiler_params=PARAMS,
        cost_estimate=cost(2 * x.size * (chans + 2 * up.shape[1]), x.size * 14),
        name="pair_output",
    )(product, x, gate, outer, w, up, down)


def outer_kernel(where_ref, *refs):
    groups, (w_ref, out_ref, right_scr, left_scr, w_scr, m_scr) = refs[:-6], refs[-6:]
    rows, width, chans = out_ref.shape
    total = 2 * sum(ref.shape[0] for ref in groups)
    depth = m_scr.shape[1] // total
    s = 0
    for ref in groups:
        for k in range(ref.shape[0]):
            both = ref[k, 2 * depth :].astype(F32)
            for far in range(2):
                at = s + far * (total // 2)
                side = ref[k, far * depth : (far + 1) * depth].astype(F32)
                right_scr[pl.ds(at, depth, stride=total), :] = side
                left_scr[pl.ds(at, rows, stride=total), :] = both
            s += 1
    right = jnp.transpose(right_scr[: depth * total]).astype(BF16)
    both = left_scr[: rows * total]
    shift = lax.bitwise_and(where_ref[1], 1) * depth
    first = pltpu.roll(both, width - shift, 1)[:, :depth]
    second = pltpu.roll(both, width - 2 * depth - shift, 1)[:, :depth]
    row = lax.broadcasted_iota(jnp.int32, first.shape, 0)
    left = jnp.where(row % total < total // 2, first, second).astype(BF16)
    w_scr[: depth * depth] = w_ref[...].astype(F32)
    for d in range(depth):
        part = w_scr[pl.ds(d, depth, stride=depth), :].astype(BF16)
        m_scr[:, d * total : (d + 1) * total] = (
            dot(left, part).astype(BF16).reshape(rows, total, chans)
        )
    for i in range(0, rows, 2):
        pair = jnp.concatenate([m_scr[i], m_scr[i + 1]], axis=1)
        result = dot(right, pair) / total
        out_ref[i] = result[:, :chans]
        out_ref[i + 1] = result[:, chans:]


def outer_update(where, groups, w, rows, chans):
    total = 2 * sum(group.shape[0] for group in groups)
    width = groups[0].shape[2]
    depth = (groups[0].shape[1] - rows) // 2
    return pl.pallas_call(
        outer_kernel,
        out_shape=jax.ShapeDtypeStruct((rows, width, chans), F32),
        in_specs=[SMEM] + [VMEM] * (len(groups) + 1),
        out_specs=VMEM,
        scratch_shapes=[
            pltpu.VMEM(((depth + 1) * total, width), F32),
            pltpu.VMEM(((rows + 1) * total, width), F32),
            pltpu.VMEM((depth * (depth + 1), chans), F32),
            pltpu.VMEM((rows, depth * total, chans), BF16),
        ],
        compiler_params=PARAMS,
        cost_estimate=cost(2 * rows * width * depth * total * chans * 2, rows * width * chans * 4),
        name="outer_product_mean",
    )(where, *groups, w)


def swap(x, n_branch, n_rows, mask):
    count = n_branch * n_rows
    return lax.ppermute(x, AXES, [(d, d ^ mask) for d in range(count)])


def own_channels_device(
    n_branch,
    n_rows,
    homolog_features,
    pairwise_input,
    transition_expand_matrix,
    transition_contract_matrix,
    factor_pair_matrices,
    outer_output_weight,
    triangle_projection_weight,
    triangle_output_weight,
    pairwise_up_weight,
    pairwise_down_weight,
):
    rows, _, chans = pairwise_input.shape
    near = 8
    halves = n_rows // near
    places = near // 2
    per = chans // (n_branch * near)
    where = jnp.stack([lax.axis_index("branch"), lax.axis_index("rows")]).astype(jnp.int32)

    far_row = swap(homolog_features, n_branch, n_rows, near)
    sent = right_operand(
        pairwise_input, triangle_projection_weight, n_branch, n_branch * n_rows, per
    )
    received = lax.all_to_all(sent, AXES, 0, 0, tiled=True)

    other = swap(pairwise_input, n_branch, n_rows, 1)
    left = left_operand(where, pairwise_input, other, triangle_projection_weight, n_branch, near)
    fresh, pieces = messages(
        where,
        left,
        homolog_features,
        far_row,
        transition_expand_matrix,
        transition_contract_matrix,
        jnp.transpose(factor_pair_matrices),
        rows,
        n_branch,
        near,
    )
    moved = [
        piece if t == 0 else swap(piece, n_branch, n_rows, t // places * n_rows + t % places * 2)
        for t, piece in zip(TARGETS, pieces)
    ]
    mine = jnp.stack([piece[per * 2 * rows :] for piece in moved])
    groups = [mine, swap(mine, n_branch, n_rows, 1)]
    outer = outer_update(where, groups, outer_output_weight, rows, chans)
    gate_tile, _ = lax.optimization_barrier((pairwise_input, moved[0]))
    gate = output_gate(gate_tile, triangle_projection_weight)

    product = triangle_product(where, received, moved, n_branch, near)
    members = [
        [b * n_rows + h * near + k for b in range(n_branch) for k in range(near)][::-1]
        for h in range(halves)
    ]
    returned = lax.all_to_all(product, AXES, 0, 0, axis_index_groups=members, tiled=True)
    pairwise_output = pair_output(
        returned,
        pairwise_input,
        gate,
        outer,
        triangle_output_weight,
        pairwise_up_weight,
        pairwise_down_weight,
    )
    return (fresh, pairwise_output)


def on_device(n_branch, n_rows, homolog_features, pairwise_input, *weights):
    rows, width, chans = pairwise_input.shape
    near = 8
    halves = n_rows // near
    fits = (
        homolog_features.shape[0] == 1
        and halves == 2
        and n_branch == 2
        and n_rows % near == 0
        and chans % (n_branch * near) == 0
        and rows == 16
        and width == 128
        and homolog_features.shape[1] == n_rows * rows == n_branch * width
        and 2 * weights[2].shape[1] == width
    )
    if fits:
        return own_channels_device(n_branch, n_rows, homolog_features, pairwise_input, *weights)
    return general_device(homolog_features, pairwise_input, *weights)


def solution(mesh):
    return jax.shard_map(
        functools.partial(on_device, mesh.shape["branch"], mesh.shape["rows"]),
        mesh=mesh,
        in_specs=(
            P(("branch", "rows"), None, None),
            P("rows", "branch", None),
            P(),
            P(),
            P(),
            P(),
            P(),
            P(),
            P(),
            P(),
        ),
        out_specs=(P(("branch", "rows"), None, None), P("rows", "branch", None)),
        check_vma=False,
    )
```
